32 devices in a mesh: shot: 8 (over y, x, core), slab: 4 (over z).
Axes of the slice: x: 2, y: 2, z: 4, core: 2. Of those that a mesh axis runs over, the one named last changes fastest.
Arguments:
- state_before: float32 [8, 64, 128, 128], P('shot', 'slab'), may hold values from -6 to 6
- state_now: float32 [8, 64, 128, 128], P('shot', 'slab'), may hold values from -6 to 6
- adjoint_after: float32 [8, 64, 128, 128], P('shot', 'slab'), may hold values from -6 to 6
- adjoint_now: float32 [8, 64, 128, 128], P('shot', 'slab'), may hold values from -6 to 6
- speed_term: float32 [64, 128, 128], P('slab'), may hold values from 0.04 to 0.18
- wavelet: float32 [8, 8], P('shot'), may hold values from -180 to 180
- source: int32 [8, 3], P('shot'), may hold values from 0 to 127, as said below
- receivers: int32 [8, 3, 1024], P('shot'), may hold values from 0 to 127, as said below
- traces: float32 [8, 8, 1024], P('shot', None, 'slab'), may hold values from -6 to 6
Outputs:
- adj_first: float32 [8, 64, 128, 128], P('shot', 'slab')
- adj_second: float32 [8, 64, 128, 128], P('shot', 'slab')
- gradient: float32 [64, 128, 128], P('slab', 'shot')
The draws below stay inside these ranges and needn't reach their ends.
Inputs may be any that keep to these rules, and one draw needn't show every extreme that they name: `source`: row 0 is a depth row below 64, row 1 a cell below 128, row 2 a cell below 128. `receivers`: row 0 is a depth row below 64, row 1 a cell below 128, row 2 a cell below 128; several receivers may share a cell.
All inputs are finite; a program needn't handle non-finite values.
Results may differ from the reference program's by a relative error of at most 0.0003.
Values sent between devices are 32-bit elements; how exact they have to be, the bound alone decides.
No kernel may reach another device: no remote copies, remote signals or barrier semaphores. Data moves between devices by JAX's collectives and lax.ppermute only.
A program may use at most 128 MiB of HBM per device.

```python
import math
import jax
import jax.numpy as jnp
from jax import lax

NY = 128
NZ = 128
STEPS = 8
NX = 64
RECV = 1024
SHOTS = 8


def draw_source(key, part):
    keys = jax.random.split(key, 3)
    depth = jax.random.randint(keys[0], (SHOTS,), 0, NX)
    across = jax.random.randint(keys[1], (SHOTS,), 0, NY)
    along = jax.random.randint(keys[2], (SHOTS,), 0, NZ)
    return jnp.stack((depth, across, along), axis=1).astype(jnp.int32)


def draw_receivers(key, part):
    keys = jax.random.split(key, 4)
    depth = jnp.minimum(jax.random.randint(keys[0], (SHOTS, RECV), 0, NX), jax.random.randint(keys[1], (SHOTS, RECV), 0, NX))
    across = jax.random.randint(keys[2], (SHOTS, RECV), 0, NY)
    along = jax.random.randint(keys[3], (SHOTS, RECV), 0, NZ)
    return jnp.stack((depth, across, along), axis=1).astype(jnp.int32)


def level_of(stream_key, extent, cuts, least, largest):
    factor_of, own = 1.0, jax.random.fold_in(stream_key, 6)
    for dim, parts in cuts:
        draws = jnp.exp(jax.random.uniform(jax.random.fold_in(own, dim), (parts,), jnp.float32, least / len(cuts), largest / len(cuts)))
        factor_of = factor_of * jnp.repeat(draws, extent[dim] // parts).reshape([-1 if axis == dim else 1 for axis in range(len(extent))])
    return factor_of


def scatter_about(key, shape, spread, reach, shards=(), held_as=jnp.bfloat16):
    array = jax.random.normal(key, shape, jnp.float32) * spread
    if len(shards) > 0:
        array = level_of(key, shape, shards, -0.22, 0.18) * array
    return jnp.clip(array, min=-reach, max=reach).astype(held_as)


def setup_inputs(seed: int = 0) -> dict:
    splits = jax.random.split(jax.random.key(seed), 10)
    return {
        "state_before": scatter_about(splits[0], (SHOTS, NX, NY, NZ), 1.0, 6.0, ((0, 8), (1, 4)), jnp.float32),
        "state_now": scatter_about(splits[1], (SHOTS, NX, NY, NZ), 1.0, 6.0, ((0, 8), (1, 4)), jnp.float32),
        "adjoint_after": scatter_about(splits[2], (SHOTS, NX, NY, NZ), 1.0, 6.0, ((0, 8), (1, 4)), jnp.float32),
        "adjoint_now": scatter_about(splits[3], (SHOTS, NX, NY, NZ), 1.0, 6.0, ((0, 8), (1, 4)), jnp.float32),
        "speed_term": jnp.clip(jnp.exp(math.log(0.18) - 1.50407746 * jax.random.uniform(splits[4], (NX, NY, NZ), jnp.float32) ** level_of(splits[4], (NX, NY, NZ), ((0, 4),), -0.2, 0.2)), 0.04, 0.18),
        "wavelet": scatter_about(splits[5], (SHOTS, STEPS), 30.0, 180.0, ((0, 8),), jnp.float32),
        "source": draw_source(jax.random.fold_in(splits[9], 71), 0),
        "receivers": draw_receivers(jax.random.fold_in(splits[9], 71), 0),
        "traces": scatter_about(splits[8], (SHOTS, STEPS, RECV), 1.0, 6.0, ((0, 8), (2, 4)), jnp.float32),
    }


stencil_weights = (-205.0 / 72.0, 8.0 / 5.0, -1.0 / 5.0, 8.0 / 315.0, -1.0 / 560.0)


def laplace(extended):
    count = extended.shape[0] - 8
    width_y = extended.shape[1]
    width_z = extended.shape[2]
    centre = extended[4:4 + count]
    sided = jnp.pad(centre, ((0, 0), (4, 4), (4, 4)))
    total = (3.0 * stencil_weights[0]) * centre
    for step in range(1, 5):
        near = extended[4 + step:4 + step + count] + extended[4 - step:4 - step + count]
        near = near + sided[:, 4 + step:4 + step + width_y, 4:4 + width_z] + sided[:, 4 - step:4 - step + width_y, 4:4 + width_z]
        near = near + sided[:, 4:4 + width_y, 4 + step:4 + step + width_z] + sided[:, 4:4 + width_y, 4 - step:4 - step + width_z]
        total = total + stencil_weights[step] * near
    return total


def lap_zero(field):
    return laplace(jnp.pad(field, ((4, 4), (0, 0), (0, 0))))


def add_cells(field, flat, values):
    shape = field.shape
    return field.reshape(-1).at[flat].add(values).reshape(shape)


def reference(state_before, state_now, adjoint_after, adjoint_now, speed_term, wavelet, source, receivers, traces):
    scale = 1.0 / (8.0 * STEPS)

    def one_shot(grad, inputs):
        before, now, after, adj_now, wave, spot, recv, trace = inputs
        spot_flat = (spot[0] * (NY * NZ) + spot[1] * NZ + spot[2]).astype(jnp.int32)
        recv_flat = (recv[0] * (NY * NZ) + recv[1] * NZ + recv[2]).astype(jnp.int32)

        def forward(carry, amount):
            prev, cur = carry
            lapl = lap_zero(cur)
            nxt = add_cells(2.0 * cur - prev + speed_term * lapl, spot_flat, amount)
            return (cur, nxt), lapl

        _, stored = lax.scan(forward, (before, now), wave)

        def backward(carry, inputs):
            later, cur, total = carry
            lapl_t, row = inputs
            nxt = add_cells(2.0 * cur - later + speed_term * lap_zero(cur), recv_flat, row)
            return (cur, nxt, total + cur * lapl_t), None

        zero = jnp.zeros(now.shape, jnp.float32)
        (second, first, total), _ = lax.scan(backward, (after, adj_now, zero), (stored, trace), reverse=True)
        return grad + total * scale, (first, second)

    grad0 = jnp.zeros((NX, NY, NZ), jnp.float32)
    gradient, (firsts, seconds) = lax.scan(one_shot, grad0, (state_before, state_now, adjoint_after, adjoint_now, wavelet, source, receivers, traces))
    return firsts, seconds, gradient
```

```python
import functools

import jax
import jax.numpy as jnp
import ml_dtypes
import numpy as np
from jax import lax
from jax.experimental import pallas as pl
from jax.experimental.pallas import tpu as pltpu
from jax.sharding import PartitionSpec as P

weights = (-205.0 / 72.0, 8.0 / 5.0, -1.0 / 5.0, 8.0 / 315.0, -1.0 / 560.0)
reach = 4
VMEM = pltpu.VMEM
SMEM = pltpu.SMEM
limit = 20 * 1024 * 1024


def band(width, centre):
    out = np.zeros((width, width), np.float64)
    for k in range(1, reach + 1):
        out += weights[k] * (np.eye(width, k=k) + np.eye(width, k=-k))
    out += centre * np.eye(width)
    high = out.astype(np.float32).astype(ml_dtypes.bfloat16)
    low = (out - high.astype(np.float64)).astype(np.float32).astype(ml_dtypes.bfloat16)
    return high, low


def band_right(width):
    high, low = band(width, 3.0 * weights[0])
    return np.block([[high, low], [high, np.zeros_like(low)]])


def band_left(width):
    high, low = band(width, 0.0)
    return np.block([[high, high], [low, np.zeros_like(low)]])


def split(v):
    high = v.astype(jnp.bfloat16)
    low = (v - high.astype(jnp.float32)).astype(jnp.bfloat16)
    return high, low


def fill_halo(parity, even, odd, halo):
    @pl.when(parity == 0)
    def _():
        halo[:reach] = odd[...]
        halo[reach:] = even[...]

    @pl.when(parity != 0)
    def _():
        halo[:reach] = even[...]
        halo[reach:] = odd[...]


def emit_edges(parity, field, even, odd):
    count = field.shape[0]

    @pl.when(parity == 0)
    def _():
        even[...] = field[count - reach :]
        odd[...] = field[:reach]

    @pl.when(parity != 0)
    def _():
        even[...] = field[:reach]
        odd[...] = field[count - reach :]


def laplace_planes(cur, halo, right, left, put):
    count, width_y, width_z = cur.shape

    def plane(i):
        if i < 0:
            return halo[reach + i]
        if i >= count:
            return halo[reach + i - count]
        return cur[i]

    for x in range(0, count, 2):
        v = [cur[x], cur[x + 1]]
        (h0, l0), (h1, l1) = split(v[0]), split(v[1])
        rows = jnp.concatenate(
            [jnp.concatenate([h0, l0], axis=1), jnp.concatenate([h1, l1], axis=1)], axis=0
        )
        along = jnp.dot(rows, right[...], preferred_element_type=jnp.float32)
        cols = jnp.concatenate(
            [jnp.concatenate([h0, h1], axis=1), jnp.concatenate([l0, l1], axis=1)], axis=0
        )
        across = jnp.dot(left[...], cols, preferred_element_type=jnp.float32)
        for j in range(2):
            rows_j = slice(j * width_y, (j + 1) * width_y)
            lanes_j = slice(j * width_z, (j + 1) * width_z)
            lap = along[rows_j, :width_z] + along[rows_j, width_z:]
            lap = lap + (across[:width_y, lanes_j] + across[width_y:, lanes_j])
            for k in range(1, reach + 1):
                lap = lap + weights[k] * (plane(x + j + k) + plane(x + j - k))
            put(x + j, v[j], lap)


def forward_kernel(parts, *refs):
    it = iter(refs)
    meta, wave, cur, even, odd, right, left = [next(it) for _ in range(7)]
    moves, stores, adds, opens = parts["moves"], parts["stores"], parts["adds"], parts["opens"]
    prev, speed = (next(it), next(it)) if moves else (None, None)
    late = next(it) if adds else None
    acc_in = next(it) if adds and not opens else None
    first, lap_first = (next(it), next(it)) if not moves else (None, None)
    nxt, even_out, odd_out = [next(it) for _ in range(3)] if moves else (None,) * 3
    lap_out = next(it) if stores else None
    acc_out = next(it) if adds and moves else None
    send, keep = (next(it), next(it)) if not moves else (None, None)
    halo = next(it)
    total = next(it) if not moves else None
    fill_halo(meta[0], even, odd, halo)

    def put(x, v, lap):
        if moves:
            nxt[x] = 2.0 * v - prev[x] + speed[x] * lap
        if stores:
            lap_out[x] = lap
        if adds:
            value = lap * late[x]
            if not opens:
                value = value + acc_in[x]
            if moves:
                acc_out[x] = value
            else:
                total[x] = (value + first[x] * lap_first[x]) * parts["scale"]

    laplace_planes(cur, halo, right, left, put)
    if moves:
        row, col, lane = meta[1], meta[2], meta[3]

        @pl.when((row >= 0) & (row < cur.shape[0]))
        def _():
            tile = pl.ds(pl.multiple_of((col // 8) * 8, 8), 8)
            shape = (8, cur.shape[2])
            hit = (lax.broadcasted_iota(jnp.int32, shape, 0) == col % 8) & (
                lax.broadcasted_iota(jnp.int32, shape, 1) == lane
            )
            nxt[row, tile, :] = nxt[row, tile, :] + jnp.where(hit, wave[parts["step"]], 0.0)

        emit_edges(meta[0], nxt, even_out, odd_out)
    else:
        chunk = send.shape[2]
        mine = meta[4] % 2
        for j in range(send.shape[0]):
            away = pl.multiple_of((2 * j + 1 - mine) * chunk, 8)
            here = pl.multiple_of((2 * j + mine) * chunk, 8)
            send[j] = total[:, pl.ds(away, chunk), :]
            keep[j] = total[:, pl.ds(here, chunk), :]


def adjoint_kernel(parts, *refs):
    it = iter(refs)
    meta, cur, later, speed, even, odd, inject, right, left = [next(it) for _ in range(9)]
    adds, edges = parts["adds"], parts["edges"]
    lap_of, acc_in = (next(it), next(it)) if adds else (None, None)
    nxt = next(it)
    even_out, odd_out = (next(it), next(it)) if edges else (None, None)
    acc_out = next(it) if adds else None
    halo = next(it)
    fill_halo(meta[0], even, odd, halo)
    width_y = cur.shape[1]

    def put(x, v, lap):
        added = inject[pl.ds(x * width_y * 8 + parts["time"], width_y, stride=8), :]
        nxt[x] = 2.0 * v - later[x] + speed[x] * lap + added
        if adds:
            acc_out[x] = acc_in[x] + v * lap_of[x]

    laplace_planes(cur, halo, right, left, put)
    if edges:
        emit_edges(meta[0], nxt, even_out, odd_out)


def scatter_kernel(meta, where_to, blocks, out):
    slabs, steps, per = blocks.shape
    group = 4
    zero_rows = 64 * 8

    @pl.loop(0, out.shape[0] // zero_rows)
    def _(i):
        out[pl.ds(pl.multiple_of(i * zero_rows, 8), zero_rows), :] = jnp.zeros(
            (zero_rows, 128), jnp.float32
        )

    rest = out.shape[0] % zero_rows
    if rest:
        out[out.shape[0] - rest :, :] = jnp.zeros((rest, 128), jnp.float32)
    lanes = lax.broadcasted_iota(jnp.int32, (8, 128), 1)
    for d in range(slabs):
        base = (meta[5] ^ d) * per
        for part in range(per // 128):
            block = blocks[d, :, part * 128 : (part + 1) * 128]

            @pl.loop(0, 128 // group)
            def _(i):
                tiles, terms, slots = [], [], []
                for u in range(group):
                    j = i * group + u
                    flat = where_to[base + part * 128 + j]
                    lane = flat & 127
                    tile = flat >> 7
                    moved = pltpu.roll(block, (lane - j) & 127, 1)
                    tiles.append(tile)
                    terms.append(jnp.where(lanes == lane, moved, 0.0))
                    slots.append(pl.ds(pl.multiple_of(tile * 8, 8), 8))
                held = [out[slot, :] for slot in slots]
                for u in range(group):
                    value = held[u] + terms[u]
                    for w in range(u):
                        same = (tiles[w] == tiles[u]).astype(jnp.float32)
                        value = value + terms[w] * same
                    held[u] = value
                for u in range(group):
                    out[slots[u], :] = held[u]


def vmem(*shape):
    return VMEM(shape, jnp.float32)


def vmem_spec():
    return pl.BlockSpec(memory_space=VMEM)


def smem_spec():
    return pl.BlockSpec(memory_space=SMEM)


def call(kernel, specs, outs, scratch, name, cycles):
    return pl.pallas_call(
        kernel,
        out_shape=outs,
        in_specs=specs,
        out_specs=jax.tree.map(lambda _: vmem_spec(), outs),
        scratch_shapes=scratch,
        compiler_params=pltpu.CompilerParams(vmem_limit_bytes=limit),
        cost_estimate=pl.CostEstimate(flops=cycles, bytes_accessed=4 << 20, transcendentals=0),
        name=name,
    )


def pair_swap(count, start):
    pairs = []
    for i in range(start, count - 1, 2):
        pairs += [(i, i + 1), (i + 1, i)]
    return pairs


def body(
    state_before,
    state_now,
    adjoint_after,
    adjoint_now,
    speed_term,
    wavelet,
    source,
    receivers,
    traces,
):
    count, width_y, width_z = speed_term.shape
    steps = wavelet.shape[1]
    slabs = lax.axis_size("slab")
    shots = lax.axis_size("shot")
    slab = lax.axis_index("slab")
    shot = lax.axis_index("shot")
    half = steps // 2
    scale = 1.0 / (8.0 * steps)
    parity = slab % 2
    even_pairs, odd_pairs = pair_swap(slabs, 0), pair_swap(slabs, 1)

    def swap(edges):
        return (
            lax.ppermute(edges[0], "slab", even_pairs),
            lax.ppermute(edges[1], "slab", odd_pairs),
        )

    def first_edges(field):
        top = count - reach
        return (
            lax.dynamic_slice_in_dim(field, jnp.where(parity == 0, top, 0), reach, 0),
            lax.dynamic_slice_in_dim(field, jnp.where(parity == 0, 0, top), reach, 0),
        )

    right = jnp.asarray(band_right(width_z))
    left = jnp.asarray(band_left(width_y))
    spot = source[0]
    meta = jnp.stack([parity, spot[0] - slab * count, spot[1], spot[2], shot, slab]).astype(jnp.int32)
    wave = wavelet[0]
    listen = receivers[0]
    depth = listen[0] - slab * count
    inside = (depth >= 0) & (depth < count)
    flat = depth * (width_y * width_z) + listen[1] * width_z + listen[2]
    where_to = jnp.where(inside, flat, count * width_y * width_z)

    blocks = traces[0][None]
    bit = 1
    while bit < slabs:
        other = lax.ppermute(blocks, "slab", [(i, i ^ bit) for i in range(slabs)])
        blocks = jnp.concatenate([blocks, other], axis=0)
        bit *= 2

    field = vmem(count, width_y, width_z)
    edge = vmem(reach, width_y, width_z)
    halo = vmem(2 * reach, width_y, width_z)
    p = {-1: state_before[0], 0: state_now[0]}
    q = {steps + 1: adjoint_after[0], steps: adjoint_now[0]}
    laps = {}
    acc = None
    p_halo = swap(first_edges(p[0]))
    q_halo = swap(first_edges(q[steps]))
    inject = call(
        scatter_kernel,
        [smem_spec(), smem_spec(), vmem_spec()],
        vmem((count * width_y + 1) * 8, width_z),
        [],
        "receivers",
        1000,
    )(meta, where_to, blocks)

    for k in range(steps):
        last = k == steps - 1
        parts = dict(moves=not last, stores=k < half, adds=k >= half, opens=k == half, step=k, scale=scale)
        args = [meta, wave, p[k], *p_halo, right, left]
        outs, scratch = [], [halo]
        if not last:
            args += [p[k - 1], speed_term]
            outs += [field, edge, edge]
        if parts["stores"]:
            outs += [field]
        if parts["adds"]:
            args += [q[k + 1]]
            if not parts["opens"]:
                args += [acc]
            if not last:
                outs += [field]
        if last:
            args += [q[1], laps[0]]
            piece = jax.ShapeDtypeStruct((shots // 2, count, width_y // shots, width_z), jnp.float32)
            outs += [piece, piece]
            scratch = scratch + [field]
        specs = [smem_spec(), smem_spec()] + [vmem_spec()] * (len(args) - 2)
        got = call(functools.partial(forward_kernel, parts), specs, outs, scratch, "forward", 1000)(*args)
        if not last:
            p[k + 1] = got[0]
            p_halo = swap(got[1:3])
            if parts["stores"]:
                laps[k] = got[3]
            else:
                acc = got[3]
        else:
            send, kept = got
            arrived = lax.ppermute(send, "shot", [(i, i ^ 1) for i in range(shots)])
            paired = kept + arrived
            mine = shot // 2
            gradient = lax.dynamic_index_in_dim(paired, mine, 0, keepdims=False)
            for m in range(1, shots // 2):
                piece = lax.dynamic_index_in_dim(paired, mine ^ m, 0, keepdims=False)
                gradient = gradient + lax.ppermute(
                    piece, "shot", [(i, i ^ (2 * m)) for i in range(shots)]
                )

        t = steps - 1 - k
        parts = dict(adds=k >= half and not last, edges=not last, time=t)
        args = [meta, q[t + 1], q[t + 2], speed_term, *q_halo, inject, right, left]
        outs = [jax.ShapeDtypeStruct((count, width_y, width_z), jnp.float32) if last else field]
        if parts["adds"]:
            args += [laps[t], acc]
        if not last:
            outs += [edge, edge]
        if parts["adds"]:
            outs += [field]
        specs = [smem_spec()] + [vmem_spec()] * (len(args) - 1)
        got = call(functools.partial(adjoint_kernel, parts), specs, outs, [halo], "adjoint", 1000)(*args)
        q[t] = got[0]
        if not last:
            q_halo = swap(got[1:3])
        if parts["adds"]:
            acc = got[3]

    return (q[0][None], q[1][None], gradient)


def solution(mesh):
    return jax.shard_map(
        body,
        mesh=mesh,
        in_specs=(
            P("shot", "slab", None, None),
            P("shot", "slab", None, None),
            P("shot", "slab", None, None),
            P("shot", "slab", None, None),
            P("slab", None, None),
            P("shot", None),
            P("shot", None),
            P("shot", None, None),
            P("shot", None, "slab"),
        ),
        out_specs=(
            P("shot", "slab", None, None),
            P("shot", "slab", None, None),
            P("slab", "shot", None),
        ),
        check_vma=False,
    )
```

```python
import functools

import jax
import jax.numpy as jnp
import ml_dtypes
import numpy as np
from jax import lax
from jax.experimental import pallas as pl
from jax.experimental.pallas import tpu as pltpu
from jax.sharding import PartitionSpec as P

weights = (-205.0 / 72.0, 8.0 / 5.0, -1.0 / 5.0, 8.0 / 315.0, -1.0 / 560.0)
reach = 4
VMEM = pltpu.VMEM
SMEM = pltpu.SMEM
HBM = pltpu.HBM
limit = 12 * 1024 * 1024


def band(width, centre):
    out = np.zeros((width, width), np.float64)
    for k in range(1, reach + 1):
        out += weights[k] * (np.eye(width, k=k) + np.eye(width, k=-k))
    out += centre * np.eye(width)
    high = out.astype(np.float32).astype(ml_dtypes.bfloat16)
    low = (out - high.astype(np.float64)).astype(np.float32).astype(ml_dtypes.bfloat16)
    return high, low


def band_right(width):
    high, low = band(width, 3.0 * weights[0])
    return np.block([[high, low], [high, np.zeros_like(low)]])


def band_left(width):
    high, low = band(width, 0.0)
    return np.block([[high, high], [low, np.zeros_like(low)]])


def split(v):
    high = v.astype(jnp.bfloat16)
    low = (v - high.astype(jnp.float32)).astype(jnp.bfloat16)
    return high, low


def fill_halo(parity, even, odd, halo):
    @pl.when(parity == 0)
    def _():
        halo[:reach] = odd[...]
        halo[reach:] = even[...]

    @pl.when(parity != 0)
    def _():
        halo[:reach] = even[...]
        halo[reach:] = odd[...]


def emit_edges(parity, field, even, odd):
    count = field.shape[0]

    @pl.when(parity == 0)
    def _():
        even[...] = field[count - reach :]
        odd[...] = field[:reach]

    @pl.when(parity != 0)
    def _():
        even[...] = field[:reach]
        odd[...] = field[count - reach :]


def laplace_planes(cur, halo, right, left, put):
    count, width_y, width_z = cur.shape

    def plane(i):
        if i < 0:
            return halo[reach + i]
        if i >= count:
            return halo[reach + i - count]
        return cur[i]

    for x in range(0, count, 2):
        v = [cur[x], cur[x + 1]]
        (h0, l0), (h1, l1) = split(v[0]), split(v[1])
        rows = jnp.concatenate(
            [jnp.concatenate([h0, l0], axis=1), jnp.concatenate([h1, l1], axis=1)], axis=0
        )
        along = jnp.dot(rows, right[...], preferred_element_type=jnp.float32)
        cols = jnp.concatenate(
            [jnp.concatenate([h0, h1], axis=1), jnp.concatenate([l0, l1], axis=1)], axis=0
        )
        across = jnp.dot(left[...], cols, preferred_element_type=jnp.float32)
        for j in range(2):
            rows_j = slice(j * width_y, (j + 1) * width_y)
            lanes_j = slice(j * width_z, (j + 1) * width_z)
            lap = along[rows_j, :width_z] + along[rows_j, width_z:]
            lap = lap + (across[:width_y, lanes_j] + across[width_y:, lanes_j])
            for k in range(1, reach + 1):
                lap = lap + weights[k] * (plane(x + j + k) + plane(x + j - k))
            put(x + j, v[j], lap)


def forward_kernel(parts, *refs):
    it = iter(refs)
    cur, even, odd, right, left = [next(it) for _ in range(5)]
    moves, stores, adds, opens = parts["moves"], parts["stores"], parts["adds"], parts["opens"]
    prev, speed, source, wave = [next(it) for _ in range(4)] if moves else (None,) * 4
    late = next(it) if adds else None
    acc_in = next(it) if adds and not opens else None
    first, lap_first = (next(it), next(it)) if not moves else (None, None)
    nxt, even_out, odd_out = [next(it) for _ in range(3)] if moves else (None,) * 3
    lap_out = next(it) if stores else None
    acc_out = next(it) if adds and moves else None
    send, keep = (next(it), next(it)) if not moves else (None, None)
    halo = next(it)
    if moves:
        spot_smem, wave_smem, spot_sem, wave_sem = [next(it) for _ in range(4)]
        spot_copy = pltpu.make_async_copy(source, spot_smem, spot_sem)
        wave_copy = pltpu.make_async_copy(wave, wave_smem, wave_sem)
        spot_copy.start()
        wave_copy.start()
    total = next(it) if not moves else None
    slab = lax.axis_index("slab")
    parity = slab % 2
    fill_halo(parity, even, odd, halo)

    def put(x, v, lap):
        if moves:
            nxt[x] = 2.0 * v - prev[x] + speed[x] * lap
        if stores:
            lap_out[x] = lap
        if adds:
            value = lap * late[x]
            if not opens:
                value = value + acc_in[x]
            if moves:
                acc_out[x] = value
            else:
                total[x] = (value + first[x] * lap_first[x]) * parts["scale"]

    laplace_planes(cur, halo, right, left, put)
    if moves:
        spot_copy.wait()
        wave_copy.wait()
        row = spot_smem[0, 0] - slab * cur.shape[0]
        col, lane = spot_smem[0, 1], spot_smem[0, 2]

        @pl.when((row >= 0) & (row < cur.shape[0]))
        def _():
            tile = pl.ds(pl.multiple_of((col // 8) * 8, 8), 8)
            shape = (8, cur.shape[2])
            hit = (lax.broadcasted_iota(jnp.int32, shape, 0) == col % 8) & (
                lax.broadcasted_iota(jnp.int32, shape, 1) == lane
            )
            nxt[row, tile, :] = nxt[row, tile, :] + jnp.where(hit, wave_smem[0, parts["step"]], 0.0)

        emit_edges(parity, nxt, even_out, odd_out)
    else:
        chunk = send.shape[2]
        mine = lax.axis_index("shot") % 2
        for j in range(send.shape[0]):
            away = pl.multiple_of((2 * j + 1 - mine) * chunk, 8)
            here = pl.multiple_of((2 * j + mine) * chunk, 8)
            send[j] = total[:, pl.ds(away, chunk), :]
            keep[j] = total[:, pl.ds(here, chunk), :]


def adjoint_kernel(parts, *refs):
    it = iter(refs)
    cur, later, speed, even, odd, inject, right, left = [next(it) for _ in range(8)]
    adds, last = parts["adds"], parts["last"]
    lap_of, acc_in = (next(it), next(it)) if adds else (None, None)
    nxt = next(it)
    even_out, odd_out = (next(it), next(it)) if not last else (None, None)
    cur_out = next(it) if last else None
    acc_out = next(it) if adds else None
    halo = next(it)
    parity = lax.axis_index("slab") % 2
    fill_halo(parity, even, odd, halo)
    width_y = cur.shape[1]
    field, copies = nxt, []
    if last:
        field, sems, cur_sem = next(it), next(it), next(it)
        copies.append(pltpu.make_async_copy(cur, cur_out, cur_sem))
        copies[0].start()

    def put(x, v, lap):
        added = inject[pl.ds(x * width_y * 8 + parts["time"], width_y, stride=8), :]
        field[x] = 2.0 * v - later[x] + speed[x] * lap + added
        if adds:
            acc_out[x] = acc_in[x] + v * lap_of[x]
        if last and x % 2:
            both = pl.ds(x - 1, 2)
            copy = pltpu.make_async_copy(field.at[both], nxt.at[both], sems.at[x // 2])
            copy.start()
            copies.append(copy)

    laplace_planes(cur, halo, right, left, put)
    if not last:
        emit_edges(parity, field, even_out, odd_out)
    for copy in copies:
        copy.wait()


def edges_kernel(*refs):
    fields, outs, sems = refs[:2], refs[2:6], refs[6]
    parity = lax.axis_index("slab") % 2
    top = fields[0].shape[0] - reach
    starts = (top * (1 - parity), top * parity)
    copies = []
    for i in range(4):
        rows = pl.ds(starts[i % 2], reach)
        copies.append(pltpu.make_async_copy(fields[i // 2].at[rows], outs[i], sems.at[i]))
        copies[-1].start()
    for copy in copies:
        copy.wait()


def load_kernel(listen, *refs):
    fields, outs, where_to, sems = refs[:5], refs[5:10], refs[10], refs[11]
    copies = [pltpu.make_async_copy(fields[i], outs[i], sems.at[i]) for i in range(5)]
    for copy in copies:
        copy.start()
    count, width_y, width_z = fields[0].shape
    depth = listen[0:1, :] - lax.axis_index("slab") * count
    inside = (depth >= 0) & (depth < count)
    flat = depth * (width_y * width_z) + listen[1:2, :] * width_z + listen[2:3, :]
    where_to[...] = jnp.where(inside, flat, count * width_y * width_z)
    for copy in copies:
        copy.wait()


def scatter_kernel(where_to, *refs):
    blocks, out = refs[:-1], refs[-1]
    steps, per = blocks[0].shape[-2:]
    group, groups = 4, 8
    zero_rows = 64 * 8
    slab = lax.axis_index("slab")

    @pl.loop(0, out.shape[0] // zero_rows)
    def _(i):
        out[pl.ds(pl.multiple_of(i * zero_rows, 8), zero_rows), :] = jnp.zeros(
            (zero_rows, 128), jnp.float32
        )

    rest = out.shape[0] % zero_rows
    if rest:
        out[out.shape[0] - rest :, :] = jnp.zeros((rest, 128), jnp.float32)
    lanes = lax.broadcasted_iota(jnp.int32, (8, 128), 1)
    d = 0
    for held_blocks in blocks:
        for e in range(held_blocks.shape[0]):
            base = (slab ^ d) * per
            d += 1
            for part in range(per // 128):
                block = held_blocks[e, :, part * 128 : (part + 1) * 128]

                @pl.loop(0, 128 // (group * groups))
                def _(i):
                    tiles, terms, slots = [], [], []
                    for u in range(group * groups):
                        j = i * (group * groups) + u
                        flat = where_to[0, base + part * 128 + j]
                        lane = flat & 127
                        tile = flat >> 7
                        moved = pltpu.roll(block, (lane - j) & 127, 1)
                        tiles.append(tile)
                        terms.append(jnp.where(lanes == lane, moved, 0.0))
                        slots.append(pl.ds(pl.multiple_of(tile * 8, 8), 8))
                    for g in range(groups):
                        own = range(g * group, (g + 1) * group)
                        held = {u: out[slots[u], :] for u in own}
                        for u in own:
                            value = held[u] + terms[u]
                            for w in range(g * group, u):
                                same = (tiles[w] == tiles[u]).astype(jnp.float32)
                                value = value + terms[w] * same
                            held[u] = value
                        for u in own:
                            out[slots[u], :] = held[u]


def pair_kernel(keep, arrived, *outs):
    mine = lax.axis_index("shot") // 2
    for m in range(len(outs)):
        outs[m][...] = keep[mine ^ m] + arrived[mine ^ m]


def sum_kernel(*refs):
    total = refs[0][...]
    for ref in refs[1:-1]:
        total = total + ref[...]
    refs[-1][...] = total


def vmem(*shape):
    return VMEM(shape, jnp.float32)


def plain(*shape):
    return jax.ShapeDtypeStruct(shape, jnp.float32)


def call(name, kernel, args, outs, scratch=(), spaces=None, out_spaces=None, micros=2):
    spec = lambda space: pl.BlockSpec(memory_space=space)
    spaces = spaces or {}
    args = [
        pltpu.with_memory_space_constraint(arg, HBM) if spaces.get(i) is HBM else arg
        for i, arg in enumerate(args)
    ]
    out_spaces = out_spaces or {}
    return pl.pallas_call(
        kernel,
        out_shape=outs,
        in_specs=[spec(spaces.get(i, VMEM)) for i in range(len(args))],
        out_specs=[spec(out_spaces.get(i, VMEM)) for i in range(len(outs))],
        scratch_shapes=scratch,
        compiler_params=pltpu.CompilerParams(vmem_limit_bytes=limit),
        cost_estimate=pl.CostEstimate(
            flops=micros * 1000000000, bytes_accessed=micros << 16, transcendentals=0
        ),
        name=name,
    )(*args)


def pair_swap(count, start):
    pairs = []
    for i in range(start, count - 1, 2):
        pairs += [(i, i + 1), (i + 1, i)]
    return pairs


def body(
    state_before,
    state_now,
    adjoint_after,
    adjoint_now,
    speed_term,
    wavelet,
    source,
    receivers,
    traces,
):
    count, width_y, width_z = speed_term.shape
    steps = wavelet.shape[1]
    slabs = lax.axis_size("slab")
    shots = lax.axis_size("shot")
    half = steps // 2
    scale = 1.0 / (8.0 * steps)
    even_pairs, odd_pairs = pair_swap(slabs, 0), pair_swap(slabs, 1)
    field = vmem(count, width_y, width_z)
    edge = vmem(reach, width_y, width_z)
    halo = vmem(2 * reach, width_y, width_z)
    dma = pltpu.SemaphoreType.DMA

    def swap(even, odd):
        return lax.ppermute(even, "slab", even_pairs), lax.ppermute(odd, "slab", odd_pairs)

    right = jnp.asarray(band_right(width_z))
    left = jnp.asarray(band_left(width_y))
    listen = receivers[0]

    blocks = [traces]
    bit = 1
    while bit < slabs:
        held = blocks[0] if len(blocks) == 1 else jnp.concatenate(blocks, axis=0)
        blocks.append(lax.ppermute(held, "slab", [(i, i ^ bit) for i in range(slabs)]))
        bit *= 2

    p0_even, p0_odd, q8_even, q8_odd = call(
        "edges", edges_kernel, [state_now[0], adjoint_now[0]], [edge] * 4, [dma((4,))], {0: HBM, 1: HBM}
    )
    p_halo = swap(p0_even, p0_odd)
    q_halo = swap(q8_even, q8_odd)
    fields = [state_before[0], state_now[0], adjoint_after[0], adjoint_now[0], speed_term]
    *loaded, where_to = call(
        "load",
        load_kernel,
        [listen, *fields],
        [field] * 5 + [VMEM((1, listen.shape[1]), jnp.int32)],
        [dma((5,))],
        {1 + i: HBM for i in range(5)},
        micros=1,
    )
    (inject,) = call(
        "receivers",
        scatter_kernel,
        [where_to, *blocks],
        [vmem((count * width_y + 1) * 8, width_z)],
        (),
        {0: SMEM},
        micros=1,
    )
    p = {-1: loaded[0], 0: loaded[1]}
    q = {steps + 1: loaded[2], steps: loaded[3]}
    speed = loaded[4]
    laps = {}
    acc = None

    for k in range(steps):
        last = k == steps - 1
        parts = dict(moves=not last, stores=k < half, adds=k >= half, opens=k == half, step=k, scale=scale)
        args = [p[k], *p_halo, right, left]
        outs, scratch, spaces = [], [halo], {}
        if not last:
            spaces = {len(args) + 2: HBM, len(args) + 3: HBM}
            args += [p[k - 1], speed, source, wavelet]
            outs += [field, edge, edge]
            scratch += [SMEM(source.shape, jnp.int32), SMEM(wavelet.shape, jnp.float32), dma, dma]
        if parts["stores"]:
            outs += [field]
        if parts["adds"]:
            args += [q[k + 1]]
            if not parts["opens"]:
                args += [acc]
            if not last:
                outs += [field]
        if last:
            args += [q[1], laps[0]]
            piece = vmem(shots // 2, count, width_y // shots, width_z)
            outs += [piece, piece]
            scratch += [field]
        got = call(
            "forward", functools.partial(forward_kernel, parts), args, outs, scratch, spaces,
            micros=0 if last else 2,
        )
        if not last:
            p[k + 1] = got[0]
            p_halo = swap(*got[1:3])
            if parts["stores"]:
                laps[k] = got[3]
            else:
                acc = got[3]
        else:
            send, kept = got
            arrived = lax.ppermute(send, "shot", [(i, i ^ 1) for i in range(shots)])
            piece = vmem(count, width_y // shots, width_z)
            pieces = call("pair", pair_kernel, [kept, arrived], [piece] * (shots // 2), micros=0)
            terms = [pieces[0]] + [
                lax.ppermute(pieces[m], "shot", [(i, i ^ (2 * m)) for i in range(shots)])
                for m in range(1, shots // 2)
            ]
            (gradient,) = call("sum", sum_kernel, terms, [plain(count, width_y // shots, width_z)], micros=0)

        t = steps - 1 - k
        parts = dict(adds=k >= half and not last, last=last, time=t)
        args = [q[t + 1], q[t + 2], speed, *q_halo, inject, right, left]
        outs, scratch, out_spaces = [field, edge, edge], [halo], {}
        if last:
            outs = [plain(count, width_y, width_z)] * 2
            scratch += [field, dma((count // 2,)), dma]
            out_spaces = {0: HBM, 1: HBM}
        if parts["adds"]:
            args += [laps[t], acc]
            outs += [field]
        got = call(
            "adjoint", functools.partial(adjoint_kernel, parts), args, outs, scratch, None, out_spaces,
            micros=30 if last else 2,
        )
        q[t] = got[0]
        if last:
            opening, second = got
        else:
            q_halo = swap(*got[1:3])
        if parts["adds"]:
            acc = got[3]

    return (opening[None], second[None], gradient)


def solution(mesh):
    return jax.shard_map(
        body,
        mesh=mesh,
        in_specs=(
            P("shot", "slab", None, None),
            P("shot", "slab", None, None),
            P("shot", "slab", None, None),
            P("shot", "slab", None, None),
            P("slab", None, None),
            P("shot", None),
            P("shot", None),
            P("shot", None, None),
            P("shot", None, "slab"),
        ),
        out_specs=(
            P("shot", "slab", None, None),
            P("shot", "slab", None, None),
            P("slab", "shot", None),
        ),
        check_vma=False,
    )
```

```python
import functools

import jax
import jax.numpy as jnp
import ml_dtypes
import numpy as np
from jax import lax
from jax.experimental import pallas as pl
from jax.experimental.pallas import tpu as pltpu
from jax.sharding import PartitionSpec as P

weights = (-205.0 / 72.0, 8.0 / 5.0, -1.0 / 5.0, 8.0 / 315.0, -1.0 / 560.0)
reach = 4
VMEM = pltpu.VMEM
SMEM = pltpu.SMEM
HBM = pltpu.HBM
limit = 12 * 1024 * 1024


def band(width, centre):
    out = np.zeros((width, width), np.float64)
    for k in range(1, reach + 1):
        out += weights[k] * (np.eye(width, k=k) + np.eye(width, k=-k))
    out += centre * np.eye(width)
    high = out.astype(np.float32).astype(ml_dtypes.bfloat16)
    low = (out - high.astype(np.float64)).astype(np.float32).astype(ml_dtypes.bfloat16)
    return high, low


def band_right(width):
    high, low = band(width, 3.0 * weights[0])
    return np.block([[high, low], [high, np.zeros_like(low)]])


def band_left(width):
    high, low = band(width, 0.0)
    return np.block([[high, high], [low, np.zeros_like(low)]])


def split(v):
    high = v.astype(jnp.bfloat16)
    low = (v - high.astype(jnp.float32)).astype(jnp.bfloat16)
    return high, low


def fill_halo(parity, even, odd, halo):
    @pl.when(parity == 0)
    def _():
        halo[:reach] = odd[...]
        halo[reach:] = even[...]

    @pl.when(parity != 0)
    def _():
        halo[:reach] = even[...]
        halo[reach:] = odd[...]


def emit_edge(upper, outer, out):
    @pl.when(upper)
    def _():
        out[...] = outer[reach:]

    @pl.when(jnp.logical_not(upper))
    def _():
        out[...] = outer[:reach]


def rows_of(count, border):
    if border:
        return list(range(reach)) + list(range(count - reach, count))
    return list(range(reach, count - reach))


def laplace_rows(border, inner, outer, halo, right, left, put):
    count, width_y, width_z = inner.shape[0] + 2 * reach, inner.shape[1], inner.shape[2]

    def plane(i):
        if i < 0:
            return halo[reach + i]
        if i < reach:
            return outer[i]
        if i < count - reach:
            return inner[i - reach]
        if i < count:
            return outer[i - count + 2 * reach]
        return halo[reach + i - count]

    rows = rows_of(count, border)
    for i in range(0, len(rows), 2):
        x = rows[i]
        v = [plane(x), plane(x + 1)]
        (h0, l0), (h1, l1) = split(v[0]), split(v[1])
        flat = jnp.concatenate(
            [jnp.concatenate([h0, l0], axis=1), jnp.concatenate([h1, l1], axis=1)], axis=0
        )
        along = jnp.dot(flat, right[...], preferred_element_type=jnp.float32)
        cols = jnp.concatenate(
            [jnp.concatenate([h0, h1], axis=1), jnp.concatenate([l0, l1], axis=1)], axis=0
        )
        across = jnp.dot(left[...], cols, preferred_element_type=jnp.float32)
        for j in range(2):
            rows_j = slice(j * width_y, (j + 1) * width_y)
            lanes_j = slice(j * width_z, (j + 1) * width_z)
            lap = along[rows_j, :width_z] + along[rows_j, width_z:]
            lap = lap + (across[:width_y, lanes_j] + across[width_y:, lanes_j])
            for k in range(1, reach + 1):
                lap = lap + weights[k] * (plane(x + j + k) + plane(x + j - k))
            put(i + j, x + j, v[j], lap)


def forward_kernel(parts, *refs):
    it = iter(refs)
    border, moves, stores = parts["border"], parts["moves"], parts["stores"]
    adds, opens = parts["adds"], parts["opens"]
    inner, outer = next(it), next(it)
    even, odd = (next(it), next(it)) if border else (None, None)
    right, left = next(it), next(it)
    prev, speed, source, wave = [next(it) for _ in range(4)] if moves else (None,) * 4
    late = next(it) if adds else None
    acc_in = next(it) if adds and not opens else None
    first, lap_first = (next(it), next(it)) if not moves else (None, None)
    nxt = next(it) if moves else None
    edge_out = next(it) if moves or not border else None
    lap_out = next(it) if stores else None
    acc_out = next(it) if adds and moves else None
    send, keep = (next(it), next(it)) if not moves else (None, None)
    halo = next(it) if border else None
    if moves:
        spot_smem, wave_smem, spot_sem, wave_sem = [next(it) for _ in range(4)]
        spot_copy = pltpu.make_async_copy(source, spot_smem, spot_sem)
        wave_copy = pltpu.make_async_copy(wave, wave_smem, wave_sem)
        spot_copy.start()
        wave_copy.start()
    total = next(it) if not moves else None
    slab = lax.axis_index("slab")
    parity = slab % 2
    count = inner.shape[0] + 2 * reach
    if border:
        fill_halo(parity, even, odd, halo)
    else:
        emit_edge(parity != 0, outer, edge_out)

    def put(i, x, v, lap):
        if moves:
            nxt[i] = 2.0 * v - prev[i] + speed[x] * lap
        if stores:
            lap_out[i] = lap
        if adds:
            value = lap * late[i]
            if not opens:
                value = value + acc_in[i]
            if moves:
                acc_out[i] = value
            else:
                total[i] = (value + first[i] * lap_first[i]) * parts["scale"]

    laplace_rows(border, inner, outer, halo, right, left, put)
    if moves:
        spot_copy.wait()
        wave_copy.wait()
        row = spot_smem[0, 0] - slab * count
        col, lane = spot_smem[0, 1], spot_smem[0, 2]
        within = (row >= reach) & (row < count - reach)
        place = row - reach
        if border:
            within = (row >= 0) & (row < count) & jnp.logical_not(within)
            place = jnp.where(row < reach, row, row - count + 2 * reach)

        @pl.when(within)
        def _():
            tile = pl.ds(pl.multiple_of((col // 8) * 8, 8), 8)
            shape = (8, inner.shape[2])
            hit = (lax.broadcasted_iota(jnp.int32, shape, 0) == col % 8) & (
                lax.broadcasted_iota(jnp.int32, shape, 1) == lane
            )
            added = jnp.where(hit, wave_smem[0, parts["step"]], 0.0)
            nxt[place, tile, :] = nxt[place, tile, :] + added

        if border:
            emit_edge(parity == 0, nxt, edge_out)
    else:
        chunk = send.shape[2]
        mine = lax.axis_index("shot") % 2
        for j in range(send.shape[0]):
            away = pl.multiple_of((2 * j + 1 - mine) * chunk, 8)
            here = pl.multiple_of((2 * j + mine) * chunk, 8)
            send[j] = total[:, pl.ds(away, chunk), :]
            keep[j] = total[:, pl.ds(here, chunk), :]


def part_copies(border, part, whole, sems, to_whole):
    count = whole.shape[0]
    if border:
        pieces = [(0, 0, reach), (reach, count - reach, reach)]
    else:
        pieces = [(0, reach, count - 2 * reach)]
    copies = []
    for n, (i, x, rows) in enumerate(pieces):
        near, far = part.at[pl.ds(i, rows)], whole.at[pl.ds(x, rows)]
        ends = (near, far) if to_whole else (far, near)
        copies.append(pltpu.make_async_copy(*ends, sems.at[n]))
    return copies


def adjoint_kernel(parts, *refs):
    it = iter(refs)
    border, adds, last = parts["border"], parts["adds"], parts["last"]
    inner, outer = next(it), next(it)
    even, odd = (next(it), next(it)) if border else (None, None)
    right, left, later, speed, inject = [next(it) for _ in range(5)]
    lap_of, acc_in = (next(it), next(it)) if adds else (None, None)
    if last and border:
        next(it)
    nxt = next(it)
    second = next(it) if last and not border else None
    edge_out = next(it) if parts["sends"] else None
    acc_out = next(it) if adds else None
    halo = next(it) if border else None
    part, copies = nxt, []
    if last:
        part, sems = next(it), next(it)
    parity = lax.axis_index("slab") % 2
    width_y = inner.shape[1]
    if border:
        fill_halo(parity, even, odd, halo)
    else:
        if parts["sends"]:
            emit_edge(parity != 0, outer, edge_out)
        if last:
            copies += part_copies(True, outer, second, sems.at[pl.ds(2, 2)], True)
            copies += part_copies(False, inner, second, sems.at[pl.ds(4, 1)], True)
            for copy in copies:
                copy.start()

    def put(i, x, v, lap):
        added = inject[pl.ds(x * width_y * 8 + parts["time"], width_y, stride=8), :]
        part[i] = 2.0 * v - later[i] + speed[x] * lap + added
        if adds:
            acc_out[i] = acc_in[i] + v * lap_of[i]

    laplace_rows(border, inner, outer, halo, right, left, put)
    if last:
        for copy in part_copies(border, part, nxt, sems, True):
            copy.start()
            copies.append(copy)
    elif border:
        emit_edge(parity == 0, part, edge_out)
    for copy in copies:
        copy.wait()


def edges_kernel(*refs):
    fields, outs, sems = refs[:2], refs[2:4], refs[4]
    parity = lax.axis_index("slab") % 2
    top = fields[0].shape[0] - reach
    rows = pl.ds(top * (1 - parity), reach)
    copies = [pltpu.make_async_copy(fields[i].at[rows], outs[i], sems.at[i]) for i in range(2)]
    for copy in copies:
        copy.start()
    for copy in copies:
        copy.wait()


def load_kernel(listen, *refs):
    fields, speed, refs = refs[:4], refs[4], refs[5:]
    parts, speed_out, where_to, tiles, edge, sems = refs[:8], *refs[8:13]
    top = fields[3].shape[0] - reach
    rows = pl.ds(top * (lax.axis_index("slab") % 2), reach)
    copies = [
        pltpu.make_async_copy(speed, speed_out, sems.at[12]),
        pltpu.make_async_copy(fields[3].at[rows], edge, sems.at[13]),
    ]
    for i in range(4):
        copies += part_copies(False, parts[2 * i], fields[i], sems.at[pl.ds(3 * i, 1)], False)
        copies += part_copies(True, parts[2 * i + 1], fields[i], sems.at[pl.ds(3 * i + 1, 2)], False)
    for copy in copies:
        copy.start()
    count, width_y, width_z = fields[0].shape
    depth = listen[0:1, :] - lax.axis_index("slab") * count
    inside = (depth >= 0) & (depth < count)
    flat = depth * (width_y * width_z) + listen[1:2, :] * width_z + listen[2:3, :]
    where_to[...] = jnp.where(inside, flat, count * width_y * width_z)
    zero_rows = 64 * 8

    @pl.loop(0, tiles.shape[0] // zero_rows)
    def _(i):
        tiles[pl.ds(pl.multiple_of(i * zero_rows, 8), zero_rows), :] = jnp.zeros(
            (zero_rows, 128), jnp.float32
        )

    rest = tiles.shape[0] % zero_rows
    if rest:
        tiles[tiles.shape[0] - rest :, :] = jnp.zeros((rest, 128), jnp.float32)
    for copy in copies:
        copy.wait()


def scatter_kernel(where_to, *refs):
    blocks, out = refs[:-3], refs[-1]
    steps, per = blocks[0].shape[-2:]
    group, groups = 4, 8
    slab = lax.axis_index("slab")
    lanes = lax.broadcasted_iota(jnp.int32, (8, 128), 1)
    d = 0
    for held_blocks in blocks:
        for e in range(held_blocks.shape[0]):
            base = (slab ^ d) * per
            d += 1
            for part in range(per // 128):
                block = held_blocks[e, :, part * 128 : (part + 1) * 128]

                @pl.loop(0, 128 // (group * groups))
                def _(i):
                    tiles, terms, slots = [], [], []
                    for u in range(group * groups):
                        j = i * (group * groups) + u
                        flat = where_to[0, base + part * 128 + j]
                        lane = flat & 127
                        tile = flat >> 7
                        moved = pltpu.roll(block, (lane - j) & 127, 1)
                        tiles.append(tile)
                        terms.append(jnp.where(lanes == lane, moved, 0.0))
                        slots.append(pl.ds(pl.multiple_of(tile * 8, 8), 8))
                    for g in range(groups):
                        own = range(g * group, (g + 1) * group)
                        held = {u: out[slots[u], :] for u in own}
                        for u in own:
                            value = held[u] + terms[u]
                            for w in range(g * group, u):
                                same = (tiles[w] == tiles[u]).astype(jnp.float32)
                                value = value + terms[w] * same
                            held[u] = value
                        for u in own:
                            out[slots[u], :] = held[u]


def pair_kernel(keep, arrived, *outs):
    mine = lax.axis_index("shot") // 2
    for m in range(len(outs)):
        outs[m][...] = keep[mine ^ m] + arrived[mine ^ m]


def sum_kernel(*refs):
    out = refs[-1]
    half = len(refs) // 2
    for border, terms in ((False, refs[:half]), (True, refs[half:-1])):
        total = terms[0][...]
        for term in terms[1:]:
            total = total + term[...]
        if border:
            out[:reach] = total[:reach]
            out[out.shape[0] - reach :] = total[reach:]
        else:
            out[reach : out.shape[0] - reach] = total


def vmem(*shape):
    return VMEM(shape, jnp.float32)


def plain(*shape):
    return jax.ShapeDtypeStruct(shape, jnp.float32)


def call(name, kernel, args, outs, scratch=(), spaces=None, out_spaces=None, micros=1, aliases=None):
    spec = lambda space: pl.BlockSpec(memory_space=space)
    spaces = spaces or {}
    args = [
        pltpu.with_memory_space_constraint(arg, HBM) if spaces.get(i) is HBM else arg
        for i, arg in enumerate(args)
    ]
    out_spaces = out_spaces or {}
    return pl.pallas_call(
        kernel,
        out_shape=outs,
        in_specs=[spec(spaces.get(i, VMEM)) for i in range(len(args))],
        out_specs=[spec(out_spaces.get(i, VMEM)) for i in range(len(outs))],
        scratch_shapes=scratch,
        input_output_aliases=aliases or {},
        compiler_params=pltpu.CompilerParams(vmem_limit_bytes=limit),
        cost_estimate=pl.CostEstimate(
            flops=micros * 1000000000, bytes_accessed=micros << 16, transcendentals=0
        ),
        name=name,
    )(*args)


def pair_swap(count, start):
    pairs = []
    for i in range(start, count - 1, 2):
        pairs += [(i, i + 1), (i + 1, i)]
    return pairs


def body(
    state_before,
    state_now,
    adjoint_after,
    adjoint_now,
    speed_term,
    wavelet,
    source,
    receivers,
    traces,
):
    count, width_y, width_z = speed_term.shape
    steps = wavelet.shape[1]
    slabs = lax.axis_size("slab")
    shots = lax.axis_size("shot")
    half = steps // 2
    scale = 1.0 / (8.0 * steps)
    even_pairs, odd_pairs = pair_swap(slabs, 0), pair_swap(slabs, 1)
    inner = count - 2 * reach
    field = vmem(count, width_y, width_z)
    part = {False: vmem(inner, width_y, width_z), True: vmem(2 * reach, width_y, width_z)}
    edge = vmem(reach, width_y, width_z)
    dma = pltpu.SemaphoreType.DMA

    def by_even(edges):
        return lax.ppermute(edges, "slab", even_pairs)

    def by_odd(edges):
        return lax.ppermute(edges, "slab", odd_pairs)

    right = jnp.asarray(band_right(width_z))
    left = jnp.asarray(band_left(width_y))
    listen = receivers[0]

    blocks = [traces]
    bit = 1
    while bit < slabs:
        held = blocks[0] if len(blocks) == 1 else jnp.concatenate(blocks, axis=0)
        blocks.append(lax.ppermute(held, "slab", [(i, i ^ bit) for i in range(slabs)]))
        bit *= 2

    p_even, q_even = call(
        "edges", edges_kernel, [state_now[0], adjoint_now[0]], [edge] * 2, [dma((2,))], {0: HBM, 1: HBM}
    )
    p_even, q_even = by_even(p_even), by_even(q_even)
    fields = [state_before[0], state_now[0], adjoint_after[0], adjoint_now[0], speed_term]
    tiles = vmem((count * width_y + 1) * 8, width_z)
    *loaded, speed, where_to, zeros, q_odd = call(
        "load",
        load_kernel,
        [listen, *fields],
        [part[False], part[True]] * 4 + [field, VMEM((1, listen.shape[1]), jnp.int32), tiles, edge],
        [dma((14,))],
        {1 + i: HBM for i in range(5)},
    )
    p = {-1: loaded[0:2], 0: loaded[2:4]}
    q = {steps + 1: loaded[4:6], steps: loaded[6:8]}
    laps, acc = {}, {False: None, True: None}

    def forward(k, border, halos):
        last = k == steps - 1
        parts = dict(
            border=border, moves=not last, stores=k < half, adds=k >= half, opens=k == half, step=k, scale=scale
        )
        args = [*p[k], *halos, right, left]
        outs, scratch, spaces = [], [part[True]] if border else [], {}
        if not last:
            spaces = {len(args) + 2: HBM, len(args) + 3: HBM}
            args += [p[k - 1][border], speed, source, wavelet]
            outs += [part[border]]
            scratch += [SMEM(source.shape, jnp.int32), SMEM(wavelet.shape, jnp.float32), dma, dma]
        if not last or not border:
            outs += [edge]
        if parts["stores"]:
            outs += [part[border]]
        if parts["adds"]:
            args += [q[k + 1][border]]
            if not parts["opens"]:
                args += [acc[border]]
            if not last:
                outs += [part[border]]
        if last:
            args += [q[1][border], laps[0][border]]
            piece = vmem(shots // 2, part[border].shape[0], width_y // shots, width_z)
            outs += [piece, piece]
            scratch += [part[border]]
        name = "forward_border" if border else "forward_inner"
        got = list(call(name, functools.partial(forward_kernel, parts), args, outs, scratch, spaces))
        nxt = None if last else got.pop(0)
        sides = None if last and border else got.pop(0)
        if last:
            return sides, got
        if parts["stores"]:
            laps.setdefault(k, [None, None])[border] = got[0]
        else:
            acc[border] = got[0]
        p.setdefault(k + 1, [None, None])[border] = nxt
        return sides

    def adjoint(k, border, halos, opening=None):
        last = k == steps - 1
        t = steps - 1 - k
        sends = not last if border else k > 0
        parts = dict(border=border, adds=k >= half and not last, last=last, time=t, sends=sends)
        args = [*q[t + 1], *halos, right, left, q[t + 2][border], speed, inject]
        outs, scratch, out_spaces, aliases = [part[border]], [part[True]] if border else [], {}, {}
        spaces = {}
        if parts["adds"]:
            args += [laps[t][border], acc[border]]
        if last:
            whole = plain(count, width_y, width_z)
            outs = [whole] if border else [whole, whole]
            out_spaces = {i: HBM for i in range(len(outs))}
            scratch += [part[border], dma((5,))]
            if border:
                spaces, aliases = {len(args): HBM}, {len(args): 0}
                args += [opening]
        if sends:
            outs += [edge]
        if parts["adds"]:
            outs += [part[border]]
        name = "adjoint_border" if border else "adjoint_inner"
        got = call(
            name, functools.partial(adjoint_kernel, parts), args, outs, scratch, spaces, out_spaces,
            micros=30 if last and border else 1, aliases=aliases,
        )
        if last:
            return got
        q.setdefault(t, [None, None])[border] = got[0]
        if parts["adds"]:
            acc[border] = got[2]
        return got[1] if sends else None

    def spread(send, kept):
        arrived = lax.ppermute(send, "shot", [(i, i ^ 1) for i in range(shots)])
        piece = vmem(*send.shape[1:])
        pieces = call("pair", pair_kernel, [kept, arrived], [piece] * (shots // 2), micros=0)
        return [pieces[0]] + [
            lax.ppermute(pieces[m], "shot", [(i, i ^ (2 * m)) for i in range(shots)])
            for m in range(1, shots // 2)
        ]

    p_odd = by_odd(forward(0, False, ()))
    q_odd = by_odd(q_odd)
    for k in range(steps - 1):
        p_even = by_even(forward(k, True, (p_even, p_odd)))
        if k == 0:
            (inject,) = call(
                "receivers",
                scatter_kernel,
                [where_to, *blocks, p[1][True], zeros],
                [tiles],
                (),
                {0: SMEM},
                aliases={2 + len(blocks): 0},
            )
            adjoint(0, False, ())
        if k + 1 < steps - 1:
            p_odd = by_odd(forward(k + 1, False, ()))
        else:
            sides, halves = forward(k + 1, False, ())
            p_odd = by_odd(sides)
            terms = spread(*halves)
        q_even = by_even(adjoint(k, True, (q_even, q_odd)))
        if k + 1 < steps - 1:
            q_odd = by_odd(adjoint(k + 1, False, ()))
        else:
            opening, second, sides = adjoint(k + 1, False, ())
            q_odd = by_odd(sides)
    _, halves = forward(steps - 1, True, (p_even, p_odd))
    terms += spread(*halves)
    (opening,) = adjoint(steps - 1, True, (q_even, q_odd), opening)
    (gradient,) = call("sum", sum_kernel, terms, [plain(count, width_y // shots, width_z)], micros=0)
    return (opening[None], second[None], gradient)


def solution(mesh):
    return jax.shard_map(
        body,
        mesh=mesh,
        in_specs=(
            P("shot", "slab", None, None),
            P("shot", "slab", None, None),
            P("shot", "slab", None, None),
            P("shot", "slab", None, None),
            P("slab", None, None),
            P("shot", None),
            P("shot", None),
            P("shot", None, None),
            P("shot", None, "slab"),
        ),
        out_specs=(
            P("shot", "slab", None, None),
            P("shot", "slab", None, None),
            P("slab", "shot", None),
        ),
        check_vma=False,
    )
```

```python
import functools

import jax
import jax.numpy as jnp
import ml_dtypes
import numpy as np
from jax import lax
from jax.experimental import pallas as pl
from jax.experimental.pallas import tpu as pltpu
from jax.sharding import PartitionSpec as P

weights = (-205.0 / 72.0, 8.0 / 5.0, -1.0 / 5.0, 8.0 / 315.0, -1.0 / 560.0)
reach = 4
VMEM = pltpu.VMEM
SMEM = pltpu.SMEM
HBM = pltpu.HBM
limit = 12 * 1024 * 1024


def band(width, centre):
    out = np.zeros((width, width), np.float64)
    for k in range(1, reach + 1):
        out += weights[k] * (np.eye(width, k=k) + np.eye(width, k=-k))
    out += centre * np.eye(width)
    high = out.astype(np.float32).astype(ml_dtypes.bfloat16)
    low = (out - high.astype(np.float64)).astype(np.float32).astype(ml_dtypes.bfloat16)
    return high, low


def band_right(width):
    high, low = band(width, 3.0 * weights[0])
    return np.block([[high, low], [high, np.zeros_like(low)]])


def band_left(width):
    high, low = band(width, 0.0)
    return np.block([[high, high], [low, np.zeros_like(low)]])


def split(v):
    high = v.astype(jnp.bfloat16)
    low = (v - high.astype(jnp.float32)).astype(jnp.bfloat16)
    return high, low


def fill_halo(parity, even, odd, halo):
    @pl.when(parity == 0)
    def _():
        halo[:reach] = odd[...]
        halo[reach:] = even[...]

    @pl.when(parity != 0)
    def _():
        halo[:reach] = even[...]
        halo[reach:] = odd[...]


def emit_edges(parity, field, even, odd):
    count = field.shape[0]

    @pl.when(parity == 0)
    def _():
        even[...] = field[count - reach :]
        odd[...] = field[:reach]

    @pl.when(parity != 0)
    def _():
        even[...] = field[:reach]
        odd[...] = field[count - reach :]


def laplace_planes(cur, halo, right, left, put, rows=None):
    count, width_y, width_z = cur.shape

    def plane(i):
        if i < 0:
            return halo[reach + i]
        if i >= count:
            return halo[reach + i - count]
        return cur[i]

    for x in (range(0, count, 2) if rows is None else rows):
        v = [cur[x], cur[x + 1]]
        (h0, l0), (h1, l1) = split(v[0]), split(v[1])
        rows = jnp.concatenate(
            [jnp.concatenate([h0, l0], axis=1), jnp.concatenate([h1, l1], axis=1)], axis=0
        )
        along = jnp.dot(rows, right[...], preferred_element_type=jnp.float32)
        cols = jnp.concatenate(
            [jnp.concatenate([h0, h1], axis=1), jnp.concatenate([l0, l1], axis=1)], axis=0
        )
        across = jnp.dot(left[...], cols, preferred_element_type=jnp.float32)
        for j in range(2):
            rows_j = slice(j * width_y, (j + 1) * width_y)
            lanes_j = slice(j * width_z, (j + 1) * width_z)
            lap = along[rows_j, :width_z] + along[rows_j, width_z:]
            lap = lap + (across[:width_y, lanes_j] + across[width_y:, lanes_j])
            for k in range(1, reach + 1):
                lap = lap + weights[k] * (plane(x + j + k) + plane(x + j - k))
            put(x + j, v[j], lap)


def forward_kernel(parts, *refs):
    it = iter(refs)
    cur, even, odd, right, left = [next(it) for _ in range(5)]
    moves, stores, adds, opens = parts["moves"], parts["stores"], parts["adds"], parts["opens"]
    prev, speed, source, wave = [next(it) for _ in range(4)] if moves else (None,) * 4
    late = next(it) if adds else None
    acc_in = next(it) if adds and not opens else None
    first, lap_first = (next(it), next(it)) if not moves else (None, None)
    nxt = next(it) if moves else None
    even_out, odd_out = (next(it), next(it)) if parts["sends"] else (None, None)
    lap_out = next(it) if stores else None
    acc_out = next(it) if adds and moves else None
    send, keep = (next(it), next(it)) if not moves else (None, None)
    halo = next(it)
    if moves:
        spot_smem, wave_smem, spot_sem, wave_sem = [next(it) for _ in range(4)]
        spot_copy = pltpu.make_async_copy(source, spot_smem, spot_sem)
        wave_copy = pltpu.make_async_copy(wave, wave_smem, wave_sem)
        spot_copy.start()
        wave_copy.start()
    total = next(it) if not moves else None
    slab = lax.axis_index("slab")
    parity = slab % 2
    fill_halo(parity, even, odd, halo)

    def put(x, v, lap):
        if moves:
            nxt[x] = 2.0 * v - prev[x] + speed[x] * lap
        if stores:
            lap_out[x] = lap
        if adds:
            value = lap * late[x]
            if not opens:
                value = value + acc_in[x]
            if moves:
                acc_out[x] = value
            else:
                total[x] = (value + first[x] * lap_first[x]) * parts["scale"]

    laplace_planes(cur, halo, right, left, put)
    if moves:
        spot_copy.wait()
        wave_copy.wait()
        row = spot_smem[0, 0] - slab * cur.shape[0]
        col, lane = spot_smem[0, 1], spot_smem[0, 2]

        @pl.when((row >= 0) & (row < cur.shape[0]))
        def _():
            tile = pl.ds(pl.multiple_of((col // 8) * 8, 8), 8)
            shape = (8, cur.shape[2])
            hit = (lax.broadcasted_iota(jnp.int32, shape, 0) == col % 8) & (
                lax.broadcasted_iota(jnp.int32, shape, 1) == lane
            )
            nxt[row, tile, :] = nxt[row, tile, :] + jnp.where(hit, wave_smem[0, parts["step"]], 0.0)

        if parts["sends"]:
            emit_edges(parity, nxt, even_out, odd_out)
    else:
        chunk = send.shape[2]
        mine = lax.axis_index("shot") % 2
        for j in range(send.shape[0]):
            away = pl.multiple_of((2 * j + 1 - mine) * chunk, 8)
            here = pl.multiple_of((2 * j + mine) * chunk, 8)
            send[j] = total[:, pl.ds(away, chunk), :]
            keep[j] = total[:, pl.ds(here, chunk), :]


def adjoint_kernel(parts, *refs):
    it = iter(refs)
    cur, later, speed, even, odd, inject, right, left = [next(it) for _ in range(8)]
    adds = parts["adds"]
    lap_of, acc_in = (next(it), next(it)) if adds else (None, None)
    nxt, even_out, odd_out = [next(it) for _ in range(3)]
    acc_out = next(it) if adds else None
    halo = next(it)
    parity = lax.axis_index("slab") % 2
    fill_halo(parity, even, odd, halo)
    width_y = cur.shape[1]

    def put(x, v, lap):
        added = inject[pl.ds(x * width_y * 8 + parts["time"], width_y, stride=8), :]
        nxt[x] = 2.0 * v - later[x] + speed[x] * lap + added
        if adds:
            acc_out[x] = acc_in[x] + v * lap_of[x]

    laplace_planes(cur, halo, right, left, put)
    emit_edges(parity, nxt, even_out, odd_out)


def last_inner_kernel(cur, later, speed, inject, right, left, opening, second, field, sems):
    count, width_y = cur.shape[:2]
    copies = [pltpu.make_async_copy(cur, second, sems.at[0])]
    copies[0].start()

    def put(x, v, lap):
        added = inject[pl.ds(x * width_y * 8, width_y, stride=8), :]
        field[x - reach] = 2.0 * v - later[x] + speed[x] * lap + added

    laplace_planes(cur, None, right, left, put, range(reach, count - reach, 2))
    inner = opening.at[pl.ds(reach, count - 2 * reach)]
    copies.append(pltpu.make_async_copy(field, inner, sems.at[1]))
    copies[1].start()
    for copy in copies:
        copy.wait()


def last_border_kernel(
    cur, later, speed, even, odd, inject, right, left, opening_in, opening, halo, field, sems
):
    count, width_y = cur.shape[:2]
    fill_halo(lax.axis_index("slab") % 2, even, odd, halo)
    top = count - reach
    copies = []
    for n, first in enumerate((0, top)):

        def put(x, v, lap):
            added = inject[pl.ds(x * width_y * 8, width_y, stride=8), :]
            field[n * reach + x - first] = 2.0 * v - later[x] + speed[x] * lap + added

        laplace_planes(cur, halo, right, left, put, range(first, first + reach, 2))
        rows = opening.at[pl.ds(first, reach)]
        copies.append(pltpu.make_async_copy(field.at[pl.ds(n * reach, reach)], rows, sems.at[n]))
        copies[n].start()
    for copy in copies:
        copy.wait()


def edges_kernel(*refs):
    fields, outs, sems = refs[:2], refs[2:6], refs[6]
    parity = lax.axis_index("slab") % 2
    top = fields[0].shape[0] - reach
    starts = (top * (1 - parity), top * parity)
    copies = []
    for i in range(4):
        rows = pl.ds(starts[i % 2], reach)
        copies.append(pltpu.make_async_copy(fields[i // 2].at[rows], outs[i], sems.at[i]))
        copies[-1].start()
    for copy in copies:
        copy.wait()


def stack_kernel(*refs):
    first = 0
    for ref in refs[:-1]:
        refs[-1][first : first + ref.shape[0]] = ref[...]
        first += ref.shape[0]


def load_kernel(listen_hbm, *refs):
    fields, outs, where_to, tiles, listen, sems = refs[:3], refs[4:7], *refs[7:]
    listen_copy = pltpu.make_async_copy(listen_hbm.at[0], listen, sems.at[3])
    listen_copy.start()
    copies = [pltpu.make_async_copy(fields[i], outs[i], sems.at[i]) for i in range(3)]
    for copy in copies:
        copy.start()
    zero_rows = 64 * 8

    @pl.loop(0, tiles.shape[0] // zero_rows)
    def _(i):
        tiles[pl.ds(pl.multiple_of(i * zero_rows, 8), zero_rows), :] = jnp.zeros(
            (zero_rows, 128), jnp.float32
        )

    rest = tiles.shape[0] % zero_rows
    if rest:
        tiles[tiles.shape[0] - rest :, :] = jnp.zeros((rest, 128), jnp.float32)
    listen_copy.wait()
    count, width_y, width_z = fields[0].shape
    depth = listen[0:1, :] - lax.axis_index("slab") * count
    inside = (depth >= 0) & (depth < count)
    flat = depth * (width_y * width_z) + listen[1:2, :] * width_z + listen[2:3, :]
    where_to[...] = jnp.where(inside, flat, count * width_y * width_z)
    for copy in copies:
        copy.wait()


def scatter_kernel(levels, where_to, *refs):
    blocks, refs = refs[:levels], refs[levels:]
    fields, stepped, _, out, outs, even_out, odd_out, sems = refs[:2], *refs[2:5], refs[5:7], *refs[7:]
    copies = [pltpu.make_async_copy(fields[i], outs[i], sems.at[i]) for i in range(2)]
    for copy in copies:
        copy.start()
    emit_edges(lax.axis_index("slab") % 2, stepped, even_out, odd_out)
    per = blocks[0].shape[-1]
    group, groups = 4, 8
    slab = lax.axis_index("slab")
    lanes = lax.broadcasted_iota(jnp.int32, (8, 128), 1)
    d = 0
    for held_blocks in blocks:
        for e in range(held_blocks.shape[0]):
            base = (slab ^ d) * per
            d += 1
            for part in range(per // 128):
                block = held_blocks[e, :, part * 128 : (part + 1) * 128]

                @pl.loop(0, 128 // (group * groups))
                def _(i):
                    tiles, terms, slots = [], [], []
                    for u in range(group * groups):
                        j = i * (group * groups) + u
                        flat = where_to[0, base + part * 128 + j]
                        lane = flat & 127
                        tile = flat >> 7
                        moved = pltpu.roll(block, (lane - j) & 127, 1)
                        tiles.append(jnp.full((8, 128), tile, jnp.int32))
                        terms.append(jnp.where(lanes == lane, moved, 0.0))
                        slots.append(pl.ds(pl.multiple_of(tile * 8, 8), 8))
                    for g in range(groups):
                        own = range(g * group, (g + 1) * group)
                        held = {u: out[slots[u], :] for u in own}
                        for u in own:
                            value = held[u] + terms[u]
                            for w in range(g * group, u):
                                value = value + jnp.where(tiles[w] == tiles[u], terms[w], 0.0)
                            held[u] = value
                        for u in own:
                            out[slots[u], :] = held[u]
    for copy in copies:
        copy.wait()


def pair_kernel(keep, arrived, _, *outs):
    mine = lax.axis_index("shot") // 2
    for m in range(len(outs)):
        outs[m][...] = keep[mine ^ m] + arrived[mine ^ m]


def sum_kernel(*refs):
    total = refs[0][...]
    for ref in refs[1:-1]:
        total = total + ref[...]
    refs[-1][...] = total


def vmem(*shape):
    return VMEM(shape, jnp.float32)


def plain(*shape):
    return jax.ShapeDtypeStruct(shape, jnp.float32)


def call(name, kernel, args, outs, scratch=(), spaces=None, out_spaces=None, micros=2, aliases=None):
    spec = lambda space: pl.BlockSpec(memory_space=space)
    spaces = spaces or {}
    args = [
        pltpu.with_memory_space_constraint(arg, HBM) if spaces.get(i) is HBM else arg
        for i, arg in enumerate(args)
    ]
    out_spaces = out_spaces or {}
    return pl.pallas_call(
        kernel,
        out_shape=outs,
        in_specs=[spec(spaces.get(i, VMEM)) for i in range(len(args))],
        out_specs=[spec(out_spaces.get(i, VMEM)) for i in range(len(outs))],
        scratch_shapes=scratch,
        input_output_aliases=aliases or {},
        compiler_params=pltpu.CompilerParams(vmem_limit_bytes=limit),
        cost_estimate=pl.CostEstimate(
            flops=micros * 1000000000, bytes_accessed=micros << 16, transcendentals=0
        ),
        name=name,
    )(*args)


def pair_swap(count, start):
    pairs = []
    for i in range(start, count - 1, 2):
        pairs += [(i, i + 1), (i + 1, i)]
    return pairs


def body(
    state_before,
    state_now,
    adjoint_after,
    adjoint_now,
    speed_term,
    wavelet,
    source,
    receivers,
    traces,
):
    count, width_y, width_z = speed_term.shape
    steps = wavelet.shape[1]
    slabs = lax.axis_size("slab")
    shots = lax.axis_size("shot")
    half = steps // 2
    scale = 1.0 / (8.0 * steps)
    even_pairs, odd_pairs = pair_swap(slabs, 0), pair_swap(slabs, 1)
    field = vmem(count, width_y, width_z)
    edge = vmem(reach, width_y, width_z)
    halo = vmem(2 * reach, width_y, width_z)
    dma = pltpu.SemaphoreType.DMA

    def swap(even, odd):
        return lax.ppermute(even, "slab", even_pairs), lax.ppermute(odd, "slab", odd_pairs)

    right = jnp.asarray(band_right(width_z))
    left = jnp.asarray(band_left(width_y))

    blocks = [traces]
    bit = 1
    while bit < slabs:
        held = blocks[0]
        if len(blocks) > 1:
            (held,) = call("stack", stack_kernel, blocks, [vmem(bit, *traces.shape[1:])], micros=0)
        blocks.append(lax.ppermute(held, "slab", [(i, i ^ bit) for i in range(slabs)]))
        bit *= 2

    p0_even, p0_odd, q8_even, q8_odd = call(
        "edges", edges_kernel, [state_now[0], adjoint_now[0]], [edge] * 4, [dma((4,))], {0: HBM, 1: HBM}
    )
    p_halo = swap(p0_even, p0_odd)
    q_halo = swap(q8_even, q8_odd)
    tiles = vmem((count * width_y + 1) * 8, width_z)
    before, now, speed, where_to, zeros = call(
        "load",
        load_kernel,
        [receivers, state_before[0], state_now[0], speed_term, held],
        [field] * 3 + [VMEM((1, receivers.shape[2]), jnp.int32), tiles],
        [VMEM(receivers.shape[1:], jnp.int32), dma((4,))],
        {i: HBM for i in range(4)},
        micros=1,
    )
    p, q = {-1: before, 0: now}, {}
    laps = {}
    acc = None

    for k in range(steps):
        last = k == steps - 1
        parts = dict(
            moves=not last, stores=k < half, adds=k >= half, opens=k == half, step=k, scale=scale,
            sends=0 < k < steps - 1,
        )
        args = [p[k], *p_halo, right, left]
        outs, scratch, spaces = [], [halo], {}
        if not last:
            spaces = {len(args) + 2: HBM, len(args) + 3: HBM}
            args += [p[k - 1], speed, source, wavelet]
            outs += [field]
            scratch += [SMEM(source.shape, jnp.int32), SMEM(wavelet.shape, jnp.float32), dma, dma]
        if parts["sends"]:
            outs += [edge, edge]
        if parts["stores"]:
            outs += [field]
        if parts["adds"]:
            args += [q[k + 1]]
            if not parts["opens"]:
                args += [acc]
            if not last:
                outs += [field]
        if last:
            args += [q[1], laps[0]]
            piece = vmem(shots // 2, count, width_y // shots, width_z)
            outs += [piece, piece]
            scratch += [field]
        got = list(
            call(
                "forward", functools.partial(forward_kernel, parts), args, outs, scratch, spaces,
                micros=0 if last else 2,
            )
        )
        if not last:
            p[k + 1] = got.pop(0)
            if parts["sends"]:
                p_halo = swap(got.pop(0), got.pop(0))
            if parts["stores"]:
                laps[k] = got.pop(0)
            else:
                acc = got.pop(0)
        if k == 0:
            at = 1 + len(blocks)
            inject, q[steps + 1], q[steps], *sides = call(
                "receivers",
                functools.partial(scatter_kernel, len(blocks)),
                [where_to, *blocks, adjoint_after[0], adjoint_now[0], p[1], zeros],
                [tiles, field, field, edge, edge],
                [dma((2,))],
                {0: SMEM, at: HBM, at + 1: HBM},
                aliases={at + 3: 0},
            )
            p_halo = swap(*sides)

        t = steps - 1 - k
        if last:
            send, kept = got
            arrived = lax.ppermute(send, "shot", [(i, i ^ 1) for i in range(shots)])
            whole = plain(count, width_y, width_z)
            opening, second = call(
                "last_inner",
                last_inner_kernel,
                [q[1], q[2], speed, inject, right, left],
                [whole, whole],
                [vmem(count - 2 * reach, width_y, width_z), dma((2,))],
                None,
                {0: HBM, 1: HBM},
                micros=30,
            )
            piece = vmem(count, width_y // shots, width_z)
            pieces = call(
                "pair", pair_kernel, [kept, arrived, opening], [piece] * (shots // 2), (), {2: HBM}, micros=0
            )
            terms = [pieces[0]] + [
                lax.ppermute(pieces[m], "shot", [(i, i ^ (2 * m)) for i in range(shots)])
                for m in range(1, shots // 2)
            ]
            (opening,) = call(
                "last_border",
                last_border_kernel,
                [q[1], q[2], speed, *q_halo, inject, right, left, opening],
                [whole],
                [halo, vmem(2 * reach, width_y, width_z), dma((2,))],
                {8: HBM},
                {0: HBM},
                micros=30,
                aliases={8: 0},
            )
            (gradient,) = call("sum", sum_kernel, terms, [plain(count, width_y // shots, width_z)], micros=0)
            break
        parts = dict(adds=k >= half, time=t)
        args = [q[t + 1], q[t + 2], speed, *q_halo, inject, right, left]
        outs = [field, edge, edge]
        if parts["adds"]:
            args += [laps[t], acc]
            outs += [field]
        got = call("adjoint", functools.partial(adjoint_kernel, parts), args, outs, [halo])
        q[t] = got[0]
        q_halo = swap(*got[1:3])
        if parts["adds"]:
            acc = got[3]

    return (opening[None], second[None], gradient)


def solution(mesh):
    return jax.shard_map(
        body,
        mesh=mesh,
        in_specs=(
            P("shot", "slab", None, None),
            P("shot", "slab", None, None),
            P("shot", "slab", None, None),
            P("shot", "slab", None, None),
            P("slab", None, None),
            P("shot", None),
            P("shot", None),
            P("shot", None, None),
            P("shot", None, "slab"),
        ),
        out_specs=(
            P("shot", "slab", None, None),
            P("shot", "slab", None, None),
            P("slab", "shot", None),
        ),
        check_vma=False,
    )
```

```python
import functools

import jax
import jax.numpy as jnp
import ml_dtypes
import numpy as np
from jax import lax
from jax.experimental import pallas as pl
from jax.experimental.pallas import tpu as pltpu
from jax.sharding import PartitionSpec as P

weights = (-205.0 / 72.0, 8.0 / 5.0, -1.0 / 5.0, 8.0 / 315.0, -1.0 / 560.0)
reach = 4
VMEM = pltpu.VMEM
SMEM = pltpu.SMEM
HBM = pltpu.HBM
limit = 12 * 1024 * 1024


def band(width, centre):
    out = np.zeros((width, width), np.float64)
    for k in range(1, reach + 1):
        out += weights[k] * (np.eye(width, k=k) + np.eye(width, k=-k))
    out += centre * np.eye(width)
    high = out.astype(np.float32).astype(ml_dtypes.bfloat16)
    low = (out - high.astype(np.float64)).astype(np.float32).astype(ml_dtypes.bfloat16)
    return high, low


def band_right(width):
    high, low = band(width, 3.0 * weights[0])
    return np.block([[high, low], [high, np.zeros_like(low)]])


def band_left(width):
    high, low = band(width, 0.0)
    return np.block([[high, high], [low, np.zeros_like(low)]])


def split(v):
    high = v.astype(jnp.bfloat16)
    low = (v - high.astype(jnp.float32)).astype(jnp.bfloat16)
    return high, low


def fill_halo(parity, even, odd, halo):
    @pl.when(parity == 0)
    def _():
        halo[:reach] = odd[...]
        halo[reach:] = even[...]

    @pl.when(parity != 0)
    def _():
        halo[:reach] = even[...]
        halo[reach:] = odd[...]


def emit_edges(parity, field, even, odd):
    count = field.shape[0]

    @pl.when(parity == 0)
    def _():
        even[...] = field[count - reach :]
        odd[...] = field[:reach]

    @pl.when(parity != 0)
    def _():
        even[...] = field[:reach]
        odd[...] = field[count - reach :]


def laplace_planes(cur, halo, right, left, put, rows=None):
    count, width_y, width_z = cur.shape

    def plane(i):
        if i < 0:
            return halo[reach + i]
        if i >= count:
            return halo[reach + i - count]
        return cur[i]

    for x in (range(0, count, 2) if rows is None else rows):
        v = [cur[x], cur[x + 1]]
        (h0, l0), (h1, l1) = split(v[0]), split(v[1])
        rows = jnp.concatenate(
            [jnp.concatenate([h0, l0], axis=1), jnp.concatenate([h1, l1], axis=1)], axis=0
        )
        along = jnp.dot(rows, right[...], preferred_element_type=jnp.float32)
        cols = jnp.concatenate(
            [jnp.concatenate([h0, h1], axis=1), jnp.concatenate([l0, l1], axis=1)], axis=0
        )
        across = jnp.dot(left[...], cols, preferred_element_type=jnp.float32)
        for j in range(2):
            rows_j = slice(j * width_y, (j + 1) * width_y)
            lanes_j = slice(j * width_z, (j + 1) * width_z)
            lap = along[rows_j, :width_z] + along[rows_j, width_z:]
            lap = lap + (across[:width_y, lanes_j] + across[width_y:, lanes_j])
            for k in range(1, reach + 1):
                lap = lap + weights[k] * (plane(x + j + k) + plane(x + j - k))
            put(x + j, v[j], lap)


def forward_kernel(parts, *refs):
    it = iter(refs)
    cur, even, odd, right, left = [next(it) for _ in range(5)]
    moves, stores, adds, opens = parts["moves"], parts["stores"], parts["adds"], parts["opens"]
    prev, speed, source, wave = [next(it) for _ in range(4)] if moves else (None,) * 4
    late = next(it) if adds else None
    acc_in = next(it) if adds and not opens else None
    first, lap_first = (next(it), next(it)) if not moves else (None, None)
    nxt = next(it) if moves else None
    even_out, odd_out = (next(it), next(it)) if parts["sends"] else (None, None)
    lap_out = next(it) if stores else None
    acc_out = next(it) if adds and moves else None
    send, keep = (next(it), next(it)) if not moves else (None, None)
    halo = next(it)
    if moves:
        spot_smem, wave_smem, spot_sem, wave_sem = [next(it) for _ in range(4)]
        spot_copy = pltpu.make_async_copy(source, spot_smem, spot_sem)
        wave_copy = pltpu.make_async_copy(wave, wave_smem, wave_sem)
        spot_copy.start()
        wave_copy.start()
    total = next(it) if not moves else None
    slab = lax.axis_index("slab")
    parity = slab % 2
    fill_halo(parity, even, odd, halo)

    def put(x, v, lap):
        if moves:
            nxt[x] = 2.0 * v - prev[x] + speed[x] * lap
        if stores:
            lap_out[x] = lap
        if adds:
            value = lap * late[x]
            if not opens:
                value = value + acc_in[x]
            if moves:
                acc_out[x] = value
            else:
                total[x] = (value + first[x] * lap_first[x]) * parts["scale"]

    laplace_planes(cur, halo, right, left, put)
    if moves:
        spot_copy.wait()
        wave_copy.wait()
        row = spot_smem[0, 0] - slab * cur.shape[0]
        col, lane = spot_smem[0, 1], spot_smem[0, 2]

        @pl.when((row >= 0) & (row < cur.shape[0]))
        def _():
            tile = pl.ds(pl.multiple_of((col // 8) * 8, 8), 8)
            shape = (8, cur.shape[2])
            hit = (lax.broadcasted_iota(jnp.int32, shape, 0) == col % 8) & (
                lax.broadcasted_iota(jnp.int32, shape, 1) == lane
            )
            nxt[row, tile, :] = nxt[row, tile, :] + jnp.where(hit, wave_smem[0, parts["step"]], 0.0)

        if parts["sends"]:
            emit_edges(parity, nxt, even_out, odd_out)
    else:
        chunk = send.shape[2]
        mine = lax.axis_index("shot") % 2
        for j in range(send.shape[0]):
            away = pl.multiple_of((2 * j + 1 - mine) * chunk, 8)
            here = pl.multiple_of((2 * j + mine) * chunk, 8)
            send[j] = total[:, pl.ds(away, chunk), :]
            keep[j] = total[:, pl.ds(here, chunk), :]


def injected(tiles, x, time, width_y):
    return tiles[pl.ds((x + reach) * width_y * 8 + time, width_y, stride=8), :]


def adjoint_kernel(parts, *refs):
    it = iter(refs)
    cur, later, speed, even, odd, right, left = [next(it) for _ in range(7)]
    adds, injects = parts["adds"], parts["injects"]
    inject = next(it) if injects else None
    lap_of, acc_in = (next(it), next(it)) if adds else (None, None)
    nxt, even_out, odd_out = [next(it) for _ in range(3)]
    acc_out = next(it) if adds else None
    halo = next(it)
    parity = lax.axis_index("slab") % 2
    fill_halo(parity, even, odd, halo)
    count, width_y = cur.shape[:2]
    if parts["late"]:
        for i in range(2 * reach):
            x = i - reach if i < reach else count + i - reach
            halo[i] = halo[i] + injected(inject, x, parts["time"] + 1, width_y)

    def put(x, v, lap):
        value = 2.0 * v - later[x] + speed[x] * lap
        nxt[x] = value + injected(inject, x, parts["time"], width_y) if injects else value
        if adds:
            acc_out[x] = acc_in[x] + v * lap_of[x]

    laplace_planes(cur, halo, right, left, put)
    emit_edges(parity, nxt, even_out, odd_out)


def last_inner_kernel(cur, later, speed, inject, right, left, opening, second, field, sems):
    count, width_y = cur.shape[:2]
    copies = [pltpu.make_async_copy(cur, second, sems.at[0])]
    copies[0].start()

    def put(x, v, lap):
        added = injected(inject, x, 0, width_y)
        field[x - reach] = 2.0 * v - later[x] + speed[x] * lap + added

    laplace_planes(cur, None, right, left, put, range(reach, count - reach, 2))
    inner = opening.at[pl.ds(reach, count - 2 * reach)]
    copies.append(pltpu.make_async_copy(field, inner, sems.at[1]))
    copies[1].start()
    for copy in copies:
        copy.wait()


def last_border_kernel(
    cur, later, speed, even, odd, inject, right, left, opening_in, opening, halo, field, sems
):
    count, width_y = cur.shape[:2]
    fill_halo(lax.axis_index("slab") % 2, even, odd, halo)
    top = count - reach
    copies = []
    for n, first in enumerate((0, top)):

        def put(x, v, lap):
            added = injected(inject, x, 0, width_y)
            field[n * reach + x - first] = 2.0 * v - later[x] + speed[x] * lap + added

        laplace_planes(cur, halo, right, left, put, range(first, first + reach, 2))
        rows = opening.at[pl.ds(first, reach)]
        copies.append(pltpu.make_async_copy(field.at[pl.ds(n * reach, reach)], rows, sems.at[n]))
        copies[n].start()
    for copy in copies:
        copy.wait()


def edges_kernel(*refs):
    fields, outs, sems = refs[:2], refs[2:6], refs[6]
    parity = lax.axis_index("slab") % 2
    top = fields[0].shape[0] - reach
    starts = (top * (1 - parity), top * parity)
    copies = []
    for i in range(4):
        rows = pl.ds(starts[i % 2], reach)
        copies.append(pltpu.make_async_copy(fields[i // 2].at[rows], outs[i], sems.at[i]))
        copies[-1].start()
    for copy in copies:
        copy.wait()


def stack_kernel(*refs):
    first = 0
    for ref in refs[:-1]:
        refs[-1][first : first + ref.shape[0]] = ref[...]
        first += ref.shape[0]


def load_kernel(listen_hbm, *refs):
    fields, outs, where_to, tiles, listen, sems = refs[:3], refs[4:7], *refs[7:]
    listen_copy = pltpu.make_async_copy(listen_hbm.at[0], listen, sems.at[3])
    listen_copy.start()
    copies = [pltpu.make_async_copy(fields[i], outs[i], sems.at[i]) for i in range(3)]
    for copy in copies:
        copy.start()
    zero_rows = 64 * 8

    @pl.loop(0, tiles.shape[0] // zero_rows)
    def _(i):
        tiles[pl.ds(pl.multiple_of(i * zero_rows, 8), zero_rows), :] = jnp.zeros(
            (zero_rows, 128), jnp.float32
        )

    rest = tiles.shape[0] % zero_rows
    if rest:
        tiles[tiles.shape[0] - rest :, :] = jnp.zeros((rest, 128), jnp.float32)
    listen_copy.wait()
    count, width_y, width_z = fields[0].shape
    held = count + 2 * reach
    depth = listen[0:1, :] - lax.axis_index("slab") * count + reach
    inside = (depth >= 0) & (depth < held)
    flat = depth * (width_y * width_z) + listen[1:2, :] * width_z + listen[2:3, :]
    where_to[...] = jnp.where(inside, flat, held * width_y * width_z)
    for copy in copies:
        copy.wait()


def scatter_kernel(levels, where_to, *refs):
    blocks, refs = refs[:levels], refs[levels:]
    field, _, out, field_out = refs
    per = blocks[0].shape[-1]
    group, groups = 8, 4
    slab = lax.axis_index("slab")
    lanes = lax.broadcasted_iota(jnp.int32, (8, 128), 1)
    d = 0
    for held_blocks in blocks:
        for e in range(held_blocks.shape[0]):
            base = (slab ^ d) * per
            d += 1
            for part in range(per // 128):
                block = held_blocks[e, :, part * 128 : (part + 1) * 128]

                @pl.loop(0, 128 // (group * groups))
                def _(i):
                    tiles, terms, slots = [], [], []
                    for u in range(group * groups):
                        j = i * (group * groups) + u
                        flat = where_to[0, base + part * 128 + j]
                        lane = flat & 127
                        tile = flat >> 7
                        moved = pltpu.roll(block, (lane - j) & 127, 1)
                        tiles.append(jnp.full((8, 128), tile, jnp.int32))
                        terms.append(jnp.where(lanes == lane, moved, 0.0))
                        slots.append(pl.ds(pl.multiple_of(tile * 8, 8), 8))
                    for g in range(groups):
                        own = range(g * group, (g + 1) * group)
                        held = {u: out[slots[u], :] for u in own}
                        for u in own:
                            value = held[u] + terms[u]
                            for w in range(g * group, u):
                                value = value + jnp.where(tiles[w] == tiles[u], terms[w], 0.0)
                            held[u] = value
                        for u in own:
                            out[slots[u], :] = held[u]
    count, width_y = field.shape[:2]
    for x in range(count):
        field_out[x] = field[x] + injected(out, x, blocks[0].shape[1] - 1, width_y)


def pair_kernel(keep, arrived, _, *outs):
    mine = lax.axis_index("shot") // 2
    for m in range(len(outs)):
        outs[m][...] = keep[mine ^ m] + arrived[mine ^ m]


def sum_kernel(*refs):
    total = refs[0][...]
    for ref in refs[1:-1]:
        total = total + ref[...]
    refs[-1][...] = total


def vmem(*shape):
    return VMEM(shape, jnp.float32)


def plain(*shape):
    return jax.ShapeDtypeStruct(shape, jnp.float32)


def call(name, kernel, args, outs, scratch=(), spaces=None, out_spaces=None, micros=2, aliases=None):
    spec = lambda space: pl.BlockSpec(memory_space=space)
    spaces = spaces or {}
    args = [
        pltpu.with_memory_space_constraint(arg, HBM) if spaces.get(i) is HBM else arg
        for i, arg in enumerate(args)
    ]
    out_spaces = out_spaces or {}
    return pl.pallas_call(
        kernel,
        out_shape=outs,
        in_specs=[spec(spaces.get(i, VMEM)) for i in range(len(args))],
        out_specs=[spec(out_spaces.get(i, VMEM)) for i in range(len(outs))],
        scratch_shapes=scratch,
        input_output_aliases=aliases or {},
        compiler_params=pltpu.CompilerParams(vmem_limit_bytes=limit),
        cost_estimate=pl.CostEstimate(
            flops=micros * 1000000000, bytes_accessed=micros << 16, transcendentals=0
        ),
        name=name,
    )(*args)


def pair_swap(count, start):
    pairs = []
    for i in range(start, count - 1, 2):
        pairs += [(i, i + 1), (i + 1, i)]
    return pairs


def body(
    state_before,
    state_now,
    adjoint_after,
    adjoint_now,
    speed_term,
    wavelet,
    source,
    receivers,
    traces,
):
    count, width_y, width_z = speed_term.shape
    steps = wavelet.shape[1]
    slabs = lax.axis_size("slab")
    shots = lax.axis_size("shot")
    half = steps // 2
    scale = 1.0 / (8.0 * steps)
    even_pairs, odd_pairs = pair_swap(slabs, 0), pair_swap(slabs, 1)
    field = vmem(count, width_y, width_z)
    edge = vmem(reach, width_y, width_z)
    halo = vmem(2 * reach, width_y, width_z)
    dma = pltpu.SemaphoreType.DMA

    def swap(even, odd):
        return lax.ppermute(even, "slab", even_pairs), lax.ppermute(odd, "slab", odd_pairs)

    right = jnp.asarray(band_right(width_z))
    left = jnp.asarray(band_left(width_y))

    blocks = [traces]
    bit = 1
    while bit < slabs:
        held = blocks[0]
        if len(blocks) > 1:
            (held,) = call("stack", stack_kernel, blocks, [vmem(bit, *traces.shape[1:])], micros=0)
        blocks.append(lax.ppermute(held, "slab", [(i, i ^ bit) for i in range(slabs)]))
        bit *= 2

    p0_even, p0_odd, q8_even, q8_odd = call(
        "edges", edges_kernel, [state_now[0], adjoint_now[0]], [edge] * 4, [dma((4,))], {0: HBM, 1: HBM}
    )
    p_halo = swap(p0_even, p0_odd)
    q_halo = swap(q8_even, q8_odd)
    tiles = vmem(((count + 2 * reach) * width_y + 1) * 8, width_z)
    before, now, speed, where_to, zeros = call(
        "load",
        load_kernel,
        [receivers, state_before[0], state_now[0], speed_term, held],
        [field] * 3 + [VMEM((1, receivers.shape[2]), jnp.int32), tiles],
        [VMEM(receivers.shape[1:], jnp.int32), dma((4,))],
        {i: HBM for i in range(4)},
        micros=1,
    )
    p = {-1: before, 0: now}
    q = {steps + 1: adjoint_after[0], steps: adjoint_now[0]}
    laps = {}
    acc = None

    for k in range(steps):
        last = k == steps - 1
        parts = dict(
            moves=not last, stores=k < half, adds=k >= half, opens=k == half, step=k, scale=scale,
            sends=not last,
        )
        args = [p[k], *p_halo, right, left]
        outs, scratch, spaces = [], [halo], {}
        if not last:
            spaces = {len(args) + 2: HBM, len(args) + 3: HBM}
            args += [p[k - 1], speed, source, wavelet]
            outs += [field]
            scratch += [SMEM(source.shape, jnp.int32), SMEM(wavelet.shape, jnp.float32), dma, dma]
        if parts["sends"]:
            outs += [edge, edge]
        if parts["stores"]:
            outs += [field]
        if parts["adds"]:
            args += [q[k + 1]]
            if not parts["opens"]:
                args += [acc]
            if not last:
                outs += [field]
        if last:
            args += [q[1], laps[0]]
            piece = vmem(shots // 2, count, width_y // shots, width_z)
            outs += [piece, piece]
            scratch += [field]
        got = list(
            call(
                "forward", functools.partial(forward_kernel, parts), args, outs, scratch, spaces,
                micros=0 if last else 2,
            )
        )
        if not last:
            p[k + 1] = got.pop(0)
            if parts["sends"]:
                p_halo = swap(got.pop(0), got.pop(0))
            if parts["stores"]:
                laps[k] = got.pop(0)
            else:
                acc = got.pop(0)
        t = steps - 1 - k
        if last:
            send, kept = got
            arrived = lax.ppermute(send, "shot", [(i, i ^ 1) for i in range(shots)])
            whole = plain(count, width_y, width_z)
            opening, second = call(
                "last_inner",
                last_inner_kernel,
                [q[1], q[2], speed, inject, right, left],
                [whole, whole],
                [vmem(count - 2 * reach, width_y, width_z), dma((2,))],
                None,
                {0: HBM, 1: HBM},
                micros=30,
            )
            piece = vmem(count, width_y // shots, width_z)
            pieces = call(
                "pair", pair_kernel, [kept, arrived, opening], [piece] * (shots // 2), (), {2: HBM}, micros=0
            )
            terms = [pieces[0]] + [
                lax.ppermute(pieces[m], "shot", [(i, i ^ (2 * m)) for i in range(shots)])
                for m in range(1, shots // 2)
            ]
            (opening,) = call(
                "last_border",
                last_border_kernel,
                [q[1], q[2], speed, *q_halo, inject, right, left, opening],
                [whole],
                [halo, vmem(2 * reach, width_y, width_z), dma((2,))],
                {8: HBM},
                {0: HBM},
                micros=30,
                aliases={8: 0},
            )
            (gradient,) = call("sum", sum_kernel, terms, [plain(count, width_y // shots, width_z)], micros=0)
            break
        parts = dict(adds=k >= half, time=t, injects=k > 0, late=k == 1)
        args = [q[t + 1], q[t + 2], speed, *q_halo, right, left]
        if k > 0:
            args += [inject]
        outs = [field, edge, edge]
        if parts["adds"]:
            args += [laps[t], acc]
            outs += [field]
        got = call("adjoint", functools.partial(adjoint_kernel, parts), args, outs, [halo])
        q[t] = got[0]
        q_halo = swap(*got[1:3])
        if parts["adds"]:
            acc = got[3]
        if k == 0:
            at = 1 + len(blocks)
            inject, q[t] = call(
                "receivers",
                functools.partial(scatter_kernel, len(blocks)),
                [where_to, *blocks, q[t], zeros],
                [tiles, field],
                (),
                {0: SMEM},
                aliases={at: 1, at + 1: 0},
            )

    return (opening[None], second[None], gradient)


def solution(mesh):
    return jax.shard_map(
        body,
        mesh=mesh,
        in_specs=(
            P("shot", "slab", None, None),
            P("shot", "slab", None, None),
            P("shot", "slab", None, None),
            P("shot", "slab", None, None),
            P("slab", None, None),
            P("shot", None),
            P("shot", None),
            P("shot", None, None),
            P("shot", None, "slab"),
        ),
        out_specs=(
            P("shot", "slab", None, None),
            P("shot", "slab", None, None),
            P("slab", "shot", None),
        ),
        check_vma=False,
    )
```

```python
import functools

import jax
import jax.numpy as jnp
import ml_dtypes
import numpy as np
from jax import lax
from jax.experimental import pallas as pl
from jax.experimental.pallas import tpu as pltpu
from jax.sharding import PartitionSpec as P

weights = (-205.0 / 72.0, 8.0 / 5.0, -1.0 / 5.0, 8.0 / 315.0, -1.0 / 560.0)
reach = 4
VMEM = pltpu.VMEM
SMEM = pltpu.SMEM
HBM = pltpu.HBM
limit = 12 * 1024 * 1024


def band(width, centre):
    out = np.zeros((width, width), np.float64)
    for k in range(1, reach + 1):
        out += weights[k] * (np.eye(width, k=k) + np.eye(width, k=-k))
    out += centre * np.eye(width)
    high = out.astype(np.float32).astype(ml_dtypes.bfloat16)
    low = (out - high.astype(np.float64)).astype(np.float32).astype(ml_dtypes.bfloat16)
    return high, low


def band_right(width):
    high, low = band(width, 3.0 * weights[0])
    return np.block([[high, low], [high, np.zeros_like(low)]])


def band_left(width):
    high, low = band(width, 0.0)
    return np.block([[high, high], [low, np.zeros_like(low)]])


def split(v):
    high = v.astype(jnp.bfloat16)
    low = (v - high.astype(jnp.float32)).astype(jnp.bfloat16)
    return high, low


def fill_halo(parity, even, odd, halo):
    @pl.when(parity == 0)
    def _():
        halo[:reach] = odd[...]
        halo[reach:] = even[...]

    @pl.when(parity != 0)
    def _():
        halo[:reach] = even[...]
        halo[reach:] = odd[...]


def emit_edges(parity, field, even, odd):
    count = field.shape[0]

    @pl.when(parity == 0)
    def _():
        even[...] = field[count - reach :]
        odd[...] = field[:reach]

    @pl.when(parity != 0)
    def _():
        even[...] = field[:reach]
        odd[...] = field[count - reach :]


def laplace_planes(cur, halo, right, left, put, rows=None):
    count, width_y, width_z = cur.shape

    def plane(i):
        if i < 0:
            return halo[reach + i]
        if i >= count:
            return halo[reach + i - count]
        return cur[i]

    for x in (range(0, count, 2) if rows is None else rows):
        v = [cur[x], cur[x + 1]]
        (h0, l0), (h1, l1) = split(v[0]), split(v[1])
        rows = jnp.concatenate(
            [jnp.concatenate([h0, l0], axis=1), jnp.concatenate([h1, l1], axis=1)], axis=0
        )
        along = jnp.dot(rows, right[...], preferred_element_type=jnp.float32)
        cols = jnp.concatenate(
            [jnp.concatenate([h0, h1], axis=1), jnp.concatenate([l0, l1], axis=1)], axis=0
        )
        across = jnp.dot(left[...], cols, preferred_element_type=jnp.float32)
        for j in range(2):
            rows_j = slice(j * width_y, (j + 1) * width_y)
            lanes_j = slice(j * width_z, (j + 1) * width_z)
            lap = along[rows_j, :width_z] + along[rows_j, width_z:]
            lap = lap + (across[:width_y, lanes_j] + across[width_y:, lanes_j])
            for k in range(1, reach + 1):
                lap = lap + weights[k] * (plane(x + j + k) + plane(x + j - k))
            put(x + j, v[j], lap)


def forward_kernel(parts, *refs):
    it = iter(refs)
    cur, odd, even, right, left = [next(it) for _ in range(5)]
    moves, stores, adds, opens = parts["moves"], parts["stores"], parts["adds"], parts["opens"]
    prev, speed, source, wave = [next(it) for _ in range(4)] if moves else (None,) * 4
    late = next(it) if adds else None
    acc_in = next(it) if adds and not opens else None
    first, lap_first = (next(it), next(it)) if not moves else (None, None)
    nxt = next(it) if moves else None
    even_out, odd_out = (next(it), next(it)) if parts["sends"] else (None, None)
    lap_out = next(it) if stores else None
    acc_out = next(it) if adds and moves else None
    send, keep = (next(it), next(it)) if not moves else (None, None)
    halo = next(it)
    if moves:
        spot_smem, wave_smem, spot_sem, wave_sem = [next(it) for _ in range(4)]
        spot_copy = pltpu.make_async_copy(source, spot_smem, spot_sem)
        wave_copy = pltpu.make_async_copy(wave, wave_smem, wave_sem)
        spot_copy.start()
        wave_copy.start()
    total = next(it) if not moves else None
    slab = lax.axis_index("slab")
    parity = slab % 2
    fill_halo(parity, even, odd, halo)

    def put(x, v, lap):
        if moves:
            nxt[x] = 2.0 * v - prev[x] + speed[x] * lap
        if stores:
            lap_out[x] = lap
        if adds:
            value = lap * late[x]
            if not opens:
                value = value + acc_in[x]
            if moves:
                acc_out[x] = value
            else:
                total[x] = (value + first[x] * lap_first[x]) * parts["scale"]

    laplace_planes(cur, halo, right, left, put)
    if moves:
        spot_copy.wait()
        wave_copy.wait()
        row = spot_smem[0, 0] - slab * cur.shape[0]
        col, lane = spot_smem[0, 1], spot_smem[0, 2]

        @pl.when((row >= 0) & (row < cur.shape[0]))
        def _():
            tile = pl.ds(pl.multiple_of((col // 8) * 8, 8), 8)
            shape = (8, cur.shape[2])
            hit = (lax.broadcasted_iota(jnp.int32, shape, 0) == col % 8) & (
                lax.broadcasted_iota(jnp.int32, shape, 1) == lane
            )
            nxt[row, tile, :] = nxt[row, tile, :] + jnp.where(hit, wave_smem[0, parts["step"]], 0.0)

        if parts["sends"]:
            emit_edges(parity, nxt, even_out, odd_out)
    else:
        chunk = send.shape[2]
        mine = lax.axis_index("shot") % 2
        for j in range(send.shape[0]):
            away = pl.multiple_of((2 * j + 1 - mine) * chunk, 8)
            here = pl.multiple_of((2 * j + mine) * chunk, 8)
            send[j] = total[:, pl.ds(away, chunk), :]
            keep[j] = total[:, pl.ds(here, chunk), :]


def injected(tiles, x, time, width_y):
    return tiles[pl.ds((x + reach) * width_y * 8 + time, width_y, stride=8), :]


def adjoint_kernel(parts, *refs):
    it = iter(refs)
    cur, later, speed, odd, even, right, left = [next(it) for _ in range(7)]
    adds, injects = parts["adds"], parts["injects"]
    inject = next(it) if injects else None
    lap_of, acc_in = (next(it), next(it)) if adds else (None, None)
    nxt, even_out, odd_out = [next(it) for _ in range(3)]
    acc_out = next(it) if adds else None
    halo = next(it)
    parity = lax.axis_index("slab") % 2
    fill_halo(parity, even, odd, halo)
    count, width_y = cur.shape[:2]
    if parts["late"]:
        for i in range(2 * reach):
            x = i - reach if i < reach else count + i - reach
            halo[i] = halo[i] + injected(inject, x, parts["time"] + 1, width_y)

    def put(x, v, lap):
        value = 2.0 * v - later[x] + speed[x] * lap
        nxt[x] = value + injected(inject, x, parts["time"], width_y) if injects else value
        if adds:
            acc_out[x] = acc_in[x] + v * lap_of[x]

    laplace_planes(cur, halo, right, left, put)
    emit_edges(parity, nxt, even_out, odd_out)


def last_inner_kernel(cur, later, speed, inject, right, left, opening, second, field, sems):
    count, width_y = cur.shape[:2]
    copies = [pltpu.make_async_copy(cur, second, sems.at[0])]
    copies[0].start()

    def put(x, v, lap):
        added = injected(inject, x, 0, width_y)
        field[x - reach] = 2.0 * v - later[x] + speed[x] * lap + added

    laplace_planes(cur, None, right, left, put, range(reach, count - reach, 2))
    inner = opening.at[pl.ds(reach, count - 2 * reach)]
    copies.append(pltpu.make_async_copy(field, inner, sems.at[1]))
    copies[1].start()
    for copy in copies:
        copy.wait()


def last_border_kernel(
    cur, later, speed, odd, even, inject, right, left, opening_in, opening, halo, field, sems
):
    count, width_y = cur.shape[:2]
    fill_halo(lax.axis_index("slab") % 2, even, odd, halo)
    top = count - reach
    copies = []
    for n, first in enumerate((0, top)):

        def put(x, v, lap):
            added = injected(inject, x, 0, width_y)
            field[n * reach + x - first] = 2.0 * v - later[x] + speed[x] * lap + added

        laplace_planes(cur, halo, right, left, put, range(first, first + reach, 2))
        rows = opening.at[pl.ds(first, reach)]
        copies.append(pltpu.make_async_copy(field.at[pl.ds(n * reach, reach)], rows, sems.at[n]))
        copies[n].start()
    for copy in copies:
        copy.wait()


def edges_kernel(*refs):
    fields, outs, sems = refs[:2], refs[2:6], refs[6]
    parity = lax.axis_index("slab") % 2
    top = fields[0].shape[0] - reach
    starts = (top * (1 - parity), top * parity)
    copies = []
    for i in range(4):
        rows = pl.ds(starts[i % 2], reach)
        copies.append(pltpu.make_async_copy(fields[i // 2].at[rows], outs[i], sems.at[i]))
        copies[-1].start()
    for copy in copies:
        copy.wait()


def stack_kernel(*refs):
    first = 0
    for ref in refs[:-1]:
        refs[-1][first : first + ref.shape[0]] = ref[...]
        first += ref.shape[0]


def load_kernel(listen_hbm, *refs):
    fields, outs, where_to, tiles, listen, sems = refs[:3], refs[4:7], *refs[7:]
    listen_copy = pltpu.make_async_copy(listen_hbm.at[0], listen, sems.at[3])
    listen_copy.start()
    copies = [pltpu.make_async_copy(fields[i], outs[i], sems.at[i]) for i in range(3)]
    for copy in copies:
        copy.start()
    zero_rows = 64 * 8

    @pl.loop(0, tiles.shape[0] // zero_rows)
    def _(i):
        tiles[pl.ds(pl.multiple_of(i * zero_rows, 8), zero_rows), :] = jnp.zeros(
            (zero_rows, 128), jnp.float32
        )

    rest = tiles.shape[0] % zero_rows
    if rest:
        tiles[tiles.shape[0] - rest :, :] = jnp.zeros((rest, 128), jnp.float32)
    listen_copy.wait()
    count, width_y, width_z = fields[0].shape
    held = count + 2 * reach
    depth = listen[0:1, :] - lax.axis_index("slab") * count + reach
    inside = (depth >= 0) & (depth < held)
    flat = depth * (width_y * width_z) + listen[1:2, :] * width_z + listen[2:3, :]
    where_to[...] = jnp.where(inside, flat, held * width_y * width_z)
    for copy in copies:
        copy.wait()


def scatter_kernel(levels, where_to, *refs):
    blocks, refs = refs[:levels], refs[levels:]
    field, _, out, field_out = refs
    per = blocks[0].shape[-1]
    group, groups = 8, 4
    slab = lax.axis_index("slab")
    lanes = lax.broadcasted_iota(jnp.int32, (8, 128), 1)
    d = 0
    for held_blocks in blocks:
        for e in range(held_blocks.shape[0]):
            base = (slab ^ d) * per
            d += 1
            for part in range(per // 128):
                block = held_blocks[e, :, part * 128 : (part + 1) * 128]

                @pl.loop(0, 128 // (group * groups))
                def _(i):
                    tiles, terms, slots = [], [], []
                    for u in range(group * groups):
                        j = i * (group * groups) + u
                        flat = where_to[0, base + part * 128 + j]
                        lane = flat & 127
                        tile = flat >> 7
                        moved = pltpu.roll(block, (lane - j) & 127, 1)
                        tiles.append(jnp.full((8, 128), tile, jnp.int32))
                        terms.append(jnp.where(lanes == lane, moved, 0.0))
                        slots.append(pl.ds(pl.multiple_of(tile * 8, 8), 8))
                    for g in range(groups):
                        own = range(g * group, (g + 1) * group)
                        held = {u: out[slots[u], :] for u in own}
                        for u in own:
                            value = held[u] + terms[u]
                            for w in range(g * group, u):
                                value = value + jnp.where(tiles[w] == tiles[u], terms[w], 0.0)
                            held[u] = value
                        for u in own:
                            out[slots[u], :] = held[u]
    count, width_y = field.shape[:2]
    for x in range(count):
        field_out[x] = field[x] + injected(out, x, blocks[0].shape[1] - 1, width_y)


def pair_kernel(keep, arrived, _, *outs):
    mine = lax.axis_index("shot") // 2
    for m in range(len(outs)):
        outs[m][...] = keep[mine ^ m] + arrived[mine ^ m]


def sum_kernel(*refs):
    total = refs[0][...]
    for ref in refs[1:-1]:
        total = total + ref[...]
    refs[-1][...] = total


def vmem(*shape):
    return VMEM(shape, jnp.float32)


def plain(*shape):
    return jax.ShapeDtypeStruct(shape, jnp.float32)


def call(name, kernel, args, outs, scratch=(), spaces=None, out_spaces=None, micros=2, aliases=None):
    spec = lambda space: pl.BlockSpec(memory_space=space)
    spaces = spaces or {}
    args = [
        pltpu.with_memory_space_constraint(arg, HBM) if spaces.get(i) is HBM else arg
        for i, arg in enumerate(args)
    ]
    out_spaces = out_spaces or {}
    return pl.pallas_call(
        kernel,
        out_shape=outs,
        in_specs=[spec(spaces.get(i, VMEM)) for i in range(len(args))],
        out_specs=[spec(out_spaces.get(i, VMEM)) for i in range(len(outs))],
        scratch_shapes=scratch,
        input_output_aliases=aliases or {},
        compiler_params=pltpu.CompilerParams(vmem_limit_bytes=limit),
        cost_estimate=pl.CostEstimate(
            flops=micros * 1000000000, bytes_accessed=micros << 16, transcendentals=0
        ),
        name=name,
    )(*args)


def pair_swap(count, start):
    pairs = []
    for i in range(start, count - 1, 2):
        pairs += [(i, i + 1), (i + 1, i)]
    return pairs


def body(
    state_before,
    state_now,
    adjoint_after,
    adjoint_now,
    speed_term,
    wavelet,
    source,
    receivers,
    traces,
):
    count, width_y, width_z = speed_term.shape
    steps = wavelet.shape[1]
    slabs = lax.axis_size("slab")
    shots = lax.axis_size("shot")
    half = steps // 2
    scale = 1.0 / (8.0 * steps)
    even_pairs, odd_pairs = pair_swap(slabs, 0), pair_swap(slabs, 1)
    field = vmem(count, width_y, width_z)
    edge = vmem(reach, width_y, width_z)
    halo = vmem(2 * reach, width_y, width_z)
    dma = pltpu.SemaphoreType.DMA

    def swap(even, odd):
        odd = lax.ppermute(odd, "slab", odd_pairs)
        return odd, lax.ppermute(even, "slab", even_pairs)

    right = jnp.asarray(band_right(width_z))
    left = jnp.asarray(band_left(width_y))

    blocks = [traces]
    bit = 1
    while bit < slabs:
        held = blocks[0]
        if len(blocks) > 1:
            (held,) = call("stack", stack_kernel, blocks, [vmem(bit, *traces.shape[1:])], micros=0)
        blocks.append(lax.ppermute(held, "slab", [(i, i ^ bit) for i in range(slabs)]))
        bit *= 2

    p0_even, p0_odd, q8_even, q8_odd = call(
        "edges", edges_kernel, [state_now[0], adjoint_now[0]], [edge] * 4, [dma((4,))], {0: HBM, 1: HBM}
    )
    p_halo = swap(p0_even, p0_odd)
    q_halo = swap(q8_even, q8_odd)
    tiles = vmem(((count + 2 * reach) * width_y + 1) * 8, width_z)
    before, now, speed, where_to, zeros = call(
        "load",
        load_kernel,
        [receivers, state_before[0], state_now[0], speed_term, held],
        [field] * 3 + [VMEM((1, receivers.shape[2]), jnp.int32), tiles],
        [VMEM(receivers.shape[1:], jnp.int32), dma((4,))],
        {i: HBM for i in range(4)},
        micros=1,
    )
    p = {-1: before, 0: now}
    q = {steps + 1: adjoint_after[0], steps: adjoint_now[0]}
    laps = {}
    acc = None

    for k in range(steps):
        last = k == steps - 1
        parts = dict(
            moves=not last, stores=k < half, adds=k >= half, opens=k == half, step=k, scale=scale,
            sends=not last,
        )
        args = [p[k], *p_halo, right, left]
        outs, scratch, spaces = [], [halo], {}
        if not last:
            spaces = {len(args) + 2: HBM, len(args) + 3: HBM}
            args += [p[k - 1], speed, source, wavelet]
            outs += [field]
            scratch += [SMEM(source.shape, jnp.int32), SMEM(wavelet.shape, jnp.float32), dma, dma]
        if parts["sends"]:
            outs += [edge, edge]
        if parts["stores"]:
            outs += [field]
        if parts["adds"]:
            args += [q[k + 1]]
            if not parts["opens"]:
                args += [acc]
            if not last:
                outs += [field]
        if last:
            args += [q[1], laps[0]]
            piece = vmem(shots // 2, count, width_y // shots, width_z)
            outs += [piece, piece]
            scratch += [field]
        got = list(
            call(
                "forward", functools.partial(forward_kernel, parts), args, outs, scratch, spaces,
                micros=0 if last else 2,
            )
        )
        if not last:
            p[k + 1] = got.pop(0)
            if parts["sends"]:
                p_halo = swap(got.pop(0), got.pop(0))
            if parts["stores"]:
                laps[k] = got.pop(0)
            else:
                acc = got.pop(0)
        t = steps - 1 - k
        if last:
            send, kept = got
            arrived = lax.ppermute(send, "shot", [(i, i ^ 1) for i in range(shots)])
            whole = plain(count, width_y, width_z)
            opening, second = call(
                "last_inner",
                last_inner_kernel,
                [q[1], q[2], speed, inject, right, left],
                [whole, whole],
                [vmem(count - 2 * reach, width_y, width_z), dma((2,))],
                None,
                {0: HBM, 1: HBM},
                micros=30,
            )
            piece = vmem(count, width_y // shots, width_z)
            pieces = call(
                "pair", pair_kernel, [kept, arrived, opening], [piece] * (shots // 2), (), {2: HBM}, micros=0
            )
            terms = [pieces[0]] + [
                lax.ppermute(pieces[m], "shot", [(i, i ^ (2 * m)) for i in range(shots)])
                for m in range(1, shots // 2)
            ]
            (opening,) = call(
                "last_border",
                last_border_kernel,
                [q[1], q[2], speed, *q_halo, inject, right, left, opening],
                [whole],
                [halo, vmem(2 * reach, width_y, width_z), dma((2,))],
                {8: HBM},
                {0: HBM},
                micros=30,
                aliases={8: 0},
            )
            (gradient,) = call("sum", sum_kernel, terms, [plain(count, width_y // shots, width_z)], micros=0)
            break
        parts = dict(adds=k >= half, time=t, injects=k > 0, late=k == 1)
        args = [q[t + 1], q[t + 2], speed, *q_halo, right, left]
        if k > 0:
            args += [inject]
        outs = [field, edge, edge]
        if parts["adds"]:
            args += [laps[t], acc]
            outs += [field]
        got = call("adjoint", functools.partial(adjoint_kernel, parts), args, outs, [halo])
        q[t] = got[0]
        q_halo = swap(*got[1:3])
        if parts["adds"]:
            acc = got[3]
        if k == 0:
            at = 1 + len(blocks)
            inject, q[t] = call(
                "receivers",
                functools.partial(scatter_kernel, len(blocks)),
                [where_to, *blocks, q[t], zeros],
                [tiles, field],
                (),
                {0: SMEM},
                aliases={at: 1, at + 1: 0},
            )

    return (opening[None], second[None], gradient)


def solution(mesh):
    return jax.shard_map(
        body,
        mesh=mesh,
        in_specs=(
            P("shot", "slab", None, None),
            P("shot", "slab", None, None),
            P("shot", "slab", None, None),
            P("shot", "slab", None, None),
            P("slab", None, None),
            P("shot", None),
            P("shot", None),
            P("shot", None, None),
            P("shot", None, "slab"),
        ),
        out_specs=(
            P("shot", "slab", None, None),
            P("shot", "slab", None, None),
            P("slab", "shot", None),
        ),
        check_vma=False,
    )
```

```python
import functools

import jax
import jax.numpy as jnp
import ml_dtypes
import numpy as np
from jax import lax
from jax.experimental import pallas as pl
from jax.experimental.pallas import tpu as pltpu
from jax.sharding import PartitionSpec as P

weights = (-205.0 / 72.0, 8.0 / 5.0, -1.0 / 5.0, 8.0 / 315.0, -1.0 / 560.0)
reach = 4
VMEM = pltpu.VMEM
SMEM = pltpu.SMEM
HBM = pltpu.HBM
limit = 12 * 1024 * 1024


def band(width, centre):
    out = np.zeros((width, width), np.float64)
    for k in range(1, reach + 1):
        out += weights[k] * (np.eye(width, k=k) + np.eye(width, k=-k))
    out += centre * np.eye(width)
    high = out.astype(np.float32).astype(ml_dtypes.bfloat16)
    low = (out - high.astype(np.float64)).astype(np.float32).astype(ml_dtypes.bfloat16)
    return high, low


def band_right(width):
    high, low = band(width, 3.0 * weights[0])
    return np.block([[high, low], [high, np.zeros_like(low)]])


def band_left(width):
    high, low = band(width, 0.0)
    return np.block([[high, high], [low, np.zeros_like(low)]])


def split(v):
    high = v.astype(jnp.bfloat16)
    low = (v - high.astype(jnp.float32)).astype(jnp.bfloat16)
    return high, low


def fill_halo(parity, even, odd, halo):
    @pl.when(parity == 0)
    def _():
        halo[:reach] = odd[...]
        halo[reach:] = even[...]

    @pl.when(parity != 0)
    def _():
        halo[:reach] = even[...]
        halo[reach:] = odd[...]


def emit_edges(parity, outer, even, odd):
    @pl.when(parity == 0)
    def _():
        even[...] = outer[reach:]
        odd[...] = outer[:reach]

    @pl.when(parity != 0)
    def _():
        even[...] = outer[:reach]
        odd[...] = outer[reach:]


def rows_of(count, border):
    if border:
        return list(range(reach)) + list(range(count - reach, count))
    return list(range(reach, count - reach))


def laplace_rows(border, inner, outer, halo, right, left, put):
    count, width_y, width_z = inner.shape[0] + 2 * reach, inner.shape[1], inner.shape[2]

    def plane(i):
        if i < 0:
            return halo[reach + i]
        if i < reach:
            return outer[i]
        if i < count - reach:
            return inner[i - reach]
        if i < count:
            return outer[i - count + 2 * reach]
        return halo[reach + i - count]

    rows = rows_of(count, border)
    for i in range(0, len(rows), 2):
        x = rows[i]
        v = [plane(x), plane(x + 1)]
        (h0, l0), (h1, l1) = split(v[0]), split(v[1])
        flat = jnp.concatenate(
            [jnp.concatenate([h0, l0], axis=1), jnp.concatenate([h1, l1], axis=1)], axis=0
        )
        along = jnp.dot(flat, right[...], preferred_element_type=jnp.float32)
        cols = jnp.concatenate(
            [jnp.concatenate([h0, h1], axis=1), jnp.concatenate([l0, l1], axis=1)], axis=0
        )
        across = jnp.dot(left[...], cols, preferred_element_type=jnp.float32)
        for j in range(2):
            rows_j = slice(j * width_y, (j + 1) * width_y)
            lanes_j = slice(j * width_z, (j + 1) * width_z)
            lap = along[rows_j, :width_z] + along[rows_j, width_z:]
            lap = lap + (across[:width_y, lanes_j] + across[width_y:, lanes_j])
            for k in range(1, reach + 1):
                lap = lap + weights[k] * (plane(x + j + k) + plane(x + j - k))
            put(i + j, x + j, v[j], lap)


def forward_kernel(parts, *refs):
    it = iter(refs)
    border, moves, stores = parts["border"], parts["moves"], parts["stores"]
    adds, opens = parts["adds"], parts["opens"]
    inner, outer = next(it), next(it)
    even, odd = (next(it), next(it)) if border else (None, None)
    right, left = next(it), next(it)
    prev, speed, source, wave = [next(it) for _ in range(4)] if moves else (None,) * 4
    late = next(it) if adds else None
    acc_in = next(it) if adds and not opens else None
    first, lap_first = (next(it), next(it)) if not moves else (None, None)
    total_inner = next(it) if border and not moves else None
    if parts["after"]:
        next(it)
    nxt = next(it) if moves else None
    even_out, odd_out = (next(it), next(it)) if moves and border else (None, None)
    lap_out = next(it) if stores else None
    acc_out = next(it) if adds and moves else None
    send, keep = (next(it), next(it)) if border and not moves else (None, None)
    halo = next(it) if border else None
    if moves:
        spot_smem, wave_smem, spot_sem, wave_sem = [next(it) for _ in range(4)]
        spot_copy = pltpu.make_async_copy(source, spot_smem, spot_sem)
        wave_copy = pltpu.make_async_copy(wave, wave_smem, wave_sem)
        spot_copy.start()
        wave_copy.start()
    total = next(it) if not moves else None
    slab = lax.axis_index("slab")
    parity = slab % 2
    count = inner.shape[0] + 2 * reach
    if border:
        fill_halo(parity, even, odd, halo)

    def put(i, x, v, lap):
        if moves:
            nxt[i] = 2.0 * v - prev[i] + speed[x] * lap
        if stores:
            lap_out[i] = lap
        if adds:
            value = lap * late[i]
            if not opens:
                value = value + acc_in[i]
            if moves:
                acc_out[i] = value
            else:
                total[i] = (value + first[i] * lap_first[i]) * parts["scale"]

    laplace_rows(border, inner, outer, halo, right, left, put)
    if moves:
        spot_copy.wait()
        wave_copy.wait()
        row = spot_smem[0, 0] - slab * count
        col, lane = spot_smem[0, 1], spot_smem[0, 2]
        within = (row >= reach) & (row < count - reach)
        place = row - reach
        if border:
            within = (row >= 0) & (row < count) & jnp.logical_not(within)
            place = jnp.where(row < reach, row, row - count + 2 * reach)

        @pl.when(within)
        def _():
            tile = pl.ds(pl.multiple_of((col // 8) * 8, 8), 8)
            shape = (8, inner.shape[2])
            hit = (lax.broadcasted_iota(jnp.int32, shape, 0) == col % 8) & (
                lax.broadcasted_iota(jnp.int32, shape, 1) == lane
            )
            added = jnp.where(hit, wave_smem[0, parts["step"]], 0.0)
            nxt[place, tile, :] = nxt[place, tile, :] + added

        if border:
            emit_edges(parity, nxt, even_out, odd_out)
    elif border:
        chunk = send.shape[2]
        mine = lax.axis_index("shot") % 2
        for j in range(send.shape[0]):
            away = pl.multiple_of((2 * j + 1 - mine) * chunk, 8)
            here = pl.multiple_of((2 * j + mine) * chunk, 8)
            for out, first_row in ((send, away), (keep, here)):
                rows = pl.ds(first_row, chunk)
                out[j, :reach] = total[:reach, rows, :]
                out[j, reach : count - reach] = total_inner[:, rows, :]
                out[j, count - reach :] = total[reach:, rows, :]


def part_copies(border, part, whole, sems, to_whole):
    count = whole.shape[0]
    if border:
        pieces = [(0, 0, reach), (reach, count - reach, reach)]
    else:
        pieces = [(0, reach, count - 2 * reach)]
    copies = []
    for n, (i, x, rows) in enumerate(pieces):
        near, far = part.at[pl.ds(i, rows)], whole.at[pl.ds(x, rows)]
        ends = (near, far) if to_whole else (far, near)
        copies.append(pltpu.make_async_copy(*ends, sems.at[n]))
    return copies


def injected(tiles, x, time, width_y):
    return tiles[pl.ds((x + reach) * width_y * 8 + time, width_y, stride=8), :]


def adjoint_kernel(parts, *refs):
    it = iter(refs)
    border, adds, last = parts["border"], parts["adds"], parts["last"]
    inner, outer = next(it), next(it)
    even, odd = (next(it), next(it)) if border else (None, None)
    right, left, later, speed = [next(it) for _ in range(4)]
    inject = next(it) if parts["injects"] else None
    lap_of, acc_in = (next(it), next(it)) if adds else (None, None)
    if last and border:
        next(it)
    if parts["after"]:
        next(it)
    nxt = next(it)
    second = next(it) if last and not border else None
    even_out, odd_out = (next(it), next(it)) if border and not last else (None, None)
    acc_out = next(it) if adds else None
    halo = next(it) if border else None
    part, copies = nxt, []
    if last:
        part, sems = next(it), next(it)
    parity = lax.axis_index("slab") % 2
    count, width_y = inner.shape[0] + 2 * reach, inner.shape[1]
    if border:
        fill_halo(parity, even, odd, halo)
        if parts["late"]:
            for i in range(2 * reach):
                x = i - reach if i < reach else count + i - reach
                halo[i] = halo[i] + injected(inject, x, parts["time"] + 1, width_y)
    elif last:
        copies += part_copies(True, outer, second, sems.at[pl.ds(2, 2)], True)
        copies += part_copies(False, inner, second, sems.at[pl.ds(4, 1)], True)
        for copy in copies:
            copy.start()

    def put(i, x, v, lap):
        value = 2.0 * v - later[i] + speed[x] * lap
        part[i] = value + injected(inject, x, parts["time"], width_y) if parts["injects"] else value
        if adds:
            acc_out[i] = acc_in[i] + v * lap_of[i]

    laplace_rows(border, inner, outer, halo, right, left, put)
    if last:
        for copy in part_copies(border, part, nxt, sems, True):
            copy.start()
            copies.append(copy)
    elif border:
        emit_edges(parity, part, even_out, odd_out)
    for copy in copies:
        copy.wait()


def edges_kernel(*refs):
    fields, outs, sems = refs[:2], refs[2:6], refs[6]
    parity = lax.axis_index("slab") % 2
    top = fields[0].shape[0] - reach
    starts = (top * (1 - parity), top * parity)
    copies = []
    for i in range(4):
        rows = pl.ds(starts[i % 2], reach)
        copies.append(pltpu.make_async_copy(fields[i // 2].at[rows], outs[i], sems.at[i]))
        copies[-1].start()
    for copy in copies:
        copy.wait()


def stack_kernel(*refs):
    first = 0
    for ref in refs[:-1]:
        refs[-1][first : first + ref.shape[0]] = ref[...]
        first += ref.shape[0]


def load_kernel(listen_hbm, *refs):
    fields, parts, speed, where_to, tiles, listen, sems = refs[:3], refs[4:8], *refs[8:]
    listen_copy = pltpu.make_async_copy(listen_hbm.at[0], listen, sems.at[7])
    copies = [listen_copy, pltpu.make_async_copy(fields[2], speed, sems.at[6])]
    for i in range(2):
        copies += part_copies(False, parts[2 * i], fields[i], sems.at[pl.ds(3 * i, 1)], False)
        copies += part_copies(True, parts[2 * i + 1], fields[i], sems.at[pl.ds(3 * i + 1, 2)], False)
    for copy in copies:
        copy.start()
    zero_rows = 64 * 8

    @pl.loop(0, tiles.shape[0] // zero_rows)
    def _(i):
        tiles[pl.ds(pl.multiple_of(i * zero_rows, 8), zero_rows), :] = jnp.zeros(
            (zero_rows, 128), jnp.float32
        )

    rest = tiles.shape[0] % zero_rows
    if rest:
        tiles[tiles.shape[0] - rest :, :] = jnp.zeros((rest, 128), jnp.float32)
    for copy in copies:
        copy.wait()
    count, width_y, width_z = fields[0].shape
    held = count + 2 * reach
    depth = listen[0:1, :] - lax.axis_index("slab") * count + reach
    inside = (depth >= 0) & (depth < held)
    flat = depth * (width_y * width_z) + listen[1:2, :] * width_z + listen[2:3, :]
    where_to[...] = jnp.where(inside, flat, held * width_y * width_z)


def load_adjoint_kernel(*refs):
    fields, parts, sems = refs[:2], refs[3:7], refs[7]
    copies = []
    for i in range(2):
        copies += part_copies(False, parts[2 * i], fields[i], sems.at[pl.ds(3 * i, 1)], False)
        copies += part_copies(True, parts[2 * i + 1], fields[i], sems.at[pl.ds(3 * i + 1, 2)], False)
    for copy in copies:
        copy.start()
    for copy in copies:
        copy.wait()


def scatter_kernel(levels, where_to, *refs):
    blocks, refs = refs[:levels], refs[levels:]
    inner, outer, _, _, out, inner_out, outer_out = refs
    per = blocks[0].shape[-1]
    group, groups = 8, 4
    slab = lax.axis_index("slab")
    lanes = lax.broadcasted_iota(jnp.int32, (8, 128), 1)
    d = 0
    for held_blocks in blocks:
        for e in range(held_blocks.shape[0]):
            base = (slab ^ d) * per
            d += 1
            for part in range(per // 128):
                block = held_blocks[e, :, part * 128 : (part + 1) * 128]

                @pl.loop(0, 128 // (group * groups))
                def _(i):
                    tiles, terms, slots = [], [], []
                    for u in range(group * groups):
                        j = i * (group * groups) + u
                        flat = where_to[0, base + part * 128 + j]
                        lane = flat & 127
                        tile = flat >> 7
                        moved = pltpu.roll(block, (lane - j) & 127, 1)
                        tiles.append(jnp.full((8, 128), tile, jnp.int32))
                        terms.append(jnp.where(lanes == lane, moved, 0.0))
                        slots.append(pl.ds(pl.multiple_of(tile * 8, 8), 8))
                    for g in range(groups):
                        own = range(g * group, (g + 1) * group)
                        held = {u: out[slots[u], :] for u in own}
                        for u in own:
                            value = held[u] + terms[u]
                            for w in range(g * group, u):
                                value = value + jnp.where(tiles[w] == tiles[u], terms[w], 0.0)
                            held[u] = value
                        for u in own:
                            out[slots[u], :] = held[u]
    count, width_y = inner.shape[0] + 2 * reach, inner.shape[1]
    for part, part_out, border in ((inner, inner_out, False), (outer, outer_out, True)):
        for i, x in enumerate(rows_of(count, border)):
            part_out[i] = part[i] + injected(out, x, blocks[0].shape[1] - 1, width_y)


def pair_kernel(keep, arrived, _, *outs):
    mine = lax.axis_index("shot") // 2
    for m in range(len(outs)):
        outs[m][...] = keep[mine ^ m] + arrived[mine ^ m]


def sum_kernel(*refs):
    total = refs[0][...]
    for ref in refs[1:-1]:
        total = total + ref[...]
    refs[-1][...] = total


def vmem(*shape):
    return VMEM(shape, jnp.float32)


def plain(*shape):
    return jax.ShapeDtypeStruct(shape, jnp.float32)


def call(name, kernel, args, outs, scratch=(), spaces=None, out_spaces=None, micros=2, aliases=None):
    spec = lambda space: pl.BlockSpec(memory_space=space)
    spaces = spaces or {}
    args = [
        pltpu.with_memory_space_constraint(arg, HBM) if spaces.get(i) is HBM else arg
        for i, arg in enumerate(args)
    ]
    out_spaces = out_spaces or {}
    return pl.pallas_call(
        kernel,
        out_shape=outs,
        in_specs=[spec(spaces.get(i, VMEM)) for i in range(len(args))],
        out_specs=[spec(out_spaces.get(i, VMEM)) for i in range(len(outs))],
        scratch_shapes=scratch,
        input_output_aliases=aliases or {},
        compiler_params=pltpu.CompilerParams(vmem_limit_bytes=limit),
        cost_estimate=pl.CostEstimate(
            flops=micros * 1000000000, bytes_accessed=micros << 16, transcendentals=0
        ),
        name=name,
    )(*args)


def pair_swap(count, start):
    pairs = []
    for i in range(start, count - 1, 2):
        pairs += [(i, i + 1), (i + 1, i)]
    return pairs


def body(
    state_before,
    state_now,
    adjoint_after,
    adjoint_now,
    speed_term,
    wavelet,
    source,
    receivers,
    traces,
):
    count, width_y, width_z = speed_term.shape
    steps = wavelet.shape[1]
    slabs = lax.axis_size("slab")
    shots = lax.axis_size("shot")
    half = steps // 2
    scale = 1.0 / (8.0 * steps)
    even_pairs, odd_pairs = pair_swap(slabs, 0), pair_swap(slabs, 1)
    inner = count - 2 * reach
    field = vmem(count, width_y, width_z)
    part = {False: vmem(inner, width_y, width_z), True: vmem(2 * reach, width_y, width_z)}
    edge = vmem(reach, width_y, width_z)
    dma = pltpu.SemaphoreType.DMA

    def swap(even, odd):
        return lax.ppermute(even, "slab", even_pairs), lax.ppermute(odd, "slab", odd_pairs)

    right = jnp.asarray(band_right(width_z))
    left = jnp.asarray(band_left(width_y))

    blocks = [traces]
    bit = 1
    while bit < slabs:
        held = blocks[0]
        if len(blocks) > 1:
            (held,) = call("stack", stack_kernel, blocks, [vmem(bit, *traces.shape[1:])], micros=0)
        blocks.append(lax.ppermute(held, "slab", [(i, i ^ bit) for i in range(slabs)]))
        bit *= 2

    p0_even, p0_odd, q8_even, q8_odd = call(
        "edges", edges_kernel, [state_now[0], adjoint_now[0]], [edge] * 4, [dma((4,))], {0: HBM, 1: HBM}
    )
    p_halo = swap(p0_even, p0_odd)
    q_halo = swap(q8_even, q8_odd)
    tiles = vmem(((count + 2 * reach) * width_y + 1) * 8, width_z)
    pair_of_parts = [part[False], part[True]]
    *loaded, speed, where_to, zeros = call(
        "load",
        load_kernel,
        [receivers, state_before[0], state_now[0], speed_term, held],
        pair_of_parts * 2 + [field, VMEM((1, receivers.shape[2]), jnp.int32), tiles],
        [VMEM(receivers.shape[1:], jnp.int32), dma((8,))],
        {i: HBM for i in range(4)},
        micros=1,
    )
    p = {-1: loaded[0:2], 0: loaded[2:4]}
    q = {}
    laps, acc = {}, {False: None, True: None}
    inject = None

    def forward(k, border, halos=(), after=()):
        last = k == steps - 1
        parts = dict(
            border=border, moves=not last, stores=k < half, adds=k >= half, opens=k == half, step=k,
            scale=scale, after=len(after) > 0,
        )
        args = [*p[k], *halos, right, left]
        outs, scratch, spaces = [], [part[True]] if border else [], {}
        if not last:
            spaces = {len(args) + 2: HBM, len(args) + 3: HBM}
            args += [p[k - 1][border], speed, source, wavelet]
            outs += [part[border]]
            scratch += [SMEM(source.shape, jnp.int32), SMEM(wavelet.shape, jnp.float32), dma, dma]
            if border:
                outs += [edge, edge]
        if parts["stores"]:
            outs += [part[border]]
        if parts["adds"]:
            args += [q[k + 1][border]]
            if not parts["opens"]:
                args += [acc[border]]
            if not last:
                outs += [part[border]]
        if last:
            args += [q[1][border], laps[0][border]]
            if border:
                args += [acc[False]]
                outs += [vmem(shots // 2, count, width_y // shots, width_z)] * 2
                scratch += [part[True]]
            else:
                outs += [part[False]]
        args += after
        name = "forward_border" if border else "forward_inner"
        got = list(
            call(
                name, functools.partial(forward_kernel, parts), args, outs, scratch, spaces,
                micros=0 if last and border else 1,
            )
        )
        if last and not border:
            acc[False] = got[0]
        if last:
            return got
        p.setdefault(k + 1, [None, None])[border] = got.pop(0)
        sides = [got.pop(0), got.pop(0)] if border else None
        if parts["stores"]:
            laps.setdefault(k, [None, None])[border] = got[0]
        else:
            acc[border] = got[0]
        return sides

    def adjoint(k, border, halos=(), opening=None, after=()):
        last = k == steps - 1
        t = steps - 1 - k
        parts = dict(
            border=border, adds=k >= half and not last, last=last, time=t, injects=k > 0, late=k == 1,
            after=len(after) > 0,
        )
        args = [*q[t + 1], *halos, right, left, q[t + 2][border], speed]
        outs, scratch, out_spaces, aliases = [part[border]], [part[True]] if border else [], {}, {}
        spaces = {}
        if k > 0:
            args += [inject]
        if parts["adds"]:
            args += [laps[t][border], acc[border]]
        if last:
            whole = plain(count, width_y, width_z)
            outs = [whole] if border else [whole, whole]
            out_spaces = {i: HBM for i in range(len(outs))}
            scratch += [part[border], dma((5,))]
            if border:
                spaces, aliases = {len(args): HBM}, {len(args): 0}
                args += [opening]
        elif border:
            outs += [edge, edge]
        if parts["adds"]:
            outs += [part[border]]
        args += after
        name = "adjoint_border" if border else "adjoint_inner"
        got = call(
            name, functools.partial(adjoint_kernel, parts), args, outs, scratch, spaces, out_spaces,
            micros=30 if last else 1, aliases=aliases,
        )
        if last:
            return got
        q.setdefault(t, [None, None])[border] = got[0]
        if parts["adds"]:
            acc[border] = got[-1]
        return got[1:3] if border else None

    forward(0, False)
    for k in range(steps - 1):
        first = [q[steps - 1 - k][False]] if k > 1 else []
        p_halo = swap(*forward(k, True, p_halo, first))
        if k == 0:
            loaded = call(
                "load_adjoint",
                load_adjoint_kernel,
                [adjoint_after[0], adjoint_now[0], p[1][True]],
                pair_of_parts * 2,
                [dma((6,))],
                {0: HBM, 1: HBM},
                micros=1,
            )
            q.update({steps + 1: loaded[0:2], steps: loaded[2:4]})
            adjoint(0, False)
        if k == 1:
            at = 1 + len(blocks)
            inject, *q[steps - 1] = call(
                "receivers",
                functools.partial(scatter_kernel, len(blocks)),
                [where_to, *blocks, *q[steps - 1], p[2][True], zeros],
                [tiles, *pair_of_parts],
                (),
                {0: SMEM},
                micros=0,
                aliases={at: 1, at + 1: 2, at + 3: 0},
            )
            adjoint(1, False)
        forward(k + 1, False)
        first = [acc[False] if k + 1 == steps - 1 else p[k + 2][False]]
        q_halo = swap(*adjoint(k, True, q_halo, after=first))
        if 0 < k < steps - 2:
            adjoint(k + 1, False)
    send, kept = forward(steps - 1, True, p_halo)
    arrived = lax.ppermute(send, "shot", [(i, i ^ 1) for i in range(shots)])
    opening, second = adjoint(steps - 1, False)
    piece = vmem(count, width_y // shots, width_z)
    pieces = call(
        "pair", pair_kernel, [kept, arrived, opening], [piece] * (shots // 2), (), {2: HBM}, micros=0
    )
    terms = [pieces[0]] + [
        lax.ppermute(pieces[m], "shot", [(i, i ^ (2 * m)) for i in range(shots)])
        for m in range(1, shots // 2)
    ]
    (opening,) = adjoint(steps - 1, True, q_halo, opening)
    (gradient,) = call("sum", sum_kernel, terms, [plain(count, width_y // shots, width_z)], micros=0)
    return (opening[None], second[None], gradient)


def solution(mesh):
    return jax.shard_map(
        body,
        mesh=mesh,
        in_specs=(
            P("shot", "slab", None, None),
            P("shot", "slab", None, None),
            P("shot", "slab", None, None),
            P("shot", "slab", None, None),
            P("slab", None, None),
            P("shot", None),
            P("shot", None),
            P("shot", None, None),
            P("shot", None, "slab"),
        ),
        out_specs=(
            P("shot", "slab", None, None),
            P("shot", "slab", None, None),
            P("slab", "shot", None),
        ),
        check_vma=False,
    )
```

```python
import functools

import jax
import jax.numpy as jnp
import ml_dtypes
import numpy as np
from jax import lax
from jax.experimental import pallas as pl
from jax.experimental.pallas import tpu as pltpu
from jax.sharding import PartitionSpec as P

weights = (-205.0 / 72.0, 8.0 / 5.0, -1.0 / 5.0, 8.0 / 315.0, -1.0 / 560.0)
reach = 4
VMEM = pltpu.VMEM
SMEM = pltpu.SMEM
HBM = pltpu.HBM
limit = 12 * 1024 * 1024


def band(width, centre):
    out = np.zeros((width, width), np.float64)
    for k in range(1, reach + 1):
        out += weights[k] * (np.eye(width, k=k) + np.eye(width, k=-k))
    out += centre * np.eye(width)
    high = out.astype(np.float32).astype(ml_dtypes.bfloat16)
    low = (out - high.astype(np.float64)).astype(np.float32).astype(ml_dtypes.bfloat16)
    return high, low


def band_right(width):
    high, low = band(width, 3.0 * weights[0])
    return np.block([[high, low], [high, np.zeros_like(low)]])


def band_left(width):
    high, low = band(width, 0.0)
    return np.block([[high, high], [low, np.zeros_like(low)]])


def split(v):
    high = v.astype(jnp.bfloat16)
    low = (v - high.astype(jnp.float32)).astype(jnp.bfloat16)
    return high, low


def fill_halo(parity, even, odd, halo):
    @pl.when(parity == 0)
    def _():
        halo[:reach] = odd[...]
        halo[reach:] = even[...]

    @pl.when(parity != 0)
    def _():
        halo[:reach] = even[...]
        halo[reach:] = odd[...]


def emit_edges(parity, outer, even, odd):
    @pl.when(parity == 0)
    def _():
        even[...] = outer[reach:]
        odd[...] = outer[:reach]

    @pl.when(parity != 0)
    def _():
        even[...] = outer[:reach]
        odd[...] = outer[reach:]


def rows_of(count, border):
    if border:
        return list(range(reach)) + list(range(count - reach, count))
    return list(range(reach, count - reach))


def laplace_rows(border, inner, outer, halo, right, left, put):
    count, width_y, width_z = inner.shape[0] + 2 * reach, inner.shape[1], inner.shape[2]

    def plane(i):
        if i < 0:
            return halo[reach + i]
        if i < reach:
            return outer[i]
        if i < count - reach:
            return inner[i - reach]
        if i < count:
            return outer[i - count + 2 * reach]
        return halo[reach + i - count]

    rows = rows_of(count, border)
    for i in range(0, len(rows), 2):
        x = rows[i]
        v = [plane(x), plane(x + 1)]
        (h0, l0), (h1, l1) = split(v[0]), split(v[1])
        flat = jnp.concatenate(
            [jnp.concatenate([h0, l0], axis=1), jnp.concatenate([h1, l1], axis=1)], axis=0
        )
        along = jnp.dot(flat, right[...], preferred_element_type=jnp.float32)
        cols = jnp.concatenate(
            [jnp.concatenate([h0, h1], axis=1), jnp.concatenate([l0, l1], axis=1)], axis=0
        )
        across = jnp.dot(left[...], cols, preferred_element_type=jnp.float32)
        for j in range(2):
            rows_j = slice(j * width_y, (j + 1) * width_y)
            lanes_j = slice(j * width_z, (j + 1) * width_z)
            lap = along[rows_j, :width_z] + along[rows_j, width_z:]
            lap = lap + (across[:width_y, lanes_j] + across[width_y:, lanes_j])
            for k in range(1, reach + 1):
                lap = lap + weights[k] * (plane(x + j + k) + plane(x + j - k))
            put(i + j, x + j, v[j], lap)


def forward_kernel(parts, *refs):
    it = iter(refs)
    border, moves, stores = parts["border"], parts["moves"], parts["stores"]
    adds, opens = parts["adds"], parts["opens"]
    inner, outer = next(it), next(it)
    even, odd = (next(it), next(it)) if border else (None, None)
    right, left = next(it), next(it)
    prev, speed, source, wave = [next(it) for _ in range(4)] if moves else (None,) * 4
    late = next(it) if adds else None
    acc_in = next(it) if adds and not opens else None
    first, lap_first = (next(it), next(it)) if not moves else (None, None)
    total_inner = next(it) if border and not moves else None
    for _ in range(parts["after"]):
        next(it)
    nxt = next(it) if moves else None
    even_out, odd_out = (next(it), next(it)) if moves and border else (None, None)
    token = next(it) if parts["token"] else None
    lap_out = next(it) if stores else None
    acc_out = next(it) if adds and moves else None
    send, keep = (next(it), next(it)) if border and not moves else (None, None)
    halo = next(it) if border else None
    if moves:
        spot_smem, wave_smem, spot_sem, wave_sem = [next(it) for _ in range(4)]
        spot_copy = pltpu.make_async_copy(source, spot_smem, spot_sem)
        wave_copy = pltpu.make_async_copy(wave, wave_smem, wave_sem)
        spot_copy.start()
        wave_copy.start()
    total = next(it) if not moves else None
    slab = lax.axis_index("slab")
    parity = slab % 2
    count = inner.shape[0] + 2 * reach
    if border:
        fill_halo(parity, even, odd, halo)

    def put(i, x, v, lap):
        if moves:
            nxt[i] = 2.0 * v - prev[i] + speed[x] * lap
        if stores:
            lap_out[i] = lap
        if adds:
            value = lap * late[i]
            if not opens:
                value = value + acc_in[i]
            if moves:
                acc_out[i] = value
            else:
                total[i] = (value + first[i] * lap_first[i]) * parts["scale"]

    laplace_rows(border, inner, outer, halo, right, left, put)
    if moves:
        spot_copy.wait()
        wave_copy.wait()
        row = spot_smem[0, 0] - slab * count
        col, lane = spot_smem[0, 1], spot_smem[0, 2]
        within = (row >= reach) & (row < count - reach)
        place = row - reach
        if border:
            within = (row >= 0) & (row < count) & jnp.logical_not(within)
            place = jnp.where(row < reach, row, row - count + 2 * reach)

        @pl.when(within)
        def _():
            tile = pl.ds(pl.multiple_of((col // 8) * 8, 8), 8)
            shape = (8, inner.shape[2])
            hit = (lax.broadcasted_iota(jnp.int32, shape, 0) == col % 8) & (
                lax.broadcasted_iota(jnp.int32, shape, 1) == lane
            )
            added = jnp.where(hit, wave_smem[0, parts["step"]], 0.0)
            nxt[place, tile, :] = nxt[place, tile, :] + added

        if border:
            emit_edges(parity, nxt, even_out, odd_out)
        if parts["token"]:
            token[...] = nxt[0, :8, :]
    elif border:
        chunk = send.shape[2]
        mine = lax.axis_index("shot") % 2
        for j in range(send.shape[0]):
            away = pl.multiple_of((2 * j + 1 - mine) * chunk, 8)
            here = pl.multiple_of((2 * j + mine) * chunk, 8)
            for out, first_row in ((send, away), (keep, here)):
                rows = pl.ds(first_row, chunk)
                out[j, :reach] = total[:reach, rows, :]
                out[j, reach : count - reach] = total_inner[:, rows, :]
                out[j, count - reach :] = total[reach:, rows, :]


def part_copies(border, part, whole, sems, to_whole):
    count = whole.shape[0]
    if border:
        pieces = [(0, 0, reach), (reach, count - reach, reach)]
    else:
        pieces = [(0, reach, count - 2 * reach)]
    copies = []
    for n, (i, x, rows) in enumerate(pieces):
        near, far = part.at[pl.ds(i, rows)], whole.at[pl.ds(x, rows)]
        ends = (near, far) if to_whole else (far, near)
        copies.append(pltpu.make_async_copy(*ends, sems.at[n]))
    return copies


def injected(tiles, x, time, width_y):
    return tiles[pl.ds((x + reach) * width_y * 8 + time, width_y, stride=8), :]


def adjoint_kernel(parts, *refs):
    it = iter(refs)
    border, adds, last = parts["border"], parts["adds"], parts["last"]
    inner, outer = next(it), next(it)
    even, odd = (next(it), next(it)) if border else (None, None)
    right, left, later, speed = [next(it) for _ in range(4)]
    inject = next(it) if parts["injects"] else None
    lap_of, acc_in = (next(it), next(it)) if adds else (None, None)
    if last and border:
        next(it)
    for _ in range(parts["after"]):
        next(it)
    nxt = next(it)
    second = next(it) if last and not border else None
    even_out, odd_out = (next(it), next(it)) if border and not last else (None, None)
    acc_out = next(it) if adds else None
    halo = next(it) if border else None
    part, copies = nxt, []
    if last:
        part, sems = next(it), next(it)
    parity = lax.axis_index("slab") % 2
    count, width_y = inner.shape[0] + 2 * reach, inner.shape[1]
    if border:
        fill_halo(parity, even, odd, halo)
        if parts["late"]:
            for i in range(2 * reach):
                x = i - reach if i < reach else count + i - reach
                halo[i] = halo[i] + injected(inject, x, parts["time"] + 1, width_y)
    elif last:
        copies += part_copies(True, outer, second, sems.at[pl.ds(2, 2)], True)
        copies += part_copies(False, inner, second, sems.at[pl.ds(4, 1)], True)
        for copy in copies:
            copy.start()

    def put(i, x, v, lap):
        value = 2.0 * v - later[i] + speed[x] * lap
        part[i] = value + injected(inject, x, parts["time"], width_y) if parts["injects"] else value
        if adds:
            acc_out[i] = acc_in[i] + v * lap_of[i]

    laplace_rows(border, inner, outer, halo, right, left, put)
    if last:
        for copy in part_copies(border, part, nxt, sems, True):
            copy.start()
            copies.append(copy)
    elif border:
        emit_edges(parity, part, even_out, odd_out)
    for copy in copies:
        copy.wait()


def edges_kernel(*refs):
    fields, traces, outs, traces_out, sems = refs[:2], refs[2], refs[3:7], *refs[7:]
    parity = lax.axis_index("slab") % 2
    top = fields[0].shape[0] - reach
    starts = (top * (1 - parity), top * parity)
    copies = []
    for i in range(4):
        rows = pl.ds(starts[i % 2], reach)
        copies.append(pltpu.make_async_copy(fields[i // 2].at[rows], outs[i], sems.at[i]))
    copies.append(pltpu.make_async_copy(traces, traces_out, sems.at[4]))
    for copy in copies:
        copy.start()
    for copy in copies:
        copy.wait()


def stack_kernel(*refs):
    first = 0
    for ref in refs[:-1]:
        refs[-1][first : first + ref.shape[0]] = ref[...]
        first += ref.shape[0]


def load_kernel(listen, *refs):
    fields, bands, parts, speed, refs = refs[:3], refs[4:6], refs[6:10], refs[10], refs[11:]
    bands_out, where_to, tiles, sems = refs[:2], *refs[2:]
    copies = [pltpu.make_async_copy(bands[i], bands_out[i], sems.at[7 + i]) for i in range(2)]
    copies.append(pltpu.make_async_copy(fields[2], speed, sems.at[6]))
    for i in range(2):
        copies += part_copies(False, parts[2 * i], fields[i], sems.at[pl.ds(3 * i, 1)], False)
        copies += part_copies(True, parts[2 * i + 1], fields[i], sems.at[pl.ds(3 * i + 1, 2)], False)
    for copy in copies:
        copy.start()
    zero_rows = 64 * 8

    @pl.loop(0, tiles.shape[0] // zero_rows)
    def _(i):
        tiles[pl.ds(pl.multiple_of(i * zero_rows, 8), zero_rows), :] = jnp.zeros(
            (zero_rows, 128), jnp.float32
        )

    rest = tiles.shape[0] % zero_rows
    if rest:
        tiles[tiles.shape[0] - rest :, :] = jnp.zeros((rest, 128), jnp.float32)
    for copy in copies:
        copy.wait()
    count, width_y, width_z = fields[0].shape
    held = count + 2 * reach
    depth = listen[0:1, :] - lax.axis_index("slab") * count + reach
    inside = (depth >= 0) & (depth < held)
    flat = depth * (width_y * width_z) + listen[1:2, :] * width_z + listen[2:3, :]
    where_to[...] = jnp.where(inside, flat, held * width_y * width_z)


def load_adjoint_kernel(*refs):
    fields, parts, sems = refs[:2], refs[3:7], refs[7]
    copies = []
    for i in range(2):
        copies += part_copies(False, parts[2 * i], fields[i], sems.at[pl.ds(3 * i, 1)], False)
        copies += part_copies(True, parts[2 * i + 1], fields[i], sems.at[pl.ds(3 * i + 1, 2)], False)
    for copy in copies:
        copy.start()
    for copy in copies:
        copy.wait()


def scatter_kernel(levels, where_to, *refs):
    blocks, refs = refs[:levels], refs[levels:]
    inner, outer, _, _, out, inner_out, outer_out = refs
    per = blocks[0].shape[-1]
    group, groups = 8, 4
    slab = lax.axis_index("slab")
    lanes = lax.broadcasted_iota(jnp.int32, (8, 128), 1)
    d = 0
    for held_blocks in blocks:
        for e in range(held_blocks.shape[0]):
            base = (slab ^ d) * per
            d += 1
            for part in range(per // 128):
                block = held_blocks[e, :, part * 128 : (part + 1) * 128]

                @pl.loop(0, 128 // (group * groups))
                def _(i):
                    tiles, terms, slots = [], [], []
                    for u in range(group * groups):
                        j = i * (group * groups) + u
                        flat = where_to[0, base + part * 128 + j]
                        lane = flat & 127
                        tile = flat >> 7
                        moved = pltpu.roll(block, (lane - j) & 127, 1)
                        tiles.append(jnp.full((8, 128), tile, jnp.int32))
                        terms.append(jnp.where(lanes == lane, moved, 0.0))
                        slots.append(pl.ds(pl.multiple_of(tile * 8, 8), 8))
                    for g in range(groups):
                        own = range(g * group, (g + 1) * group)
                        held = {u: out[slots[u], :] for u in own}
                        for u in own:
                            value = held[u] + terms[u]
                            for w in range(g * group, u):
                                value = value + jnp.where(tiles[w] == tiles[u], terms[w], 0.0)
                            held[u] = value
                        for u in own:
                            out[slots[u], :] = held[u]
    count, width_y = inner.shape[0] + 2 * reach, inner.shape[1]
    for part, part_out, border in ((inner, inner_out, False), (outer, outer_out, True)):
        for i, x in enumerate(rows_of(count, border)):
            part_out[i] = part[i] + injected(out, x, blocks[0].shape[1] - 1, width_y)


def pair_kernel(keep, arrived, _, *outs):
    mine = lax.axis_index("shot") // 2
    for m in range(len(outs)):
        outs[m][...] = keep[mine ^ m] + arrived[mine ^ m]


def sum_kernel(*refs):
    total = refs[0][...]
    for ref in refs[1:-1]:
        total = total + ref[...]
    refs[-1][...] = total


def vmem(*shape):
    return VMEM(shape, jnp.float32)


def plain(*shape):
    return jax.ShapeDtypeStruct(shape, jnp.float32)


def call(name, kernel, args, outs, scratch=(), spaces=None, out_spaces=None, micros=2, aliases=None):
    spec = lambda space: pl.BlockSpec(memory_space=space)
    spaces = spaces or {}
    args = [
        pltpu.with_memory_space_constraint(arg, HBM) if spaces.get(i) is HBM else arg
        for i, arg in enumerate(args)
    ]
    out_spaces = out_spaces or {}
    return pl.pallas_call(
        kernel,
        out_shape=outs,
        in_specs=[spec(spaces.get(i, VMEM)) for i in range(len(args))],
        out_specs=[spec(out_spaces.get(i, VMEM)) for i in range(len(outs))],
        scratch_shapes=scratch,
        input_output_aliases=aliases or {},
        compiler_params=pltpu.CompilerParams(vmem_limit_bytes=limit),
        cost_estimate=pl.CostEstimate(
            flops=micros * 1000000000, bytes_accessed=micros << 16, transcendentals=0
        ),
        name=name,
    )(*args)


def pair_swap(count, start):
    pairs = []
    for i in range(start, count - 1, 2):
        pairs += [(i, i + 1), (i + 1, i)]
    return pairs


def body(
    state_before,
    state_now,
    adjoint_after,
    adjoint_now,
    speed_term,
    wavelet,
    source,
    receivers,
    traces,
):
    count, width_y, width_z = speed_term.shape
    steps = wavelet.shape[1]
    slabs = lax.axis_size("slab")
    shots = lax.axis_size("shot")
    half = steps // 2
    scale = 1.0 / (8.0 * steps)
    even_pairs, odd_pairs = pair_swap(slabs, 0), pair_swap(slabs, 1)
    inner = count - 2 * reach
    field = vmem(count, width_y, width_z)
    part = {False: vmem(inner, width_y, width_z), True: vmem(2 * reach, width_y, width_z)}
    edge = vmem(reach, width_y, width_z)
    dma = pltpu.SemaphoreType.DMA

    def swap(even, odd):
        return lax.ppermute(even, "slab", even_pairs), lax.ppermute(odd, "slab", odd_pairs)

    p0_even, p0_odd, q8_even, q8_odd, own = call(
        "edges",
        edges_kernel,
        [state_now[0], adjoint_now[0], traces],
        [edge] * 4 + [vmem(*traces.shape)],
        [dma((5,))],
        {0: HBM, 1: HBM, 2: HBM},
    )
    p_halo = swap(p0_even, p0_odd)
    q_halo = swap(q8_even, q8_odd)
    blocks = [own]
    bit = 1
    while bit < slabs:
        held = traces
        if len(blocks) > 1:
            (held,) = call("stack", stack_kernel, blocks, [vmem(bit, *traces.shape[1:])], micros=0)
        blocks.append(lax.ppermute(held, "slab", [(i, i ^ bit) for i in range(slabs)]))
        bit *= 2
    tiles = vmem(((count + 2 * reach) * width_y + 1) * 8, width_z)
    pair_of_parts = [part[False], part[True]]
    bands = [jnp.asarray(band_right(width_z)), jnp.asarray(band_left(width_y))]
    *loaded, speed, right, left, where_to, zeros = call(
        "load",
        load_kernel,
        [receivers[0], state_before[0], state_now[0], speed_term, held, *bands],
        pair_of_parts * 2
        + [field, *(VMEM(band.shape, band.dtype) for band in bands)]
        + [VMEM((1, receivers.shape[2]), jnp.int32), tiles],
        [dma((9,))],
        {i: HBM for i in (1, 2, 3, 5, 6)},
        micros=1,
    )
    p = {-1: loaded[0:2], 0: loaded[2:4]}
    q = {}
    laps, acc = {}, {False: None, True: None}
    inject = None
    meets, met = (1, 3, 5), {}

    def forward(k, border, halos=(), after=()):
        last = k == steps - 1
        token = border and k in meets
        parts = dict(
            border=border, moves=not last, stores=k < half, adds=k >= half, opens=k == half, step=k,
            scale=scale, after=len(after), token=token,
        )
        args = [*p[k], *halos, right, left]
        outs, scratch, spaces = [], [part[True]] if border else [], {}
        if not last:
            spaces = {len(args) + 2: HBM, len(args) + 3: HBM}
            args += [p[k - 1][border], speed, source, wavelet]
            outs += [part[border]]
            scratch += [SMEM(source.shape, jnp.int32), SMEM(wavelet.shape, jnp.float32), dma, dma]
            if border:
                outs += [edge, edge]
            if token:
                outs += [vmem(8, width_z)]
        if parts["stores"]:
            outs += [part[border]]
        if parts["adds"]:
            args += [q[k + 1][border]]
            if not parts["opens"]:
                args += [acc[border]]
            if not last:
                outs += [part[border]]
        if last:
            args += [q[1][border], laps[0][border]]
            if border:
                args += [acc[False]]
                outs += [vmem(shots // 2, count, width_y // shots, width_z)] * 2
                scratch += [part[True]]
            else:
                outs += [part[False]]
        args += after
        name = "forward_border" if border else "forward_inner"
        got = list(
            call(
                name, functools.partial(forward_kernel, parts), args, outs, scratch, spaces,
                micros=0 if last and border else 1,
            )
        )
        if last and not border:
            acc[False] = got[0]
        if last:
            return got
        p.setdefault(k + 1, [None, None])[border] = got.pop(0)
        sides = [got.pop(0), got.pop(0)] if border else None
        if token:
            met[k] = lax.ppermute(got.pop(0), "shot", [(i, i ^ 1) for i in range(shots)])
        if parts["stores"]:
            laps.setdefault(k, [None, None])[border] = got[0]
        else:
            acc[border] = got[0]
        return sides

    def adjoint(k, border, halos=(), opening=None, after=()):
        last = k == steps - 1
        t = steps - 1 - k
        parts = dict(
            border=border, adds=k >= half and not last, last=last, time=t, injects=k > 0, late=k == 1,
            after=len(after),
        )
        args = [*q[t + 1], *halos, right, left, q[t + 2][border], speed]
        outs, scratch, out_spaces, aliases = [part[border]], [part[True]] if border else [], {}, {}
        spaces = {}
        if k > 0:
            args += [inject]
        if parts["adds"]:
            args += [laps[t][border], acc[border]]
        if last:
            whole = plain(count, width_y, width_z)
            outs = [whole] if border else [whole, whole]
            out_spaces = {i: HBM for i in range(len(outs))}
            scratch += [part[border], dma((5,))]
            if border:
                spaces, aliases = {len(args): HBM}, {len(args): 0}
                args += [opening]
        elif border:
            outs += [edge, edge]
        if parts["adds"]:
            outs += [part[border]]
        args += after
        name = "adjoint_border" if border else "adjoint_inner"
        got = call(
            name, functools.partial(adjoint_kernel, parts), args, outs, scratch, spaces, out_spaces,
            micros=30 if last else 1, aliases=aliases,
        )
        if last:
            return got
        q.setdefault(t, [None, None])[border] = got[0]
        if parts["adds"]:
            acc[border] = got[-1]
        return got[1:3] if border else None

    forward(0, False)
    for k in range(steps - 1):
        first = [q[steps - 1 - k][False]] if k > 1 else []
        p_halo = swap(*forward(k, True, p_halo, first))
        if k == 0:
            loaded = call(
                "load_adjoint",
                load_adjoint_kernel,
                [adjoint_after[0], adjoint_now[0], p[1][True]],
                pair_of_parts * 2,
                [dma((6,))],
                {0: HBM, 1: HBM},
                micros=1,
            )
            q.update({steps + 1: loaded[0:2], steps: loaded[2:4]})
            adjoint(0, False)
        if k == 1:
            at = 1 + len(blocks)
            inject, *q[steps - 1] = call(
                "receivers",
                functools.partial(scatter_kernel, len(blocks)),
                [where_to, *blocks, *q[steps - 1], p[2][True], zeros],
                [tiles, *pair_of_parts],
                (),
                {0: SMEM},
                micros=0,
                aliases={at: 1, at + 1: 2, at + 3: 0},
            )
            adjoint(1, False)
        forward(k + 1, False)
        first = [acc[False] if k + 1 == steps - 1 else p[k + 2][False]]
        if k in meets:
            first += [met[k]]
        q_halo = swap(*adjoint(k, True, q_halo, after=first))
        if 0 < k < steps - 2:
            adjoint(k + 1, False)
    send, kept = forward(steps - 1, True, p_halo)
    arrived = lax.ppermute(send, "shot", [(i, i ^ 1) for i in range(shots)])
    opening, second = adjoint(steps - 1, False)
    piece = vmem(count, width_y // shots, width_z)
    pieces = call(
        "pair", pair_kernel, [kept, arrived, opening], [piece] * (shots // 2), (), {2: HBM}, micros=0
    )
    terms = [pieces[0]] + [
        lax.ppermute(pieces[m], "shot", [(i, i ^ (2 * m)) for i in range(shots)])
        for m in range(1, shots // 2)
    ]
    (opening,) = adjoint(steps - 1, True, q_halo, opening)
    (gradient,) = call("sum", sum_kernel, terms, [plain(count, width_y // shots, width_z)], micros=0)
    return (opening[None], second[None], gradient)


def solution(mesh):
    return jax.shard_map(
        body,
        mesh=mesh,
        in_specs=(
            P("shot", "slab", None, None),
            P("shot", "slab", None, None),
            P("shot", "slab", None, None),
            P("shot", "slab", None, None),
            P("slab", None, None),
            P("shot", None),
            P("shot", None),
            P("shot", None, None),
            P("shot", None, "slab"),
        ),
        out_specs=(
            P("shot", "slab", None, None),
            P("shot", "slab", None, None),
            P("slab", "shot", None),
        ),
        check_vma=False,
    )
```

```python
import functools

import jax
import jax.numpy as jnp
import ml_dtypes
import numpy as np
from jax import lax
from jax.experimental import pallas as pl
from jax.experimental.pallas import tpu as pltpu
from jax.sharding import PartitionSpec as P

weights = (-205.0 / 72.0, 8.0 / 5.0, -1.0 / 5.0, 8.0 / 315.0, -1.0 / 560.0)
reach = 4
VMEM = pltpu.VMEM
SMEM = pltpu.SMEM
HBM = pltpu.HBM
limit = 12 * 1024 * 1024


def band(width, centre):
    out = np.zeros((width, width), np.float64)
    for k in range(1, reach + 1):
        out += weights[k] * (np.eye(width, k=k) + np.eye(width, k=-k))
    out += centre * np.eye(width)
    high = out.astype(np.float32).astype(ml_dtypes.bfloat16)
    low = (out - high.astype(np.float64)).astype(np.float32).astype(ml_dtypes.bfloat16)
    return high, low


def band_right(width):
    high, low = band(width, 3.0 * weights[0])
    return np.block([[high, low], [high, np.zeros_like(low)]])


def band_left(width):
    high, low = band(width, 0.0)
    return np.block([[high, high], [low, np.zeros_like(low)]])


def split(v):
    high = v.astype(jnp.bfloat16)
    low = (v - high.astype(jnp.float32)).astype(jnp.bfloat16)
    return high, low


def fill_halo(parity, even, odd, halo):
    @pl.when(parity == 0)
    def _():
        halo[:reach] = odd[...]
        halo[reach:] = even[...]

    @pl.when(parity != 0)
    def _():
        halo[:reach] = even[...]
        halo[reach:] = odd[...]


def emit_edges(parity, outer, even, odd):
    @pl.when(parity == 0)
    def _():
        even[...] = outer[reach:]
        odd[...] = outer[:reach]

    @pl.when(parity != 0)
    def _():
        even[...] = outer[:reach]
        odd[...] = outer[reach:]


def rows_of(count, border):
    if border:
        return list(range(reach)) + list(range(count - reach, count))
    return list(range(reach, count - reach))


def laplace_rows(border, inner, outer, halo, right, left, put):
    count, width_y, width_z = inner.shape[0] + 2 * reach, inner.shape[1], inner.shape[2]

    def plane(i):
        if i < 0:
            return halo[reach + i]
        if i < reach:
            return outer[i]
        if i < count - reach:
            return inner[i - reach]
        if i < count:
            return outer[i - count + 2 * reach]
        return halo[reach + i - count]

    rows = rows_of(count, border)
    for i in range(0, len(rows), 2):
        x = rows[i]
        v = [plane(x), plane(x + 1)]
        (h0, l0), (h1, l1) = split(v[0]), split(v[1])
        flat = jnp.concatenate(
            [jnp.concatenate([h0, l0], axis=1), jnp.concatenate([h1, l1], axis=1)], axis=0
        )
        along = jnp.dot(flat, right[...], preferred_element_type=jnp.float32)
        cols = jnp.concatenate(
            [jnp.concatenate([h0, h1], axis=1), jnp.concatenate([l0, l1], axis=1)], axis=0
        )
        across = jnp.dot(left[...], cols, preferred_element_type=jnp.float32)
        for j in range(2):
            rows_j = slice(j * width_y, (j + 1) * width_y)
            lanes_j = slice(j * width_z, (j + 1) * width_z)
            lap = along[rows_j, :width_z] + along[rows_j, width_z:]
            lap = lap + (across[:width_y, lanes_j] + across[width_y:, lanes_j])
            for k in range(1, reach + 1):
                lap = lap + weights[k] * (plane(x + j + k) + plane(x + j - k))
            put(i + j, x + j, v[j], lap)


def forward_kernel(parts, *refs):
    it = iter(refs)
    border, moves, stores = parts["border"], parts["moves"], parts["stores"]
    adds, opens = parts["adds"], parts["opens"]
    inner, outer = next(it), next(it)
    even, odd = (next(it), next(it)) if border else (None, None)
    right, left = next(it), next(it)
    prev, speed, source, wave = [next(it) for _ in range(4)] if moves else (None,) * 4
    late = next(it) if adds else None
    acc_in = next(it) if adds and not opens else None
    first, lap_first = (next(it), next(it)) if not moves else (None, None)
    total_inner = next(it) if border and not moves else None
    for _ in range(parts["after"]):
        next(it)
    nxt = next(it) if moves else None
    even_out, odd_out = (next(it), next(it)) if moves and border else (None, None)
    lap_out = next(it) if stores else None
    acc_out = next(it) if adds and moves else None
    send, keep = (next(it), next(it)) if border and not moves else (None, None)
    halo = next(it) if border else None
    if moves:
        spot_smem, wave_smem, spot_sem, wave_sem = [next(it) for _ in range(4)]
        spot_copy = pltpu.make_async_copy(source, spot_smem, spot_sem)
        wave_copy = pltpu.make_async_copy(wave, wave_smem, wave_sem)
        spot_copy.start()
        wave_copy.start()
    total = next(it) if not moves else None
    slab = lax.axis_index("slab")
    parity = slab % 2
    count = inner.shape[0] + 2 * reach
    if border:
        fill_halo(parity, even, odd, halo)

    def put(i, x, v, lap):
        if moves:
            nxt[i] = 2.0 * v - prev[i] + speed[x] * lap
        if stores:
            lap_out[i] = lap
        if adds:
            value = lap * late[i]
            if not opens:
                value = value + acc_in[i]
            if moves:
                acc_out[i] = value
            else:
                total[i] = (value + first[i] * lap_first[i]) * parts["scale"]

    laplace_rows(border, inner, outer, halo, right, left, put)
    if moves:
        spot_copy.wait()
        wave_copy.wait()
        row = spot_smem[0, 0] - slab * count
        col, lane = spot_smem[0, 1], spot_smem[0, 2]
        within = (row >= reach) & (row < count - reach)
        place = row - reach
        if border:
            within = (row >= 0) & (row < count) & jnp.logical_not(within)
            place = jnp.where(row < reach, row, row - count + 2 * reach)

        @pl.when(within)
        def _():
            tile = pl.ds(pl.multiple_of((col // 8) * 8, 8), 8)
            shape = (8, inner.shape[2])
            hit = (lax.broadcasted_iota(jnp.int32, shape, 0) == col % 8) & (
                lax.broadcasted_iota(jnp.int32, shape, 1) == lane
            )
            added = jnp.where(hit, wave_smem[0, parts["step"]], 0.0)
            nxt[place, tile, :] = nxt[place, tile, :] + added

        if border:
            emit_edges(parity, nxt, even_out, odd_out)
    elif border:
        chunk = send.shape[2]
        mine = lax.axis_index("shot") % 2
        for j in range(send.shape[0]):
            away = pl.multiple_of((2 * j + 1 - mine) * chunk, 8)
            here = pl.multiple_of((2 * j + mine) * chunk, 8)
            for out, first_row in ((send, away), (keep, here)):
                rows = pl.ds(first_row, chunk)
                out[j, :reach] = total[:reach, rows, :]
                out[j, reach : count - reach] = total_inner[:, rows, :]
                out[j, count - reach :] = total[reach:, rows, :]


def part_copies(border, part, whole, sems, to_whole):
    count = whole.shape[0]
    if border:
        pieces = [(0, 0, reach), (reach, count - reach, reach)]
    else:
        pieces = [(0, reach, count - 2 * reach)]
    copies = []
    for n, (i, x, rows) in enumerate(pieces):
        near, far = part.at[pl.ds(i, rows)], whole.at[pl.ds(x, rows)]
        ends = (near, far) if to_whole else (far, near)
        copies.append(pltpu.make_async_copy(*ends, sems.at[n]))
    return copies


def injected(tiles, x, time, width_y):
    return tiles[pl.ds((x + reach) * width_y * 8 + time, width_y, stride=8), :]


def adjoint_kernel(parts, *refs):
    it = iter(refs)
    border, adds, last = parts["border"], parts["adds"], parts["last"]
    inner, outer = next(it), next(it)
    even, odd = (next(it), next(it)) if border else (None, None)
    right, left, later, speed = [next(it) for _ in range(4)]
    inject = next(it) if parts["injects"] else None
    lap_of, acc_in = (next(it), next(it)) if adds else (None, None)
    if last and border:
        next(it)
    for _ in range(parts["after"]):
        next(it)
    nxt = next(it)
    second = next(it) if last and not border else None
    even_out, odd_out = (next(it), next(it)) if border and not last else (None, None)
    acc_out = next(it) if adds else None
    halo = next(it) if border else None
    part, copies = nxt, []
    if last:
        part, sems = next(it), next(it)
    parity = lax.axis_index("slab") % 2
    count, width_y = inner.shape[0] + 2 * reach, inner.shape[1]
    if border:
        fill_halo(parity, even, odd, halo)
        if parts["late"]:
            for i in range(2 * reach):
                x = i - reach if i < reach else count + i - reach
                halo[i] = halo[i] + injected(inject, x, parts["time"] + 1, width_y)
    elif last:
        copies += part_copies(True, outer, second, sems.at[pl.ds(2, 2)], True)
        copies += part_copies(False, inner, second, sems.at[pl.ds(4, 1)], True)
        for copy in copies:
            copy.start()

    def put(i, x, v, lap):
        value = 2.0 * v - later[i] + speed[x] * lap
        part[i] = value + injected(inject, x, parts["time"], width_y) if parts["injects"] else value
        if adds:
            acc_out[i] = acc_in[i] + v * lap_of[i]

    laplace_rows(border, inner, outer, halo, right, left, put)
    if last:
        for copy in part_copies(border, part, nxt, sems, True):
            copy.start()
            copies.append(copy)
    elif border:
        emit_edges(parity, part, even_out, odd_out)
    for copy in copies:
        copy.wait()


def edges_kernel(*refs):
    fields, traces, outs, traces_out, sems = refs[:2], refs[2], refs[3:7], *refs[7:]
    parity = lax.axis_index("slab") % 2
    top = fields[0].shape[0] - reach
    starts = (top * (1 - parity), top * parity)
    copies = []
    for i in range(4):
        rows = pl.ds(starts[i % 2], reach)
        copies.append(pltpu.make_async_copy(fields[i // 2].at[rows], outs[i], sems.at[i]))
    copies.append(pltpu.make_async_copy(traces, traces_out, sems.at[4]))
    for copy in copies:
        copy.start()
    for copy in copies:
        copy.wait()


def stack_kernel(*refs):
    first = 0
    for ref in refs[:-1]:
        refs[-1][first : first + ref.shape[0]] = ref[...]
        first += ref.shape[0]


def load_kernel(listen, *refs):
    fields, bands, parts, speed, refs = refs[:3], refs[4:6], refs[6:10], refs[10], refs[11:]
    bands_out, where_to, tiles, sems = refs[:2], *refs[2:]
    copies = [pltpu.make_async_copy(bands[i], bands_out[i], sems.at[7 + i]) for i in range(2)]
    copies.append(pltpu.make_async_copy(fields[2], speed, sems.at[6]))
    for i in range(2):
        copies += part_copies(False, parts[2 * i], fields[i], sems.at[pl.ds(3 * i, 1)], False)
        copies += part_copies(True, parts[2 * i + 1], fields[i], sems.at[pl.ds(3 * i + 1, 2)], False)
    for copy in copies:
        copy.start()
    zero_rows = 64 * 8

    @pl.loop(0, tiles.shape[0] // zero_rows)
    def _(i):
        tiles[pl.ds(pl.multiple_of(i * zero_rows, 8), zero_rows), :] = jnp.zeros(
            (zero_rows, 128), jnp.float32
        )

    rest = tiles.shape[0] % zero_rows
    if rest:
        tiles[tiles.shape[0] - rest :, :] = jnp.zeros((rest, 128), jnp.float32)
    for copy in copies:
        copy.wait()
    count, width_y, width_z = fields[0].shape
    held = count + 2 * reach
    depth = listen[0:1, :] - lax.axis_index("slab") * count + reach
    inside = (depth >= 0) & (depth < held)
    flat = depth * (width_y * width_z) + listen[1:2, :] * width_z + listen[2:3, :]
    where_to[...] = jnp.where(inside, flat, held * width_y * width_z)


def load_adjoint_kernel(*refs):
    fields, parts, sems = refs[:2], refs[3:7], refs[7]
    copies = []
    for i in range(2):
        copies += part_copies(False, parts[2 * i], fields[i], sems.at[pl.ds(3 * i, 1)], False)
        copies += part_copies(True, parts[2 * i + 1], fields[i], sems.at[pl.ds(3 * i + 1, 2)], False)
    for copy in copies:
        copy.start()
    for copy in copies:
        copy.wait()


def scatter_kernel(levels, where_to, *refs):
    blocks, refs = refs[:levels], refs[levels:]
    inner, outer, _, _, out, inner_out, outer_out = refs
    per = blocks[0].shape[-1]
    group, groups = 8, 8
    slab = lax.axis_index("slab")
    lanes = lax.broadcasted_iota(jnp.int32, (8, 128), 1)
    d = 0
    for held_blocks in blocks:
        for e in range(held_blocks.shape[0]):
            base = (slab ^ d) * per
            d += 1
            for part in range(per // 128):
                block = held_blocks[e, :, part * 128 : (part + 1) * 128]

                @pl.loop(0, 128 // (group * groups))
                def _(i):
                    def gather(g):
                        tiles, terms, slots = [], [], []
                        for u in range(g * group, (g + 1) * group):
                            j = i * (group * groups) + u
                            flat = where_to[0, base + part * 128 + j]
                            lane = flat & 127
                            tile = flat >> 7
                            moved = pltpu.roll(block, (lane - j) & 127, 1)
                            tiles.append(jnp.full((8, 128), tile, jnp.int32))
                            terms.append(jnp.where(lanes == lane, moved, 0.0))
                            slots.append(pl.ds(pl.multiple_of(tile * 8, 8), 8))
                        return tiles, terms, slots

                    ahead = [gather(0), gather(1)]
                    for g in range(groups):
                        tiles, terms, slots = ahead.pop(0)
                        if g + 2 < groups:
                            ahead.append(gather(g + 2))
                        held = [out[slot, :] for slot in slots]
                        for u in range(group):
                            value = held[u] + terms[u]
                            for w in range(u):
                                value = value + jnp.where(tiles[w] == tiles[u], terms[w], 0.0)
                            held[u] = value
                        for u in range(group):
                            out[slots[u], :] = held[u]

    count, width_y = inner.shape[0] + 2 * reach, inner.shape[1]
    for part, part_out, border in ((inner, inner_out, False), (outer, outer_out, True)):
        for i, x in enumerate(rows_of(count, border)):
            part_out[i] = part[i] + injected(out, x, blocks[0].shape[1] - 1, width_y)


def pair_kernel(keep, arrived, _, *outs):
    mine = lax.axis_index("shot") // 2
    for m in range(len(outs)):
        outs[m][...] = keep[mine ^ m] + arrived[mine ^ m]


def sum_kernel(*refs):
    total = refs[0][...]
    for ref in refs[1:-1]:
        total = total + ref[...]
    refs[-1][...] = total


def vmem(*shape):
    return VMEM(shape, jnp.float32)


def plain(*shape):
    return jax.ShapeDtypeStruct(shape, jnp.float32)


def call(name, kernel, args, outs, scratch=(), spaces=None, out_spaces=None, micros=2, aliases=None):
    spec = lambda space: pl.BlockSpec(memory_space=space)
    spaces = spaces or {}
    args = [
        pltpu.with_memory_space_constraint(arg, HBM) if spaces.get(i) is HBM else arg
        for i, arg in enumerate(args)
    ]
    out_spaces = out_spaces or {}
    return pl.pallas_call(
        kernel,
        out_shape=outs,
        in_specs=[spec(spaces.get(i, VMEM)) for i in range(len(args))],
        out_specs=[spec(out_spaces.get(i, VMEM)) for i in range(len(outs))],
        scratch_shapes=scratch,
        input_output_aliases=aliases or {},
        compiler_params=pltpu.CompilerParams(vmem_limit_bytes=limit),
        cost_estimate=pl.CostEstimate(
            flops=micros * 1000000000, bytes_accessed=micros << 16, transcendentals=0
        ),
        name=name,
    )(*args)


def pair_swap(count, start):
    pairs = []
    for i in range(start, count - 1, 2):
        pairs += [(i, i + 1), (i + 1, i)]
    return pairs


def body(
    state_before,
    state_now,
    adjoint_after,
    adjoint_now,
    speed_term,
    wavelet,
    source,
    receivers,
    traces,
):
    count, width_y, width_z = speed_term.shape
    steps = wavelet.shape[1]
    slabs = lax.axis_size("slab")
    shots = lax.axis_size("shot")
    half = steps // 2
    scale = 1.0 / (8.0 * steps)
    even_pairs, odd_pairs = pair_swap(slabs, 0), pair_swap(slabs, 1)
    inner = count - 2 * reach
    field = vmem(count, width_y, width_z)
    part = {False: vmem(inner, width_y, width_z), True: vmem(2 * reach, width_y, width_z)}
    edge = vmem(reach, width_y, width_z)
    dma = pltpu.SemaphoreType.DMA

    def swap(even, odd):
        return lax.ppermute(even, "slab", even_pairs), lax.ppermute(odd, "slab", odd_pairs)

    p0_even, p0_odd, q8_even, q8_odd, own = call(
        "edges",
        edges_kernel,
        [state_now[0], adjoint_now[0], traces],
        [edge] * 4 + [vmem(*traces.shape)],
        [dma((5,))],
        {0: HBM, 1: HBM, 2: HBM},
    )
    p_halo = swap(p0_even, p0_odd)
    q_halo = swap(q8_even, q8_odd)
    blocks = [own]
    bit = 1
    while bit < slabs:
        held = traces
        if len(blocks) > 1:
            (held,) = call("stack", stack_kernel, blocks, [vmem(bit, *traces.shape[1:])], micros=0)
        blocks.append(lax.ppermute(held, "slab", [(i, i ^ bit) for i in range(slabs)]))
        bit *= 2
    tiles = vmem(((count + 2 * reach) * width_y + 1) * 8, width_z)
    pair_of_parts = [part[False], part[True]]
    bands = [jnp.asarray(band_right(width_z)), jnp.asarray(band_left(width_y))]
    *loaded, speed, right, left, where_to, zeros = call(
        "load",
        load_kernel,
        [receivers[0], state_before[0], state_now[0], speed_term, held, *bands],
        pair_of_parts * 2
        + [field, *(VMEM(band.shape, band.dtype) for band in bands)]
        + [VMEM((1, receivers.shape[2]), jnp.int32), tiles],
        [dma((9,))],
        {i: HBM for i in (1, 2, 3, 5, 6)},
        micros=1,
    )
    p = {-1: loaded[0:2], 0: loaded[2:4]}
    q = {}
    laps, acc = {}, {False: None, True: None}
    inject = None

    def forward(k, border, halos=(), after=()):
        last = k == steps - 1
        parts = dict(
            border=border, moves=not last, stores=k < half, adds=k >= half, opens=k == half, step=k,
            scale=scale, after=len(after),
        )
        args = [*p[k], *halos, right, left]
        outs, scratch, spaces = [], [part[True]] if border else [], {}
        if not last:
            spaces = {len(args) + 2: HBM, len(args) + 3: HBM}
            args += [p[k - 1][border], speed, source, wavelet]
            outs += [part[border]]
            scratch += [SMEM(source.shape, jnp.int32), SMEM(wavelet.shape, jnp.float32), dma, dma]
            if border:
                outs += [edge, edge]
        if parts["stores"]:
            outs += [part[border]]
        if parts["adds"]:
            args += [q[k + 1][border]]
            if not parts["opens"]:
                args += [acc[border]]
            if not last:
                outs += [part[border]]
        if last:
            args += [q[1][border], laps[0][border]]
            if border:
                args += [acc[False]]
                outs += [vmem(shots // 2, count, width_y // shots, width_z)] * 2
                scratch += [part[True]]
            else:
                outs += [part[False]]
        args += after
        name = "forward_border" if border else "forward_inner"
        got = list(
            call(
                name, functools.partial(forward_kernel, parts), args, outs, scratch, spaces,
                micros=0 if last and border else 1,
            )
        )
        if last and not border:
            acc[False] = got[0]
        if last:
            return got
        p.setdefault(k + 1, [None, None])[border] = got.pop(0)
        sides = [got.pop(0), got.pop(0)] if border else None
        if parts["stores"]:
            laps.setdefault(k, [None, None])[border] = got[0]
        else:
            acc[border] = got[0]
        return sides

    def adjoint(k, border, halos=(), opening=None, after=()):
        last = k == steps - 1
        t = steps - 1 - k
        parts = dict(
            border=border, adds=k >= half and not last, last=last, time=t, injects=k > 0, late=k == 1,
            after=len(after),
        )
        args = [*q[t + 1], *halos, right, left, q[t + 2][border], speed]
        outs, scratch, out_spaces, aliases = [part[border]], [part[True]] if border else [], {}, {}
        spaces = {}
        if k > 0:
            args += [inject]
        if parts["adds"]:
            args += [laps[t][border], acc[border]]
        if last:
            whole = plain(count, width_y, width_z)
            outs = [whole] if border else [whole, whole]
            out_spaces = {i: HBM for i in range(len(outs))}
            scratch += [part[border], dma((5,))]
            if border:
                spaces, aliases = {len(args): HBM}, {len(args): 0}
                args += [opening]
        elif border:
            outs += [edge, edge]
        if parts["adds"]:
            outs += [part[border]]
        args += after
        name = "adjoint_border" if border else "adjoint_inner"
        got = call(
            name, functools.partial(adjoint_kernel, parts), args, outs, scratch, spaces, out_spaces,
            micros=30 if last else 1, aliases=aliases,
        )
        if last:
            return got
        q.setdefault(t, [None, None])[border] = got[0]
        if parts["adds"]:
            acc[border] = got[-1]
        return got[1:3] if border else None

    forward(0, False)
    for k in range(steps - 1):
        first = [q[steps - 1 - k][False]] if k > 1 else []
        p_halo = swap(*forward(k, True, p_halo, first))
        if k == 0:
            loaded = call(
                "load_adjoint",
                load_adjoint_kernel,
                [adjoint_after[0], adjoint_now[0], p[1][True]],
                pair_of_parts * 2,
                [dma((6,))],
                {0: HBM, 1: HBM},
                micros=1,
            )
            q.update({steps + 1: loaded[0:2], steps: loaded[2:4]})
            adjoint(0, False)
        if k == 1:
            at = 1 + len(blocks)
            inject, *q[steps - 1] = call(
                "receivers",
                functools.partial(scatter_kernel, len(blocks)),
                [where_to, *blocks, *q[steps - 1], p[2][True], zeros],
                [tiles, *pair_of_parts],
                (),
                {0: SMEM},
                micros=0,
                aliases={at: 1, at + 1: 2, at + 3: 0},
            )
            adjoint(1, False)
        forward(k + 1, False)
        first = [acc[False] if k + 1 == steps - 1 else p[k + 2][False]]
        q_halo = swap(*adjoint(k, True, q_halo, after=first))
        if 0 < k < steps - 2:
            adjoint(k + 1, False)
    send, kept = forward(steps - 1, True, p_halo)
    arrived = lax.ppermute(send, "shot", [(i, i ^ 1) for i in range(shots)])
    opening, second = adjoint(steps - 1, False)
    piece = vmem(count, width_y // shots, width_z)
    pieces = call(
        "pair", pair_kernel, [kept, arrived, opening], [piece] * (shots // 2), (), {2: HBM}, micros=0
    )
    terms = [pieces[0]] + [
        lax.ppermute(pieces[m], "shot", [(i, i ^ (2 * m)) for i in range(shots)])
        for m in range(1, shots // 2)
    ]
    (opening,) = adjoint(steps - 1, True, q_halo, opening)
    (gradient,) = call("sum", sum_kernel, terms, [plain(count, width_y // shots, width_z)], micros=0)
    return (opening[None], second[None], gradient)


def solution(mesh):
    return jax.shard_map(
        body,
        mesh=mesh,
        in_specs=(
            P("shot", "slab", None, None),
            P("shot", "slab", None, None),
            P("shot", "slab", None, None),
            P("shot", "slab", None, None),
            P("slab", None, None),
            P("shot", None),
            P("shot", None),
            P("shot", None, None),
            P("shot", None, "slab"),
        ),
        out_specs=(
            P("shot", "slab", None, None),
            P("shot", "slab", None, None),
            P("slab", "shot", None),
        ),
        check_vma=False,
    )
```

```python
import functools

import jax
import jax.numpy as jnp
import ml_dtypes
import numpy as np
from jax import lax
from jax.experimental import pallas as pl
from jax.experimental.pallas import tpu as pltpu
from jax.sharding import PartitionSpec as P

weights = (-205.0 / 72.0, 8.0 / 5.0, -1.0 / 5.0, 8.0 / 315.0, -1.0 / 560.0)
reach = 4
VMEM = pltpu.VMEM
SMEM = pltpu.SMEM
HBM = pltpu.HBM
limit = 12 * 1024 * 1024


def band(width, centre):
    out = np.zeros((width, width), np.float64)
    for k in range(1, reach + 1):
        out += weights[k] * (np.eye(width, k=k) + np.eye(width, k=-k))
    out += centre * np.eye(width)
    high = out.astype(np.float32).astype(ml_dtypes.bfloat16)
    low = (out - high.astype(np.float64)).astype(np.float32).astype(ml_dtypes.bfloat16)
    return high, low


def band_right(width):
    high, low = band(width, 3.0 * weights[0])
    return np.block([[high, low], [high, np.zeros_like(low)]])


def band_left(width):
    high, low = band(width, 0.0)
    return np.block([[high, high], [low, np.zeros_like(low)]])


def split(v):
    high = v.astype(jnp.bfloat16)
    low = (v - high.astype(jnp.float32)).astype(jnp.bfloat16)
    return high, low


def fill_halo(parity, even, odd, halo):
    @pl.when(parity == 0)
    def _():
        halo[:reach] = odd[...]
        halo[reach:] = even[...]

    @pl.when(parity != 0)
    def _():
        halo[:reach] = even[...]
        halo[reach:] = odd[...]


def emit_edges(parity, outer, even, odd):
    @pl.when(parity == 0)
    def _():
        even[...] = outer[reach:]
        odd[...] = outer[:reach]

    @pl.when(parity != 0)
    def _():
        even[...] = outer[:reach]
        odd[...] = outer[reach:]


def rows_of(count, border):
    if border:
        return list(range(reach)) + list(range(count - reach, count))
    return list(range(reach, count - reach))


def laplace_rows(border, inner, outer, halo, right, left, put):
    count, width_y, width_z = inner.shape[0] + 2 * reach, inner.shape[1], inner.shape[2]

    def plane(i):
        if i < 0:
            return halo[reach + i]
        if i < reach:
            return outer[i]
        if i < count - reach:
            return inner[i - reach]
        if i < count:
            return outer[i - count + 2 * reach]
        return halo[reach + i - count]

    rows = rows_of(count, border)
    for i in range(0, len(rows), 2):
        x = rows[i]
        v = [plane(x), plane(x + 1)]
        (h0, l0), (h1, l1) = split(v[0]), split(v[1])
        flat = jnp.concatenate(
            [jnp.concatenate([h0, l0], axis=1), jnp.concatenate([h1, l1], axis=1)], axis=0
        )
        along = jnp.dot(flat, right[...], preferred_element_type=jnp.float32)
        cols = jnp.concatenate(
            [jnp.concatenate([h0, h1], axis=1), jnp.concatenate([l0, l1], axis=1)], axis=0
        )
        across = jnp.dot(left[...], cols, preferred_element_type=jnp.float32)
        for j in range(2):
            rows_j = slice(j * width_y, (j + 1) * width_y)
            lanes_j = slice(j * width_z, (j + 1) * width_z)
            lap = along[rows_j, :width_z] + along[rows_j, width_z:]
            lap = lap + (across[:width_y, lanes_j] + across[width_y:, lanes_j])
            for k in range(1, reach + 1):
                lap = lap + weights[k] * (plane(x + j + k) + plane(x + j - k))
            put(i + j, x + j, v[j], lap)


def forward_kernel(parts, *refs):
    it = iter(refs)
    border, moves, stores = parts["border"], parts["moves"], parts["stores"]
    adds, opens = parts["adds"], parts["opens"]
    inner, outer = next(it), next(it)
    even, odd = (next(it), next(it)) if border else (None, None)
    right, left = next(it), next(it)
    prev, speed, source, wave = [next(it) for _ in range(4)] if moves else (None,) * 4
    late = next(it) if adds else None
    acc_in = next(it) if adds and not opens else None
    first, lap_first = (next(it), next(it)) if not moves else (None, None)
    total_inner = next(it) if border and not moves else None
    for _ in range(parts["after"]):
        next(it)
    nxt = next(it) if moves else None
    even_out, odd_out = (next(it), next(it)) if moves and border else (None, None)
    lap_out = next(it) if stores else None
    acc_out = next(it) if adds and moves else None
    send, keep = (next(it), next(it)) if border and not moves else (None, None)
    halo = next(it) if border else None
    if moves:
        spot_smem, wave_smem, spot_sem, wave_sem = [next(it) for _ in range(4)]
        spot_copy = pltpu.make_async_copy(source, spot_smem, spot_sem)
        wave_copy = pltpu.make_async_copy(wave, wave_smem, wave_sem)
        spot_copy.start()
        wave_copy.start()
    total = next(it) if not moves else None
    slab = lax.axis_index("slab")
    parity = slab % 2
    count = inner.shape[0] + 2 * reach
    if border:
        fill_halo(parity, even, odd, halo)

    def put(i, x, v, lap):
        if moves:
            nxt[i] = 2.0 * v - prev[i] + speed[x] * lap
        if stores:
            lap_out[i] = lap
        if adds:
            value = lap * late[i]
            if not opens:
                value = value + acc_in[i]
            if moves:
                acc_out[i] = value
            else:
                total[i] = (value + first[i] * lap_first[i]) * parts["scale"]

    laplace_rows(border, inner, outer, halo, right, left, put)
    if moves:
        spot_copy.wait()
        wave_copy.wait()
        row = spot_smem[0, 0] - slab * count
        col, lane = spot_smem[0, 1], spot_smem[0, 2]
        within = (row >= reach) & (row < count - reach)
        place = row - reach
        if border:
            within = (row >= 0) & (row < count) & jnp.logical_not(within)
            place = jnp.where(row < reach, row, row - count + 2 * reach)

        @pl.when(within)
        def _():
            tile = pl.ds(pl.multiple_of((col // 8) * 8, 8), 8)
            shape = (8, inner.shape[2])
            hit = (lax.broadcasted_iota(jnp.int32, shape, 0) == col % 8) & (
                lax.broadcasted_iota(jnp.int32, shape, 1) == lane
            )
            added = jnp.where(hit, wave_smem[0, parts["step"]], 0.0)
            nxt[place, tile, :] = nxt[place, tile, :] + added

        if border:
            emit_edges(parity, nxt, even_out, odd_out)
    elif border:
        chunk = send.shape[2]
        mine = lax.axis_index("shot") % 2
        for j in range(send.shape[0]):
            away = pl.multiple_of((2 * j + 1 - mine) * chunk, 8)
            here = pl.multiple_of((2 * j + mine) * chunk, 8)
            for out, first_row in ((send, away), (keep, here)):
                rows = pl.ds(first_row, chunk)
                out[j, :reach] = total[:reach, rows, :]
                out[j, reach : count - reach] = total_inner[:, rows, :]
                out[j, count - reach :] = total[reach:, rows, :]


def part_copies(border, part, whole, sems, to_whole):
    count = whole.shape[0]
    if border:
        pieces = [(0, 0, reach), (reach, count - reach, reach)]
    else:
        pieces = [(0, reach, count - 2 * reach)]
    copies = []
    for n, (i, x, rows) in enumerate(pieces):
        near, far = part.at[pl.ds(i, rows)], whole.at[pl.ds(x, rows)]
        ends = (near, far) if to_whole else (far, near)
        copies.append(pltpu.make_async_copy(*ends, sems.at[n]))
    return copies


def injected(tiles, x, time, width_y):
    return tiles[pl.ds((x + reach) * width_y * 8 + time, width_y, stride=8), :]


def adjoint_kernel(parts, *refs):
    it = iter(refs)
    border, adds, last = parts["border"], parts["adds"], parts["last"]
    inner, outer = next(it), next(it)
    even, odd = (next(it), next(it)) if border else (None, None)
    right, left, later, speed = [next(it) for _ in range(4)]
    inject = next(it) if parts["injects"] else None
    lap_of, acc_in = (next(it), next(it)) if adds else (None, None)
    if last and border:
        next(it)
    for _ in range(parts["after"]):
        next(it)
    nxt = next(it)
    second = next(it) if last and not border else None
    even_out, odd_out = (next(it), next(it)) if border and not last else (None, None)
    acc_out = next(it) if adds else None
    halo = next(it) if border else None
    part, copies = nxt, []
    if last:
        part, sems = next(it), next(it)
    parity = lax.axis_index("slab") % 2
    count, width_y = inner.shape[0] + 2 * reach, inner.shape[1]
    if border:
        fill_halo(parity, even, odd, halo)
        if parts["late"]:
            for i in range(2 * reach):
                x = i - reach if i < reach else count + i - reach
                halo[i] = halo[i] + injected(inject, x, parts["time"] + 1, width_y)
    elif last:
        copies += part_copies(True, outer, second, sems.at[pl.ds(2, 2)], True)
        copies += part_copies(False, inner, second, sems.at[pl.ds(4, 1)], True)
        for copy in copies:
            copy.start()

    def put(i, x, v, lap):
        value = 2.0 * v - later[i] + speed[x] * lap
        part[i] = value + injected(inject, x, parts["time"], width_y) if parts["injects"] else value
        if adds:
            acc_out[i] = acc_in[i] + v * lap_of[i]

    laplace_rows(border, inner, outer, halo, right, left, put)
    if last:
        for copy in part_copies(border, part, nxt, sems, True):
            copy.start()
            copies.append(copy)
    elif border:
        emit_edges(parity, part, even_out, odd_out)
    for copy in copies:
        copy.wait()


def edges_kernel(*refs):
    fields, traces, outs, traces_out, sems = refs[:2], refs[2], refs[3:7], *refs[7:]
    parity = lax.axis_index("slab") % 2
    top = fields[0].shape[0] - reach
    starts = (top * (1 - parity), top * parity)
    copies = []
    for i in range(4):
        rows = pl.ds(starts[i % 2], reach)
        copies.append(pltpu.make_async_copy(fields[i // 2].at[rows], outs[i], sems.at[i]))
    copies.append(pltpu.make_async_copy(traces, traces_out, sems.at[4]))
    for copy in copies:
        copy.start()
    for copy in copies:
        copy.wait()


def stack_kernel(*refs):
    first = 0
    for ref in refs[:-1]:
        refs[-1][first : first + ref.shape[0]] = ref[...]
        first += ref.shape[0]


def load_kernel(listen, *refs):
    fields, bands, parts, speed, refs = refs[:3], refs[4:6], refs[6:10], refs[10], refs[11:]
    bands_out, where_to, tiles, sems = refs[:2], *refs[2:]
    copies = [pltpu.make_async_copy(bands[i], bands_out[i], sems.at[7 + i]) for i in range(2)]
    copies.append(pltpu.make_async_copy(fields[2], speed, sems.at[6]))
    for i in range(2):
        copies += part_copies(False, parts[2 * i], fields[i], sems.at[pl.ds(3 * i, 1)], False)
        copies += part_copies(True, parts[2 * i + 1], fields[i], sems.at[pl.ds(3 * i + 1, 2)], False)
    for copy in copies:
        copy.start()
    zero_rows = 64 * 8

    @pl.loop(0, tiles.shape[0] // zero_rows)
    def _(i):
        tiles[pl.ds(pl.multiple_of(i * zero_rows, 8), zero_rows), :] = jnp.zeros(
            (zero_rows, 128), jnp.float32
        )

    rest = tiles.shape[0] % zero_rows
    if rest:
        tiles[tiles.shape[0] - rest :, :] = jnp.zeros((rest, 128), jnp.float32)
    for copy in copies:
        copy.wait()
    count, width_y, width_z = fields[0].shape
    held = count + 2 * reach
    depth = listen[0:1, :] - lax.axis_index("slab") * count + reach
    inside = (depth >= 0) & (depth < held)
    flat = depth * (width_y * width_z) + listen[1:2, :] * width_z + listen[2:3, :]
    where_to[...] = jnp.where(inside, flat, held * width_y * width_z)


def load_adjoint_kernel(*refs):
    fields, parts, sems = refs[:2], refs[3:7], refs[7]
    copies = []
    for i in range(2):
        copies += part_copies(False, parts[2 * i], fields[i], sems.at[pl.ds(3 * i, 1)], False)
        copies += part_copies(True, parts[2 * i + 1], fields[i], sems.at[pl.ds(3 * i + 1, 2)], False)
    for copy in copies:
        copy.start()
    for copy in copies:
        copy.wait()


def scatter_kernel(levels, where_to, *refs):
    blocks, refs = refs[:levels], refs[levels:]
    inner, outer, _, _, out, inner_out, outer_out = refs
    per = blocks[0].shape[-1]
    group, groups = 8, 8
    slab = lax.axis_index("slab")
    lanes = lax.broadcasted_iota(jnp.int32, (8, 128), 1)
    d = 0
    for held_blocks in blocks:
        for e in range(held_blocks.shape[0]):
            base = (slab ^ d) * per
            d += 1
            for part in range(per // 128):
                block = held_blocks[e, :, part * 128 : (part + 1) * 128]

                @pl.loop(0, 128 // (group * groups))
                def _(i):
                    def gather(g):
                        tiles, terms, slots = [], [], []
                        for u in range(g * group, (g + 1) * group):
                            j = i * (group * groups) + u
                            flat = where_to[0, base + part * 128 + j]
                            lane = flat & 127
                            tile = flat >> 7
                            moved = pltpu.roll(block, (lane - j) & 127, 1)
                            tiles.append(jnp.full((8, 128), tile, jnp.int32))
                            terms.append(jnp.where(lanes == lane, moved, 0.0))
                            slots.append(pl.ds(pl.multiple_of(tile * 8, 8), 8))
                        return tiles, terms, slots

                    ahead = [gather(0), gather(1)]
                    for g in range(groups):
                        tiles, terms, slots = ahead.pop(0)
                        if g + 2 < groups:
                            ahead.append(gather(g + 2))
                        held = [out[slot, :] for slot in slots]
                        for u in range(group):
                            value = held[u] + terms[u]
                            for w in range(u):
                                value = value + jnp.where(tiles[w] == tiles[u], terms[w], 0.0)
                            held[u] = value
                        for u in range(group):
                            out[slots[u], :] = held[u]

    count, width_y = inner.shape[0] + 2 * reach, inner.shape[1]
    for part, part_out, border in ((inner, inner_out, False), (outer, outer_out, True)):
        for i, x in enumerate(rows_of(count, border)):
            part_out[i] = part[i] + injected(out, x, blocks[0].shape[1] - 1, width_y)


def pair_kernel(keep, arrived, _, *outs):
    mine = lax.axis_index("shot") // 2
    for m in range(len(outs)):
        outs[m][...] = keep[mine ^ m] + arrived[mine ^ m]


def sum_kernel(*refs):
    total = refs[0][...]
    for ref in refs[1:-1]:
        total = total + ref[...]
    refs[-1][...] = total


def vmem(*shape):
    return VMEM(shape, jnp.float32)


def plain(*shape):
    return jax.ShapeDtypeStruct(shape, jnp.float32)


def call(name, kernel, args, outs, scratch=(), spaces=None, out_spaces=None, micros=2, aliases=None):
    spec = lambda space: pl.BlockSpec(memory_space=space)
    spaces = spaces or {}
    args = [
        pltpu.with_memory_space_constraint(arg, HBM) if spaces.get(i) is HBM else arg
        for i, arg in enumerate(args)
    ]
    out_spaces = out_spaces or {}
    return pl.pallas_call(
        kernel,
        out_shape=outs,
        in_specs=[spec(spaces.get(i, VMEM)) for i in range(len(args))],
        out_specs=[spec(out_spaces.get(i, VMEM)) for i in range(len(outs))],
        scratch_shapes=scratch,
        input_output_aliases=aliases or {},
        compiler_params=pltpu.CompilerParams(vmem_limit_bytes=limit),
        cost_estimate=pl.CostEstimate(
            flops=micros * 1000000000, bytes_accessed=micros << 16, transcendentals=0
        ),
        name=name,
    )(*args)


def pair_swap(count, start):
    pairs = []
    for i in range(start, count - 1, 2):
        pairs += [(i, i + 1), (i + 1, i)]
    return pairs


def body(
    state_before,
    state_now,
    adjoint_after,
    adjoint_now,
    speed_term,
    wavelet,
    source,
    receivers,
    traces,
):
    count, width_y, width_z = speed_term.shape
    steps = wavelet.shape[1]
    slabs = lax.axis_size("slab")
    shots = lax.axis_size("shot")
    half = steps // 2
    scale = 1.0 / (8.0 * steps)
    even_pairs, odd_pairs = pair_swap(slabs, 0), pair_swap(slabs, 1)
    inner = count - 2 * reach
    field = vmem(count, width_y, width_z)
    part = {False: vmem(inner, width_y, width_z), True: vmem(2 * reach, width_y, width_z)}
    edge = vmem(reach, width_y, width_z)
    dma = pltpu.SemaphoreType.DMA

    def swap(even, odd):
        return lax.ppermute(even, "slab", even_pairs), lax.ppermute(odd, "slab", odd_pairs)

    p0_even, p0_odd, q8_even, q8_odd, own = call(
        "edges",
        edges_kernel,
        [state_now[0], adjoint_now[0], traces],
        [edge] * 4 + [vmem(*traces.shape)],
        [dma((5,))],
        {0: HBM, 1: HBM, 2: HBM},
    )
    p_halo = swap(p0_even, p0_odd)
    q_halo = swap(q8_even, q8_odd)
    blocks = [own]
    bit = 1
    while bit < slabs:
        held = traces
        if len(blocks) > 1:
            (held,) = call("stack", stack_kernel, blocks, [vmem(bit, *traces.shape[1:])], micros=0)
        blocks.append(lax.ppermute(held, "slab", [(i, i ^ bit) for i in range(slabs)]))
        bit *= 2
    tiles = vmem(((count + 2 * reach) * width_y + 1) * 8, width_z)
    pair_of_parts = [part[False], part[True]]
    bands = [jnp.asarray(band_right(width_z)), jnp.asarray(band_left(width_y))]
    *loaded, speed, right, left, where_to, zeros = call(
        "load",
        load_kernel,
        [receivers[0], state_before[0], state_now[0], speed_term, held, *bands],
        pair_of_parts * 2
        + [field, *(VMEM(band.shape, band.dtype) for band in bands)]
        + [VMEM((1, receivers.shape[2]), jnp.int32), tiles],
        [dma((9,))],
        {i: HBM for i in (1, 2, 3, 5, 6)},
        micros=1,
    )
    p = {-1: loaded[0:2], 0: loaded[2:4]}
    q = {}
    laps, acc = {}, {False: None, True: None}
    inject = None

    def forward(k, border, halos=(), after=()):
        last = k == steps - 1
        parts = dict(
            border=border, moves=not last, stores=k < half, adds=k >= half, opens=k == half, step=k,
            scale=scale, after=len(after),
        )
        args = [*p[k], *halos, right, left]
        outs, scratch, spaces = [], [part[True]] if border else [], {}
        if not last:
            spaces = {len(args) + 2: HBM, len(args) + 3: HBM}
            args += [p[k - 1][border], speed, source, wavelet]
            outs += [part[border]]
            scratch += [SMEM(source.shape, jnp.int32), SMEM(wavelet.shape, jnp.float32), dma, dma]
            if border:
                outs += [edge, edge]
        if parts["stores"]:
            outs += [part[border]]
        if parts["adds"]:
            args += [q[k + 1][border]]
            if not parts["opens"]:
                args += [acc[border]]
            if not last:
                outs += [part[border]]
        if last:
            args += [q[1][border], laps[0][border]]
            if border:
                args += [acc[False]]
                outs += [vmem(shots // 2, count, width_y // shots, width_z)] * 2
                scratch += [part[True]]
            else:
                outs += [part[False]]
        args += after
        name = "forward_border" if border else "forward_inner"
        got = list(
            call(
                name, functools.partial(forward_kernel, parts), args, outs, scratch, spaces,
                micros=0 if last and border else 1,
            )
        )
        if last and not border:
            acc[False] = got[0]
        if last:
            return got
        p.setdefault(k + 1, [None, None])[border] = got.pop(0)
        sides = [got.pop(0), got.pop(0)] if border else None
        if parts["stores"]:
            laps.setdefault(k, [None, None])[border] = got[0]
        else:
            acc[border] = got[0]
        return sides

    def adjoint(k, border, halos=(), opening=None, after=()):
        last = k == steps - 1
        t = steps - 1 - k
        parts = dict(
            border=border, adds=k >= half and not last, last=last, time=t, injects=k > 0, late=k == 1,
            after=len(after),
        )
        args = [*q[t + 1], *halos, right, left, q[t + 2][border], speed]
        outs, scratch, out_spaces, aliases = [part[border]], [part[True]] if border else [], {}, {}
        spaces = {}
        if k > 0:
            args += [inject]
        if parts["adds"]:
            args += [laps[t][border], acc[border]]
        if last:
            whole = plain(count, width_y, width_z)
            outs = [whole] if border else [whole, whole]
            out_spaces = {i: HBM for i in range(len(outs))}
            scratch += [part[border], dma((5,))]
            if border:
                spaces, aliases = {len(args): HBM}, {len(args): 0}
                args += [opening]
        elif border:
            outs += [edge, edge]
        if parts["adds"]:
            outs += [part[border]]
        args += after
        name = "adjoint_border" if border else "adjoint_inner"
        got = call(
            name, functools.partial(adjoint_kernel, parts), args, outs, scratch, spaces, out_spaces,
            micros=30 if last else 1, aliases=aliases,
        )
        if last:
            return got
        q.setdefault(t, [None, None])[border] = got[0]
        if parts["adds"]:
            acc[border] = got[-1]
        return got[1:3] if border else None

    forward(0, False)
    for k in range(steps - 1):
        first = [q[steps - 1 - k][False]] if k > 2 else []
        p_halo = swap(*forward(k, True, p_halo, first))
        if k == 0:
            loaded = call(
                "load_adjoint",
                load_adjoint_kernel,
                [adjoint_after[0], adjoint_now[0], p[1][True]],
                pair_of_parts * 2,
                [dma((6,))],
                {0: HBM, 1: HBM},
                micros=1,
            )
            q.update({steps + 1: loaded[0:2], steps: loaded[2:4]})
            adjoint(0, False)
        if k == 1:
            at = 1 + len(blocks)
            inject, *q[steps - 1] = call(
                "receivers",
                functools.partial(scatter_kernel, len(blocks)),
                [where_to, *blocks, *q[steps - 1], p[2][True], zeros],
                [tiles, *pair_of_parts],
                (),
                {0: SMEM},
                micros=0,
                aliases={at: 1, at + 1: 2, at + 3: 0},
            )
            adjoint(1, False)
        forward(k + 1, False)
        first = [acc[False] if k + 1 == steps - 1 else p[k + 2][False]] if k > 0 else []
        q_halo = swap(*adjoint(k, True, q_halo, after=first))
        if 0 < k < steps - 2:
            adjoint(k + 1, False)
    send, kept = forward(steps - 1, True, p_halo)
    arrived = lax.ppermute(send, "shot", [(i, i ^ 1) for i in range(shots)])
    opening, second = adjoint(steps - 1, False)
    piece = vmem(count, width_y // shots, width_z)
    pieces = call(
        "pair", pair_kernel, [kept, arrived, opening], [piece] * (shots // 2), (), {2: HBM}, micros=0
    )
    terms = [pieces[0]] + [
        lax.ppermute(pieces[m], "shot", [(i, i ^ (2 * m)) for i in range(shots)])
        for m in range(1, shots // 2)
    ]
    (opening,) = adjoint(steps - 1, True, q_halo, opening)
    (gradient,) = call("sum", sum_kernel, terms, [plain(count, width_y // shots, width_z)], micros=0)
    return (opening[None], second[None], gradient)


def solution(mesh):
    return jax.shard_map(
        body,
        mesh=mesh,
        in_specs=(
            P("shot", "slab", None, None),
            P("shot", "slab", None, None),
            P("shot", "slab", None, None),
            P("shot", "slab", None, None),
            P("slab", None, None),
            P("shot", None),
            P("shot", None),
            P("shot", None, None),
            P("shot", None, "slab"),
        ),
        out_specs=(
            P("shot", "slab", None, None),
            P("shot", "slab", None, None),
            P("slab", "shot", None),
        ),
        check_vma=False,
    )
```
